32 devices in a mesh: exp: 8 (over z, x), edp: 4 (over y, core).
Axes of the slice: x: 2, y: 2, z: 4, core: 2. Of those that a mesh axis runs over, the one named last changes fastest.
Arguments:
- out_grad: bfloat16 [4096, 2560], P(('exp', 'edp')), may hold values from -6 to 6
- combine: bfloat16 [4096, 6], P(('exp', 'edp')), may hold values from 0.099609375 to 1.59375
- token_expert_choice: int32 [4096, 6], P(('exp', 'edp')), may hold values from 0 to 7, as said below
- slots: int32 [4096, 6], P(('exp', 'edp')), may hold values from 0 to 64, as said below
- counts: int32 [32, 8], P(('exp', 'edp')), may hold values from 0 to 64, as said below
- down_weight: bfloat16 [8, 768, 2560], P('exp', 'edp'), may hold values from -0.125 to 0.125
- stored_gate_preact: bfloat16 [8, 4, 512, 768], P('exp', 'edp'), may hold values from -6 to 6
- stored_up_preact: bfloat16 [8, 4, 512, 768], P('exp', 'edp'), may hold values from -6 to 6
Outputs:
- gate_preact_gradient: bfloat16 [8, 4, 512, 768], P('exp', 'edp')
- up_preact_gradient: bfloat16 [8, 4, 512, 768], P('exp', 'edp')
- down_matrix_gradient: bfloat16 [8, 768, 2560], P('exp', 'edp')
- combine_weight_gradient: float32 [4096, 6], P(('exp', 'edp'))
The draws below stay inside these ranges and needn't reach their ends.
Inputs may be any that keep to these rules, and one draw needn't show every extreme that they name: `token_expert_choice`: each row names 6 different experts. `slots`: the rank of the choice among the rows of the same device that name the same expert, in row order, or 64 where that rank reaches 64 and the choice is dropped. `counts`: for each device and expert, the number of that device's rows that name the expert, but at most 64.
All inputs are finite; a program needn't handle non-finite values.
Results may differ from the reference program's by a relative error of at most 0.0057.
Values may be sent and summed in bfloat16 or wider, within the bound.
No kernel may reach another device: no remote copies, remote signals or barrier semaphores. Data moves between devices by JAX's collectives and lax.ppermute only.
A program may use at most 128 MiB of HBM per device.

```python
import math
import jax
import jax.numpy as jnp
from jax import lax

D = 2560
FEEDFORWARD_UNITS = 768
TOPK = 6
TOK_DEV = 128
ROUTED_EXPERTS = 8
SOURCES = 32
TOKENS = 4096
SLOT_CAPACITY = 64
RECEIVE_SLOTS = 512
N_EXP = 8
N_EDP = 4


def routing(key):
    base = jax.random.fold_in(key, 7)
    key_scores, key_bias, key_hot = jax.random.split(base, 3)
    raw_scores = jax.random.randint(key_scores, (TOKENS, ROUTED_EXPERTS), 0, 2 ** 20, dtype=jnp.int32)
    bias = jax.random.randint(key_bias, (ROUTED_EXPERTS,), 0, 2 ** 19, dtype=jnp.int32)
    hot_expert = jax.random.randint(key_hot, (), 0, ROUTED_EXPERTS, dtype=jnp.int32)
    local_row = jnp.arange(TOKENS, dtype=jnp.int32) % TOK_DEV
    expert_range = jnp.arange(ROUTED_EXPERTS, dtype=jnp.int32)
    boost = jnp.where((local_row[:, None] <= SLOT_CAPACITY) & (expert_range[None, :] == hot_expert), 2 ** 22, 0).astype(jnp.int32)
    ranked = (raw_scores + bias[None, :] + boost) * ROUTED_EXPERTS + expert_range[None, :]
    chosen_ids = lax.top_k(ranked, TOPK)[1].astype(jnp.int32)
    chosen = jnp.sum((chosen_ids[:, :, None] == expert_range[None, None, :]).astype(jnp.int32), axis=1)
    per_device = chosen.reshape(SOURCES, TOK_DEV, ROUTED_EXPERTS)
    before = (jnp.cumsum(per_device, axis=1) - per_device).reshape(TOKENS, ROUTED_EXPERTS)
    ranks = jnp.take_along_axis(before, chosen_ids, axis=1)
    slot_table = jnp.minimum(ranks, SLOT_CAPACITY).astype(jnp.int32)
    count_table = jnp.minimum(jnp.sum(per_device, axis=1), SLOT_CAPACITY).astype(jnp.int32)
    return (chosen_ids, slot_table, count_table)


def draw_token_expert_choice(key, part):
    return routing(key)[0]


def draw_slots(key, part):
    return routing(key)[1]


def draw_counts(key, part):
    return routing(key)[2]


def level_of(rng, extent, cuts, least, largest):
    def one(position, blocks):
        draws = jax.random.uniform(jax.random.fold_in(jax.random.fold_in(rng, 6), position), (blocks,), jnp.float32, least / len(cuts), largest / len(cuts))
        return jnp.repeat(jnp.exp(draws), extent[position] // blocks).reshape((-1,) + (1,) * (len(extent) - position - 1))

    loudness = one(*cuts[0])
    for cut in cuts[1:]:
        loudness = loudness * one(*cut)
    return loudness


def centred(stream_key, shape, spread, bound, pieces=(), held_as=jnp.bfloat16):
    result = jax.random.normal(stream_key, shape, jnp.float32) * spread
    if len(pieces) > 0:
        result = level_of(stream_key, shape, pieces, -0.22, 0.18) * result
    return jnp.clip(result, min=-bound, max=bound).astype(held_as)


def setup_inputs(seed: int = 0) -> dict:
    seeds = jax.random.split(jax.random.key(seed), 9)
    return {
        "out_grad": centred(seeds[0], (TOKENS, D), 1.0, 6.0, ((0, 32),)),
        "combine": jnp.clip(jnp.exp(math.log(1.59375) - 2.7725887 * jax.random.uniform(seeds[1], (TOKENS, TOPK), jnp.float32) ** level_of(seeds[1], (TOKENS, TOPK), ((0, 32),), -0.2, 0.2)), 0.099609375, 1.59375).astype(jnp.bfloat16),
        "token_expert_choice": draw_token_expert_choice(jax.random.fold_in(seeds[8], 71), 0),
        "slots": draw_slots(jax.random.fold_in(seeds[8], 71), 0),
        "counts": draw_counts(jax.random.fold_in(seeds[8], 71), 0),
        "down_weight": centred(seeds[5], (ROUTED_EXPERTS, FEEDFORWARD_UNITS, D), D ** -0.5, 0.125, ((0, 8), (1, 4))),
        "stored_gate_preact": centred(seeds[6], (ROUTED_EXPERTS, N_EDP, RECEIVE_SLOTS, FEEDFORWARD_UNITS), 1.0, 6.0, ((0, 8), (1, 4))),
        "stored_up_preact": centred(seeds[7], (ROUTED_EXPERTS, N_EDP, RECEIVE_SLOTS, FEEDFORWARD_UNITS), 1.0, 6.0, ((0, 8), (1, 4))),
    }


def reference(out_grad, combine, token_expert_choice, slots, counts, down_weight, stored_gate_preact, stored_up_preact):
    tok_index = jnp.arange(TOKENS, dtype=jnp.int32)
    device = tok_index // TOK_DEV
    sender_expert_shard = device // N_EDP
    sender_data_shard = device % N_EDP
    row_total = ROUTED_EXPERTS * N_EDP * RECEIVE_SLOTS
    destination_slot = (token_expert_choice * N_EDP + sender_data_shard[:, None]) * RECEIVE_SLOTS + sender_expert_shard[:, None] * SLOT_CAPACITY + slots
    destination_slot = jnp.where(slots < SLOT_CAPACITY, destination_slot, row_total).astype(jnp.int32)
    flat_target = destination_slot.reshape(-1)
    row_ids = jnp.broadcast_to(tok_index[:, None] + 1, destination_slot.shape).astype(jnp.int32).reshape(-1)
    sender_rows = jnp.zeros((row_total,), jnp.int32).at[flat_target].set(row_ids, mode="drop")
    received_weight = jnp.zeros((row_total,), jnp.bfloat16).at[flat_target].set(combine.reshape(-1), mode="drop")
    count_table = jnp.transpose(counts.reshape(N_EXP, N_EDP, ROUTED_EXPERTS), (2, 1, 0))
    valid_mask = (jnp.arange(SLOT_CAPACITY, dtype=jnp.int32)[None, None, None, :] < count_table[:, :, :, None]).astype(jnp.float32)
    valid_mask = valid_mask.reshape(ROUTED_EXPERTS, N_EDP * RECEIVE_SLOTS)
    padded_grad = jnp.concatenate([jnp.zeros((1, D), jnp.bfloat16), out_grad], axis=0)

    def per_expert(inputs):
        rows_here, weight_here, live_here, matrix, gate_here, up_here = inputs
        grad_rows = padded_grad[rows_here]
        scaled = live_here * weight_here.astype(jnp.float32)
        proj = lax.dot_general(grad_rows, matrix, (((1,), (1,)), ((), ())), preferred_element_type=jnp.float32)
        gate_pre = gate_here.astype(jnp.float32)
        up_pre = up_here.astype(jnp.float32)
        sigmoid_gate = jax.nn.sigmoid(gate_pre)
        silu_gate = gate_pre * sigmoid_gate
        hidden = (silu_gate * up_pre).astype(jnp.bfloat16)
        weighted = (scaled[:, None] * grad_rows.astype(jnp.float32)).astype(jnp.bfloat16)
        grad_matrix = lax.dot_general(hidden, weighted, (((0,), (0,)), ((), ())), preferred_element_type=jnp.float32)
        grad_hidden = scaled[:, None] * proj
        gate_preact_gradient = (grad_hidden * up_pre * sigmoid_gate * (1.0 + gate_pre * (1.0 - sigmoid_gate))).astype(jnp.bfloat16)
        up_preact_gradient = (grad_hidden * silu_gate).astype(jnp.bfloat16)
        score = live_here * jnp.sum(proj * hidden.astype(jnp.float32), axis=1)
        return gate_preact_gradient, up_preact_gradient, score, grad_matrix.astype(jnp.bfloat16)

    gate_preact_gradient, up_preact_gradient, score, down_matrix_gradient = lax.map(per_expert, (
        sender_rows.reshape(ROUTED_EXPERTS, N_EDP * RECEIVE_SLOTS),
        received_weight.reshape(ROUTED_EXPERTS, N_EDP * RECEIVE_SLOTS),
        valid_mask,
        down_weight,
        stored_gate_preact.reshape(ROUTED_EXPERTS, N_EDP * RECEIVE_SLOTS, FEEDFORWARD_UNITS),
        stored_up_preact.reshape(ROUTED_EXPERTS, N_EDP * RECEIVE_SLOTS, FEEDFORWARD_UNITS)))
    returned = jnp.concatenate([score.reshape(-1), jnp.zeros((1,), jnp.float32)])
    combine_weight_gradient = returned[destination_slot]
    return (gate_preact_gradient.reshape(ROUTED_EXPERTS, N_EDP, RECEIVE_SLOTS, FEEDFORWARD_UNITS), up_preact_gradient.reshape(ROUTED_EXPERTS, N_EDP, RECEIVE_SLOTS, FEEDFORWARD_UNITS), down_matrix_gradient, combine_weight_gradient)
```

```python
import functools

import jax
import jax.numpy as jnp
from jax import lax
from jax.experimental import pallas as pl
from jax.experimental.pallas import tpu as pltpu
from jax.sharding import PartitionSpec as P


def flip(n, mask):
    return [(i, i ^ mask) for i in range(n)]


def column_cuts(width):
    unit = width // 20
    return [(0, 14 * unit), (14 * unit, width)]


VMEM = pl.BlockSpec(memory_space=pltpu.VMEM)
SMEM = pl.BlockSpec(memory_space=pltpu.SMEM)
BLOCK = pl.BlockSpec()
ANY = pl.BlockSpec(memory_space=pl.ANY)
LANES = 128
CODE, WEIGHT, CHOICE, SLOT = 0, 8, 16, 24


def call(body, outs, specs, megabytes, flops=0, moved=0, scratch=(), after=(), out_specs=None):
    def ordered(*refs):
        body(*refs[len(after) :])

    kernel = pl.pallas_call(
        ordered,
        out_shape=outs,
        in_specs=[ANY] * len(after) + list(specs),
        out_specs=out_specs or [VMEM] * len(outs),
        scratch_shapes=scratch,
        compiler_params=pltpu.CompilerParams(vmem_limit_bytes=megabytes * 1024 * 1024),
        cost_estimate=pl.CostEstimate(flops=flops, bytes_accessed=moved, transcendentals=0),
    )
    return functools.partial(kernel, *after)


def routing_body(
    capacity, n_exp, cut, choice_ref, slot_ref, combine_ref, counts_ref, tok_ref, meta_ref, raw_ref, *outs
):
    topk = choice_ref.shape[0]
    columns = cut[1] - cut[0]
    choice = choice_ref[...]
    slot = slot_ref[...]
    limit = jnp.zeros_like(slot)
    for expert in range(n_exp):
        limit = jnp.where(choice == expert, counts_ref[0, expert], limit)
    kept = slot < capacity
    live = kept & (slot < limit)
    meta_ref[...] = jnp.zeros_like(meta_ref)
    meta_ref[CODE : CODE + topk, :] = jnp.where(kept, choice * capacity + slot, -1).astype(jnp.float32)
    meta_ref[WEIGHT : WEIGHT + topk, :] = jnp.where(live, combine_ref[...].astype(jnp.float32), 0.0)
    meta_ref[CHOICE : CHOICE + topk, :] = choice.astype(jnp.float32)
    meta_ref[SLOT : SLOT + topk, :] = slot.astype(jnp.float32)
    raw_ref[:, :columns] = tok_ref[:, cut[0] : cut[1]]
    raw_ref[:, columns:] = meta_ref[...].T.astype(jnp.bfloat16)
    select(capacity, topk, meta_ref, tok_ref[...], outs, True)


def places(target, capacity):
    return (lax.broadcasted_iota(jnp.int32, (capacity, LANES), 0) + target).astype(jnp.float32)


def pick(meta, topk, want):
    hit = meta[CODE : CODE + 1, :] == want
    for k in range(1, topk):
        hit = hit | (meta[CODE + k : CODE + k + 1, :] == want)
    return jnp.where(hit, 1.0, 0.0)


def weight_of(meta, topk, want):
    weight = jnp.zeros(want.shape, jnp.float32)
    for k in range(topk):
        weight = jnp.where(
            meta[CODE + k : CODE + k + 1, :] == want, meta[WEIGHT + k : WEIGHT + k + 1, :], weight
        )
    return jnp.sum(weight, axis=1, keepdims=True)


def select(capacity, topk, meta, rows, outs, weights):
    here = lax.axis_index("exp")
    columns = rows.shape[1]
    wants = [places((here ^ m) * capacity, capacity) for m in range(len(outs))]
    onehot = jnp.concatenate([pick(meta, topk, w) for w in wants], axis=0).astype(jnp.bfloat16)
    chosen = jnp.dot(onehot, rows, preferred_element_type=jnp.float32).astype(jnp.bfloat16)
    for m, out in enumerate(outs):
        out[:, :columns] = chosen[m * capacity : (m + 1) * capacity]
        if weights:
            weight = weight_of(meta, topk, wants[m])
            out[:, columns:] = jnp.broadcast_to(weight, (capacity, LANES)).astype(jnp.bfloat16)


def select_first_body(capacity, topk, cuts, raw_ref, tok_ref, *refs):
    *outs, following_ref, meta_ref = refs
    columns = raw_ref.shape[1] - LANES
    block = raw_ref[:, columns:].astype(jnp.float32).T
    slot = block[SLOT : SLOT + 8]
    meta_ref[...] = block
    meta_ref[CODE : CODE + 8, :] = jnp.where(
        slot < capacity, block[CHOICE : CHOICE + 8] * capacity + slot, -1.0
    )
    select(capacity, topk, meta_ref, raw_ref[:, :columns], outs, True)
    following_ref[...] = tok_ref[:, cuts[1][0] : cuts[1][1]]


def select_more_body(capacity, topk, raw_ref, meta_ref, *outs):
    select(capacity, topk, meta_ref, raw_ref[...], outs, False)


def source_rows(capacity, n):
    source = lax.axis_index("exp") ^ n
    return pl.ds(pl.multiple_of(source * capacity, capacity), capacity)


def factors_body(
    capacity, n_edp, gate_ref, up_ref, hidden_ref, gate_factor_ref, up_factor_ref, turned_ref, scratch
):
    data = lax.axis_index("edp")
    rows, units = gate_ref.shape
    shard = units // n_edp
    for n in range(rows // capacity):
        at = pl.ds(n * capacity, capacity)
        there = source_rows(capacity, n)
        gate_pre = gate_ref[there, :].astype(jnp.float32)
        up_pre = up_ref[there, :].astype(jnp.float32)
        sigmoid_gate = jax.nn.sigmoid(gate_pre)
        silu_gate = gate_pre * sigmoid_gate
        hidden_ref[at, :] = (silu_gate * up_pre).astype(jnp.bfloat16)
        gate_factor_ref[at, :] = up_pre * sigmoid_gate * (1.0 + gate_pre * (1.0 - sigmoid_gate))
        up_factor_ref[at, :] = silu_gate
    scratch[...] = hidden_ref[...].T
    for n in range(n_edp):
        turned_ref[n] = scratch[pl.ds(pl.multiple_of((data ^ n) * shard, 64), shard), :]


def add_cores(keep_ref, from_core_ref, sum_ref):
    sum_ref[...] = (keep_ref[1] + from_core_ref[...].astype(jnp.float32)).astype(jnp.bfloat16)


def output_body(width, keep_ref, from_core_ref, from_y_ref, out_ref, *_):
    out_ref[...] = (
        keep_ref[0]
        + from_core_ref[...].astype(jnp.float32)
        + from_y_ref[...].astype(jnp.float32)
    ).astype(jnp.bfloat16)


def returned_body(capacity, n_exp, choice_ref, slot_ref, counts_ref, score_ref, out_ref):
    topk, tokens = choice_ref.shape
    choice = choice_ref[...]
    slot = slot_ref[...]
    limit = jnp.zeros_like(slot)
    for expert in range(n_exp):
        limit = jnp.where(choice == expert, counts_ref[0, expert], limit)
    live = (slot < capacity) & (slot < limit)
    rank = lax.broadcasted_iota(jnp.int32, (capacity, tokens), 0)
    expert = lax.broadcasted_iota(jnp.int32, (n_exp, tokens), 0)
    found = []
    for k in range(topk):
        onehot = jnp.where(rank == slot[k : k + 1, :], 1.0, 0.0)
        all_experts = jnp.dot(
            score_ref[...], onehot, precision=lax.Precision.HIGHEST, preferred_element_type=jnp.float32
        )
        mine = jnp.where(expert == choice[k : k + 1, :], all_experts, 0.0)
        found.append(jnp.sum(mine, axis=0, keepdims=True))
    out_ref[...] = jnp.where(live, jnp.concatenate(found, axis=0), 0.0)


def term_body(far, cut, tile, turned_ref, *refs):
    own, others, scales, (keep_ref, *send_refs, weighted) = (
        refs[:far], refs[far : 2 * far], refs[2 * far : 3 * far], refs[3 * far :]
    )
    capacity = own[0].shape[0]
    n_edp = turned_ref.shape[0]
    columns = cut[1] - cut[0]
    for half, (pieces, weights) in enumerate(((own, own), (others, scales))):
        shift = cut[0] if half == 0 else 0
        for m in range(far):
            at = pl.ds((half * far + m) * capacity, capacity)
            scale = weights[m][:, weights[m].shape[1] - LANES :].astype(jnp.float32)
            for i in range(0, columns, LANES):
                weighted[at, i : i + LANES] = (
                    scale * pieces[m][:, shift + i : shift + i + LANES].astype(jnp.float32)
                ).astype(jnp.bfloat16)
    for i in range(columns // tile):
        lanes = pl.ds(i * tile, tile)
        for n in range(n_edp):
            term = jnp.dot(turned_ref[n], weighted[:, lanes], preferred_element_type=jnp.float32)
            if n % 2 == 0:
                keep_ref[n // 2, :, lanes] = term
            else:
                send_refs[n // 2][:, lanes] = term.astype(jnp.bfloat16)


def nt(a, b):
    return lax.dot_general(a, b, (((1,), (1,)), ((), ())), preferred_element_type=jnp.float32)


def finish(proj, weights, hidden, gate_factor, up_factor):
    part = proj * hidden.astype(jnp.float32)
    lanes = part[:, :LANES]
    for i in range(LANES, part.shape[1], LANES):
        lanes = lanes + part[:, i : i + LANES]
    score = jnp.sum(lanes.T, axis=0, keepdims=True)
    scaled = weights * proj
    gate = (gate_factor * scaled).astype(jnp.bfloat16)
    up = (up_factor * scaled).astype(jnp.bfloat16)
    return gate, up, score


def weights_of(refs):
    return jnp.concatenate([r[:, r.shape[1] - LANES :][:, 0:1] for r in refs], axis=0).astype(jnp.float32)


def project_own_body(far, *refs):
    shards, own, refs = refs[:4], refs[4 : 4 + far], refs[4 + far :]
    hidden_ref, gate_factor_ref, up_factor_ref, weight_ref, gate_ref, up_ref, score_ref = refs
    data = lax.axis_index("edp")
    shard, width = shards[0].shape
    capacity = own[0].shape[0]
    for n in range(4):
        weight_ref[pl.ds(pl.multiple_of((data ^ n) * shard, 64), shard), :] = shards[n][...]
    rows = jnp.concatenate([p[:, :width] for p in own], axis=0)
    proj = nt(rows, weight_ref[...])
    for m in range(0, far, 2):
        at = slice(m * capacity, (m + 2) * capacity)
        gate_ref[at, :], up_ref[at, :], score = finish(
            proj[at], weights_of(own[m : m + 2]), hidden_ref[at, :], gate_factor_ref[at, :], up_factor_ref[at, :]
        )
        score_ref[m // 2 : m // 2 + 1, :] = score


def project_far_body(far, cut, *refs):
    pieces, (weight_ref, proj_ref) = refs[:far], refs[far:]
    rows = jnp.concatenate([p[:, : cut[1] - cut[0]] for p in pieces], axis=0)
    proj_ref[...] = nt(rows, weight_ref[:, cut[0] : cut[1]])


def final_body(far, cut, *refs):
    pieces, scales, refs = refs[:far], refs[far : 2 * far], refs[2 * far :]
    (
        weight_ref, proj_ref, hidden_ref, gate_factor_ref, up_factor_ref,
        own_gate_ref, own_up_ref, own_score_ref, gate_ref, up_ref, score_ref,
    ) = refs
    here = lax.axis_index("exp")
    capacity = pieces[0].shape[0]
    rows = jnp.concatenate([p[...] for p in pieces], axis=0)
    proj = proj_ref[...] + nt(rows, weight_ref[:, cut[0] : cut[1]])
    for m in range(0, far, 2):
        near = slice(m * capacity, (m + 2) * capacity)
        at = slice((far + m) * capacity, (far + m + 2) * capacity)
        found = finish(
            proj[near], weights_of(scales[m : m + 2]), hidden_ref[at, :], gate_factor_ref[at, :], up_factor_ref[at, :]
        )
        held = own_gate_ref[near, :], own_up_ref[near, :], own_score_ref[m // 2 : m // 2 + 1, :]
        for first, (gate, up, score) in ((far + m, found), (m, held)):
            for i in range(2):
                mine = slice(i * capacity, (i + 1) * capacity)
                there = source_rows(capacity, first + i)
                gate_ref[there, :] = gate[mine]
                up_ref[there, :] = up[mine]
                score_ref[pl.ds(here ^ (first + i), 1), :] = score[:, mine]


def relayed(
    out_grad,
    combine,
    token_expert_choice,
    slots,
    counts,
    down_weight,
    stored_gate_preact,
    stored_up_preact,
):
    n_exp = lax.axis_size("exp")
    n_edp = lax.axis_size("edp")
    capacity = stored_gate_preact.shape[2] // n_exp
    units = stored_gate_preact.shape[3]
    rows = n_exp * capacity
    tok_rows, width = out_grad.shape
    topk = slots.shape[1]
    shard = units // n_edp
    far = n_exp // 2
    cuts = column_cuts(width)
    sizes = [b - a for a, b in cuts]
    bf16, f32 = jnp.bfloat16, jnp.float32

    def shape(*dims, dtype=bf16):
        return jax.ShapeDtypeStruct(dims, dtype)

    def hop(x, axis, mask, after=None):
        if after is not None:
            x, _ = lax.optimization_barrier((x, after))
        return lax.ppermute(x, axis, flip(lax.axis_size(axis), mask))

    def spread(found):
        return [found[0]] + [hop(found[m], "exp", m) for m in range(1, far)]

    meta, payload, *found = call(
        functools.partial(routing_body, capacity, n_exp, cuts[0]),
        [shape(LANES, LANES, dtype=f32), shape(tok_rows, sizes[0] + LANES)]
        + [shape(capacity, width + LANES)] * far,
        [BLOCK, BLOCK, BLOCK, SMEM, BLOCK],
        56,
        flops=2 * far * capacity * tok_rows * width,
        moved=out_grad.size * 4,
    )(token_expert_choice.T, slots.T, combine.T, counts, out_grad)
    raw = hop(payload, "exp", far)
    own = spread(found)
    hidden, gate_factor, up_factor, turned = call(
        functools.partial(factors_body, capacity, n_edp),
        [
            shape(rows, units),
            shape(rows, units, dtype=f32),
            shape(rows, units, dtype=f32),
            shape(n_edp, shard, rows),
        ],
        [VMEM] * 2,
        24,
        flops=40 * rows * units,
        moved=16 * rows * units,
        scratch=[pltpu.VMEM((units, rows), bf16)],
        after=[own[0]],
    )(stored_gate_preact[0, 0], stored_up_preact[0, 0])
    weight_core = hop(down_weight[0], "edp", 1)
    weight_y = hop(down_weight[0], "edp", 2, (weight_core, payload))

    def term(k, others, scales, after=()):
        return call(
            functools.partial(term_body, far, cuts[k], 256),
            [shape(2, shard, sizes[k], dtype=f32)] + [shape(shard, sizes[k])] * 2,
            [VMEM] * (1 + 3 * far),
            24,
            flops=2 * rows * units * sizes[k],
            moved=4 * (rows + units) * sizes[k],
            scratch=[pltpu.VMEM((rows, sizes[k]), bf16)],
            after=after,
        )(turned, *own, *others, *scales)

    def cores(send):
        return [hop(send[i], "edp", 1) for i in range(2)]

    def across(k, keep, from_core, after=()):
        (sent,) = call(
            add_cores, [shape(shard, sizes[k])], [VMEM] * 2, 8, flops=1, moved=1, after=after
        )(keep, from_core)
        return sent

    def output(k, keep, from_core, from_y):
        (part,) = call(functools.partial(output_body, width), [shape(shard, sizes[k])], [VMEM] * 3, 8)(
            keep, from_core, from_y
        )
        return part

    *found, payload, far_meta = call(
        functools.partial(select_first_body, capacity, topk, cuts),
        [shape(capacity, sizes[0] + LANES)] * far
        + [shape(tok_rows, sizes[1]), shape(LANES, LANES, dtype=f32)],
        [VMEM] * 2,
        16,
        flops=2 * far * capacity * tok_rows * sizes[0],
        moved=4 * far * capacity * sizes[0],
        after=[*own[1:], hidden, weight_y],
    )(raw, out_grad)
    far0 = spread(found)
    raw = hop(payload, "exp", far)
    weight_both = hop(weight_y, "edp", 1, far_meta)
    found = call(
        functools.partial(select_more_body, capacity, topk),
        [shape(capacity, sizes[1])] * far,
        [VMEM] * 2,
        16,
        flops=2 * far * capacity * tok_rows * sizes[1],
        moved=4 * far * capacity * sizes[1],
        after=[*far0[1:], weight_both],
    )(raw, far_meta)
    far1 = spread(found)
    keep0, *send0 = term(0, far0, far0, [far1[0]])
    core0 = cores(send0)
    sent0 = across(0, keep0, core0[1], core0[:1])
    part0 = output(0, keep0, core0[0], hop(sent0, "edp", 2))
    weight, own_gate, own_up, own_score = call(
        functools.partial(project_own_body, far),
        [
            shape(units, width),
            shape(far * capacity, units),
            shape(far * capacity, units),
            shape(far // 2, 2 * capacity, dtype=f32),
        ],
        [VMEM] * (7 + far),
        32,
        flops=1,
        moved=1,
        after=[sent0],
    )(down_weight[0], weight_core, weight_y, weight_both, *own, hidden, gate_factor, up_factor)
    (proj,) = call(
        functools.partial(project_far_body, far, cuts[0]),
        [shape(far * capacity, units, dtype=f32)],
        [VMEM] * (1 + far),
        24,
        flops=1,
        moved=1,
        after=[own_score],
    )(*far0, weight)
    keep1, *send1 = term(1, far1, far0, [proj])
    core1 = cores(send1)
    gate_preact_gradient, up_preact_gradient, score = call(
        functools.partial(final_body, far, cuts[1]),
        [shape(rows, units), shape(rows, units), shape(n_exp, capacity, dtype=f32)],
        [VMEM] * (2 * far + 8),
        32,
        flops=rows * units * sizes[1],
        moved=8 * rows * units,
        after=[keep1],
    )(*far1, *far0, weight, proj, hidden, gate_factor, up_factor, own_gate, own_up, own_score)
    sent1 = across(1, keep1, core1[1], [score, core1[0]])
    part1 = output(1, keep1, core1[0], hop(sent1, "edp", 2))
    returned = lax.all_to_all(score, "exp", split_axis=0, concat_axis=0)
    (combine_weight_gradient,) = call(
        functools.partial(returned_body, capacity, n_exp),
        [shape(topk, tok_rows, dtype=f32)],
        [VMEM, VMEM, SMEM, VMEM],
        8,
    )(token_expert_choice.T, slots.T, counts, returned)
    return (
        gate_preact_gradient[None, None],
        up_preact_gradient[None, None],
        jnp.concatenate([part0, part1], axis=1)[None],
        combine_weight_gradient.T,
    )


def direct(
    out_grad,
    combine,
    token_expert_choice,
    slots,
    counts,
    down_weight,
    stored_gate_preact,
    stored_up_preact,
):
    experts_here = lax.axis_size("exp")
    capacity = stored_gate_preact.shape[2] // experts_here
    tok_rows = out_grad.shape[0]
    model_width = out_grad.shape[1]
    slot_index = jnp.where(
        slots < capacity, token_expert_choice * capacity + slots, experts_here * capacity
    )
    flat_index = slot_index.reshape(-1)
    row_ids = jnp.broadcast_to(
        jnp.arange(tok_rows, dtype=jnp.int32)[:, None] + 1, slot_index.shape
    ).reshape(-1)
    sender_rows = (
        jnp.zeros((experts_here * capacity,), jnp.int32).at[flat_index].set(row_ids, mode="drop")
    )
    padded_grad = jnp.concatenate([jnp.zeros((1, model_width), out_grad.dtype), out_grad], axis=0)
    send_grad = padded_grad[sender_rows].reshape(experts_here, capacity, model_width)
    send_weight = (
        jnp.zeros((experts_here * capacity,), combine.dtype)
        .at[flat_index]
        .set(combine.reshape(-1), mode="drop")
    )
    send_weight = send_weight.reshape(experts_here, capacity)
    send_count = counts.reshape(experts_here, 1)
    recv_grad, received_weight, recv_count = (
        lax.all_to_all(send_grad, "exp", split_axis=0, concat_axis=0, tiled=True),
        lax.all_to_all(send_weight, "exp", split_axis=0, concat_axis=0, tiled=True),
        lax.all_to_all(send_count, "exp", split_axis=0, concat_axis=0, tiled=True),
    )
    live_mask = (jnp.arange(capacity, dtype=jnp.int32)[None, :] < recv_count).astype(jnp.float32)
    scaled = (live_mask * received_weight.astype(jnp.float32)).reshape(-1)
    live_rows = live_mask.reshape(-1)
    grad_rows = recv_grad.reshape(-1, model_width)
    proj = lax.dot_general(
        grad_rows,
        lax.all_gather(down_weight, "edp", axis=1, tiled=True)[0],
        (((1,), (1,)), ((), ())),
        preferred_element_type=jnp.float32,
    )
    gate_pre = stored_gate_preact[0, 0].astype(jnp.float32)
    up_pre = stored_up_preact[0, 0].astype(jnp.float32)
    sigmoid_gate = jax.nn.sigmoid(gate_pre)
    silu_gate = gate_pre * sigmoid_gate
    hidden = (silu_gate * up_pre).astype(jnp.bfloat16)
    weighted = (scaled[:, None] * grad_rows.astype(jnp.float32)).astype(jnp.bfloat16)
    grad_hidden = scaled[:, None] * proj
    gate_preact_gradient = (
        grad_hidden * up_pre * sigmoid_gate * (1.0 + gate_pre * (1.0 - sigmoid_gate))
    ).astype(jnp.bfloat16)
    up_preact_gradient = (grad_hidden * silu_gate).astype(jnp.bfloat16)
    score = (live_rows * jnp.sum(proj * hidden.astype(jnp.float32), axis=1)).reshape(
        experts_here, capacity
    )
    returned_scores = lax.all_to_all(score, "exp", split_axis=0, concat_axis=0, tiled=True)
    summed = lax.psum_scatter(
        lax.dot_general(
            hidden, weighted, (((0,), (0,)), ((), ())), preferred_element_type=jnp.float32
        ),
        "edp",
        scatter_dimension=0,
        tiled=True,
    )
    returned = jnp.concatenate([returned_scores.reshape(-1), jnp.zeros((1,), jnp.float32)])
    combine_weight_gradient = returned[slot_index]
    down_matrix_gradient = summed.astype(jnp.bfloat16)[None]
    return (
        gate_preact_gradient[None, None],
        up_preact_gradient[None, None],
        down_matrix_gradient,
        combine_weight_gradient,
    )


def solution(mesh):
    n_exp, n_edp = mesh.shape["exp"], mesh.shape["edp"]

    def on_device(*arrays):
        tok_rows = arrays[0].shape[0]
        capacity = arrays[6].shape[2] // n_exp
        if n_exp == 8 and n_edp == 4 and tok_rows == LANES and tok_rows <= 2 * capacity:
            return relayed(*arrays)
        return direct(*arrays)

    return jax.shard_map(
        on_device,
        mesh=mesh,
        in_specs=(
            P(("exp", "edp"), None),
            P(("exp", "edp"), None),
            P(("exp", "edp"), None),
            P(("exp", "edp"), None),
            P(("exp", "edp"), None),
            P("exp", "edp", None),
            P("exp", "edp", None, None),
            P("exp", "edp", None, None),
        ),
        out_specs=(
            P("exp", "edp", None, None),
            P("exp", "edp", None, None),
            P("exp", "edp", None),
            P(("exp", "edp"), None),
        ),
        check_vma=False,
    )
```

```python
import functools

import jax
import jax.numpy as jnp
from jax import lax
from jax.experimental import pallas as pl
from jax.experimental.pallas import tpu as pltpu
from jax.sharding import PartitionSpec as P


def flip(n, mask):
    return [(i, i ^ mask) for i in range(n)]


def column_cuts(width):
    unit = width // 20
    return [(0, 15 * unit), (15 * unit, width)]


VMEM = pl.BlockSpec(memory_space=pltpu.VMEM)
SMEM = pl.BlockSpec(memory_space=pltpu.SMEM)
BLOCK = pl.BlockSpec()
ANY = pl.BlockSpec(memory_space=pl.ANY)
LANES = 128
CODE, WEIGHT, CHOICE, SLOT = 0, 8, 16, 24


def call(body, outs, specs, megabytes, flops=0, moved=0, scratch=(), after=(), out_specs=None, aliases=()):
    def ordered(*refs):
        body(*refs[len(after) :])

    kernel = pl.pallas_call(
        ordered,
        out_shape=outs,
        in_specs=[ANY] * len(after) + list(specs),
        out_specs=out_specs or [VMEM] * len(outs),
        scratch_shapes=scratch,
        input_output_aliases={len(after) + i: o for i, o in aliases},
        compiler_params=pltpu.CompilerParams(vmem_limit_bytes=megabytes * 1024 * 1024),
        cost_estimate=pl.CostEstimate(flops=flops, bytes_accessed=moved, transcendentals=0),
    )
    return functools.partial(kernel, *after)


def routing_body(
    capacity, n_exp, choice_ref, slot_ref, combine_ref, counts_ref, tok_ref, meta_ref, raw_ref, *outs
):
    topk = choice_ref.shape[0]
    columns = tok_ref.shape[1]
    choice = choice_ref[...]
    slot = slot_ref[...]
    limit = jnp.zeros_like(slot)
    for expert in range(n_exp):
        limit = jnp.where(choice == expert, counts_ref[0, expert], limit)
    kept = slot < capacity
    live = kept & (slot < limit)
    meta_ref[...] = jnp.zeros_like(meta_ref)
    meta_ref[CODE : CODE + topk, :] = jnp.where(kept, choice * capacity + slot, -1).astype(jnp.float32)
    meta_ref[WEIGHT : WEIGHT + topk, :] = jnp.where(live, combine_ref[...].astype(jnp.float32), 0.0)
    meta_ref[CHOICE : CHOICE + topk, :] = choice.astype(jnp.float32)
    meta_ref[SLOT : SLOT + topk, :] = slot.astype(jnp.float32)
    raw_ref[:, :columns] = tok_ref[...]
    raw_ref[:, columns:] = meta_ref[...].T.astype(jnp.bfloat16)
    select(capacity, topk, meta_ref, tok_ref[...], outs)


def places(target, capacity):
    return (lax.broadcasted_iota(jnp.int32, (capacity, LANES), 0) + target).astype(jnp.float32)


def pick(meta, topk, want):
    hit = meta[CODE : CODE + 1, :] == want
    for k in range(1, topk):
        hit = hit | (meta[CODE + k : CODE + k + 1, :] == want)
    return jnp.where(hit, 1.0, 0.0)


def weight_of(meta, topk, want):
    weight = jnp.zeros(want.shape, jnp.float32)
    for k in range(topk):
        weight = jnp.where(
            meta[CODE + k : CODE + k + 1, :] == want, meta[WEIGHT + k : WEIGHT + k + 1, :], weight
        )
    return jnp.sum(weight, axis=1, keepdims=True)


def select(capacity, topk, meta, rows, outs, own_meta=None):
    here = lax.axis_index("exp")
    columns = rows.shape[1]
    wants = [places((here ^ m) * capacity, capacity) for m in range(len(outs))]
    onehot = jnp.concatenate([pick(meta, topk, w) for w in wants], axis=0).astype(jnp.bfloat16)
    chosen = jnp.dot(onehot, rows, preferred_element_type=jnp.float32).astype(jnp.bfloat16)
    for m, out in enumerate(outs):
        out[:, :columns] = chosen[m * capacity : (m + 1) * capacity]
        if own_meta is not None:
            lane = lax.broadcasted_iota(jnp.int32, (capacity, LANES), 1)
            weight, own_weight = (weight_of(x, topk, wants[m]) for x in (meta, own_meta))
            out[:, columns:] = jnp.where(lane < LANES // 2, weight, own_weight).astype(jnp.bfloat16)


def select_first_body(capacity, topk, cut, raw_ref, own_meta_ref, *refs):
    *outs, meta_ref = refs
    columns = raw_ref.shape[1] - LANES
    block = raw_ref[:, columns:].astype(jnp.float32).T
    slot = block[SLOT : SLOT + 8]
    meta_ref[...] = block
    meta_ref[CODE : CODE + 8, :] = jnp.where(
        slot < capacity, block[CHOICE : CHOICE + 8] * capacity + slot, -1.0
    )
    select(capacity, topk, meta_ref, raw_ref[:, cut[0] : cut[1]], outs, own_meta_ref)


def select_more_body(capacity, topk, cut, raw_ref, meta_ref, *outs):
    select(capacity, topk, meta_ref, raw_ref[:, cut[0] : cut[1]], outs)


def source_rows(capacity, n):
    source = lax.axis_index("exp") ^ n
    return pl.ds(pl.multiple_of(source * capacity, capacity), capacity)


def factors_body(
    capacity, n_edp, gate_ref, up_ref, meta_ref,
    hidden_ref, gate_factor_ref, up_factor_ref, turned_ref, meta_out_ref, scratch,
):
    data = lax.axis_index("edp")
    rows, units = gate_ref.shape
    shard = units // n_edp
    for n in range(rows // capacity):
        at = pl.ds(n * capacity, capacity)
        there = source_rows(capacity, n)
        gate_pre = gate_ref[there, :].astype(jnp.float32)
        up_pre = up_ref[there, :].astype(jnp.float32)
        sigmoid_gate = jax.nn.sigmoid(gate_pre)
        silu_gate = gate_pre * sigmoid_gate
        hidden_ref[at, :] = (silu_gate * up_pre).astype(jnp.bfloat16)
        gate_factor_ref[at, :] = up_pre * sigmoid_gate * (1.0 + gate_pre * (1.0 - sigmoid_gate))
        up_factor_ref[at, :] = silu_gate
    meta_out_ref[...] = meta_ref[...]
    scratch[...] = hidden_ref[...].T
    for n in range(n_edp):
        turned_ref[n] = scratch[pl.ds(pl.multiple_of((data ^ n) * shard, 64), shard), :]


def add_cores(across_ref, *refs):
    *from_core, sum_ref = refs
    start = 0
    for ref in from_core:
        rows = pl.ds(start, ref.shape[0])
        start += ref.shape[0]
        sum_ref[rows, :] = (across_ref[rows, :] + ref[...].astype(jnp.float32)).astype(jnp.bfloat16)


def last_body(capacity, n_exp, cuts, choice_ref, slot_ref, counts_ref, score_ref, *refs):
    sums, (out_ref, weight_ref, held, held_weight, sems) = refs[: 3 * len(cuts)], refs[3 * len(cuts) :]
    copies = []
    for k, (a, b) in enumerate(cuts):
        keep_ref, from_core_ref, from_y_ref = sums[3 * k : 3 * k + 3]
        held[:, a:b] = (
            keep_ref[...] + from_core_ref[...].astype(jnp.float32) + from_y_ref[...].astype(jnp.float32)
        ).astype(jnp.bfloat16)
        lanes = pl.ds(a, b - a)
        copies.append(pltpu.make_async_copy(held.at[:, lanes], out_ref.at[:, lanes], sems.at[k]))
        copies[-1].start()
    topk, tokens = choice_ref.shape
    choice = choice_ref[...]
    slot = slot_ref[...]
    limit = jnp.zeros_like(slot)
    for expert in range(n_exp):
        limit = jnp.where(choice == expert, counts_ref[0, expert], limit)
    live = (slot < capacity) & (slot < limit)
    table = score_ref[...]
    high = table.astype(jnp.bfloat16)
    rest = table - high.astype(jnp.float32)
    middle = rest.astype(jnp.bfloat16)
    low = (rest - middle.astype(jnp.float32)).astype(jnp.bfloat16)
    split = jnp.concatenate([high, middle, low], axis=0)
    rank = lax.broadcasted_iota(jnp.int32, (capacity, tokens), 0)
    expert = lax.broadcasted_iota(jnp.int32, (n_exp, tokens), 0)
    found = []
    for k in range(topk):
        onehot = jnp.where(rank == slot[k : k + 1, :], 1.0, 0.0).astype(jnp.bfloat16)
        parts = jnp.dot(split, onehot, preferred_element_type=jnp.float32)
        every = parts[:n_exp] + parts[n_exp : 2 * n_exp] + parts[2 * n_exp :]
        mine = jnp.where(expert == choice[k : k + 1, :], every, 0.0)
        found.append(jnp.sum(mine, axis=0, keepdims=True))
    held_weight[...] = jnp.where(live, jnp.concatenate(found, axis=0), 0.0)
    copies.append(pltpu.make_async_copy(held_weight, weight_ref, sems.at[len(cuts)]))
    copies[-1].start()
    for copy in copies:
        copy.wait()


def weigh(far, cut, own, others, scales, weighted):
    capacity = own[0].shape[0]
    columns = cut[1] - cut[0]
    for half, pieces in enumerate((own, others)):
        shift = cut[0] if half == 0 else 0
        for m in range(far):
            at = pl.ds((half * far + m) * capacity, capacity)
            scale = jnp.broadcast_to(weights_of(scales[m : m + 1], half == 0), (capacity, LANES))
            for i in range(0, columns, LANES):
                weighted[at, i : i + LANES] = (
                    scale * pieces[m][:, shift + i : shift + i + LANES].astype(jnp.float32)
                ).astype(jnp.bfloat16)


def terms(tile, turned_ref, weighted, outs):
    for i in range(weighted.shape[1] // tile):
        lanes = pl.ds(i * tile, tile)
        for n, refs in outs:
            term = jnp.dot(turned_ref[n], weighted[:, lanes], preferred_element_type=jnp.float32)
            high = term.shape[0] // len(refs)
            for j, ref in enumerate(refs):
                ref[:, lanes] = term[j * high : (j + 1) * high].astype(ref.dtype)


def first_term_body(far, cut, tile, turned_ref, *refs):
    own, others, (send_ref, weighted) = refs[:far], refs[far : 2 * far], refs[2 * far :]
    weigh(far, cut, own, others, others, weighted)
    terms(tile, turned_ref, weighted, [(3, [send_ref])])


def more_terms_body(tile, shards, turned_ref, weighted, *refs):
    terms(tile, turned_ref, weighted, [(n, [ref]) for n, ref in zip(shards, refs)])


def term_body(far, cut, tile, turned_ref, *refs):
    own, others, scales, (own_ref, across_ref, send_ref, *send_across_refs, weighted) = (
        refs[:far], refs[far : 2 * far], refs[2 * far : 3 * far], refs[3 * far :]
    )
    weigh(far, cut, own, others, scales, weighted)
    outs = [(3, send_across_refs), (2, [across_ref]), (1, [send_ref]), (0, [own_ref])]
    terms(tile, turned_ref, weighted, outs)


def nt(a, b):
    return lax.dot_general(a, b, (((1,), (1,)), ((), ())), preferred_element_type=jnp.float32)


def finish(proj, weights, hidden, gate_factor, up_factor):
    part = proj * hidden.astype(jnp.float32)
    lanes = part[:, :LANES]
    for i in range(LANES, part.shape[1], LANES):
        lanes = lanes + part[:, i : i + LANES]
    score = jnp.sum(lanes.T, axis=0, keepdims=True)
    scaled = weights * proj
    gate = (gate_factor * scaled).astype(jnp.bfloat16)
    up = (up_factor * scaled).astype(jnp.bfloat16)
    return gate, up, score


def weights_of(refs, own):
    at = LANES // 2 if own else 0
    return jnp.concatenate(
        [r[:, r.shape[1] - LANES :][:, at : at + 1] for r in refs], axis=0
    ).astype(jnp.float32)


def project_own_body(far, *refs):
    shards, own, (weight_ref, proj_ref) = refs[:4], refs[4 : 4 + far], refs[4 + far :]
    data = lax.axis_index("edp")
    shard = shards[0].shape[0]
    for n in range(4):
        weight_ref[pl.ds(pl.multiple_of((data ^ n) * shard, 64), shard), :] = shards[n][...]
    proj_ref[...] = nt(jnp.concatenate([p[...] for p in own], axis=0), weight_ref[...])


def finish_half(first, far, proj, weights, hidden_ref, gate_factor_ref, up_factor_ref, outs, held, sems):
    here = lax.axis_index("exp")
    count = 2 * (proj.shape[0] // far)
    scores, copies = [], []
    for m in range(0, far, 2):
        near = slice(m * count // 2, m * count // 2 + count)
        at = slice((first + m) * count // 2, (first + m) * count // 2 + count)
        gate, up, score = finish(
            proj[near], weights[near], hidden_ref[at, :], gate_factor_ref[at, :], up_factor_ref[at, :]
        )
        scores.append(score)
        lower = pl.multiple_of(((here ^ (first + m)) // 2) * count, count)
        for i in range(2):
            mine = slice(i * count // 2, (i + 1) * count // 2)
            within = pl.multiple_of(lax.rem(here ^ i, 2) * (count // 2), count // 2)
            there = pl.ds(m // 2 * count + within, count // 2)
            held[0, there, :] = gate[mine]
            held[1, there, :] = up[mine]
        for i, out in enumerate(outs):
            copy = pltpu.make_async_copy(
                held.at[i, pl.ds(m // 2 * count, count), :], out.at[pl.ds(lower, count), :], sems.at[m // 2, i]
            )
            copy.start()
            copies.append(copy)
    return scores, copies


def project_far_body(far, cut, *refs):
    pieces, refs = refs[:far], refs[far:]
    weight_ref, own_proj_ref, hidden_ref, gate_factor_ref, up_factor_ref, *outs = refs
    proj_ref, gate_ref, up_ref, score_ref, held, sems = outs
    scores, copies = finish_half(
        0, far, own_proj_ref[...], weights_of(pieces, True), hidden_ref, gate_factor_ref, up_factor_ref,
        (gate_ref, up_ref), held, sems,
    )
    for i, score in enumerate(scores):
        score_ref[i : i + 1, :] = score
    rows = jnp.concatenate([p[:, : cut[1] - cut[0]] for p in pieces], axis=0)
    proj_ref[...] = nt(rows, weight_ref[:, cut[0] : cut[1]])
    for copy in copies:
        copy.wait()


def final_body(far, cut, *refs):
    pieces, scales, refs = refs[:far], refs[far : 2 * far], refs[2 * far :]
    (
        weight_ref, proj_ref, hidden_ref, gate_factor_ref, up_factor_ref, own_score_ref, _, _,
        gate_ref, up_ref, score_ref, held, sems,
    ) = refs
    here = lax.axis_index("exp")
    capacity = pieces[0].shape[0]
    rows = jnp.concatenate([p[...] for p in pieces], axis=0)
    proj = proj_ref[...] + nt(rows, weight_ref[:, cut[0] : cut[1]])
    scores, copies = finish_half(
        far, far, proj, weights_of(scales, False), hidden_ref, gate_factor_ref, up_factor_ref,
        (gate_ref, up_ref), held, sems,
    )
    for m in range(0, far, 2):
        for first, score in ((far + m, scores[m // 2]), (m, own_score_ref[m // 2 : m // 2 + 1, :])):
            for i in range(2):
                score_ref[pl.ds(here ^ (first + i), 1), :] = score[:, i * capacity : (i + 1) * capacity]
    for copy in copies:
        copy.wait()


def relayed(
    out_grad,
    combine,
    token_expert_choice,
    slots,
    counts,
    down_weight,
    stored_gate_preact,
    stored_up_preact,
):
    n_exp = lax.axis_size("exp")
    n_edp = lax.axis_size("edp")
    capacity = stored_gate_preact.shape[2] // n_exp
    units = stored_gate_preact.shape[3]
    rows = n_exp * capacity
    tok_rows, width = out_grad.shape
    topk = slots.shape[1]
    shard = units // n_edp
    far = n_exp // 2
    cuts = column_cuts(width)
    sizes = [b - a for a, b in cuts]
    splits = [1, 2]
    bf16, f32 = jnp.bfloat16, jnp.float32

    def shape(*dims, dtype=bf16):
        return jax.ShapeDtypeStruct(dims, dtype)

    def hop(x, axis, mask, after=None):
        if after is not None:
            x, _ = lax.optimization_barrier((x, after))
        return lax.ppermute(x, axis, flip(lax.axis_size(axis), mask))

    def spread(found):
        return [found[0]] + [hop(found[m], "exp", m) for m in range(1, far)]

    meta, payload, *found = call(
        functools.partial(routing_body, capacity, n_exp),
        [shape(LANES, LANES, dtype=f32), shape(tok_rows, width + LANES)]
        + [shape(capacity, width)] * far,
        [BLOCK, BLOCK, BLOCK, SMEM, BLOCK],
        56,
        flops=2 * far * capacity * tok_rows * width,
        moved=out_grad.size * 4,
    )(token_expert_choice.T, slots.T, combine.T, counts, out_grad)
    raw = hop(payload, "exp", far)
    own = spread(found)
    hidden, gate_factor, up_factor, turned, meta = call(
        functools.partial(factors_body, capacity, n_edp),
        [
            shape(rows, units),
            shape(rows, units, dtype=f32),
            shape(rows, units, dtype=f32),
            shape(n_edp, shard, rows),
            shape(LANES, LANES, dtype=f32),
        ],
        [VMEM] * 3,
        24,
        flops=40 * rows * units,
        moved=16 * rows * units,
        scratch=[pltpu.VMEM((units, rows), bf16)],
        after=[own[0]],
    )(stored_gate_preact[0, 0], stored_up_preact[0, 0], meta)
    weight_core = hop(down_weight[0], "edp", 1)
    weight_y = hop(down_weight[0], "edp", 2, (weight_core, payload))

    def term(k, others, scales, after=()):
        return call(
            functools.partial(term_body, far, cuts[k], 640),
            [shape(shard, sizes[k], dtype=f32)] * 2
            + [shape(shard, sizes[k])]
            + [shape(shard // splits[k], sizes[k])] * splits[k],
            [VMEM] * (1 + 3 * far),
            24,
            flops=2 * rows * units * sizes[k],
            moved=4 * (rows + units) * sizes[k],
            scratch=[pltpu.VMEM((rows, sizes[k]), bf16)],
            after=after,
        )(turned, *own, *others, *scales)

    def cores(send):
        return [hop(x, "edp", 1) for x in send]

    def across(k, mine, from_core, after=()):
        (sent,) = call(add_cores, [shape(shard, sizes[k])], [VMEM] * (1 + splits[k]), 8, after=after)(
            mine, *from_core
        )
        return sent, hop(sent, "edp", 2)

    *found, far_meta = call(
        functools.partial(select_first_body, capacity, topk, cuts[0]),
        [shape(capacity, sizes[0] + LANES)] * far
        + [shape(LANES, LANES, dtype=f32)],
        [VMEM] * 2,
        16,
        flops=2 * far * capacity * tok_rows * sizes[0],
        moved=4 * far * capacity * sizes[0],
        after=[*own[1:], hidden, weight_y],
    )(raw, meta)
    far0 = spread(found)
    weight_both = hop(weight_y, "edp", 1, far_meta)
    weight, own_proj = call(
        functools.partial(project_own_body, far),
        [shape(units, width), shape(far * capacity, units, dtype=f32)],
        [VMEM] * (4 + far),
        32,
    )(down_weight[0], weight_core, weight_y, weight_both, *own)
    first0, weighted = call(
        functools.partial(first_term_body, far, cuts[0], 640),
        [shape(shard, sizes[0]), shape(rows, sizes[0])],
        [VMEM] * (1 + 2 * far),
        24,
        after=[own_proj],
    )(turned, *own, *far0)
    first0 = hop(first0, "edp", 1)
    def more_terms(shards, outs, after=()):
        return call(
            functools.partial(more_terms_body, 640, shards), outs, [VMEM] * 2, 24, after=after
        )(turned, weighted)

    across0, send0 = more_terms([2, 1], [shape(shard, sizes[0], dtype=f32), shape(shard, sizes[0])])
    core0 = hop(send0, "edp", 1)
    sent0, from_y0 = across(0, across0, [first0])
    found = call(
        functools.partial(select_more_body, capacity, topk, cuts[1]),
        [shape(capacity, sizes[1])] * far,
        [VMEM] * 2,
        16,
        flops=2 * far * capacity * tok_rows * sizes[1],
        moved=4 * far * capacity * sizes[1],
        after=[sent0],
    )(raw, far_meta)
    far1 = spread(found)
    half_scratch = [
        pltpu.VMEM((2, far * capacity, units), bf16),
        pltpu.SemaphoreType.DMA((far // 2, 2)),
    ]
    proj, gate_preact_gradient, up_preact_gradient, own_score = call(
        functools.partial(project_far_body, far, cuts[0]),
        [
            shape(far * capacity, units, dtype=f32),
            shape(rows, units),
            shape(rows, units),
            shape(far // 2, 2 * capacity, dtype=f32),
        ],
        [VMEM] * (5 + far),
        24,
        scratch=half_scratch,
        after=[sent0, far1[0], core0],
        out_specs=[VMEM, ANY, ANY, VMEM],
    )(*far0, weight, own_proj, hidden, gate_factor, up_factor)
    (keep0,) = more_terms([0], [shape(shard, sizes[0], dtype=f32)], [proj])
    keep1, across1, *send1 = term(1, far1, far0, [keep0])
    core1 = cores(send1)
    gate_preact_gradient, up_preact_gradient, score = call(
        functools.partial(final_body, far, cuts[1]),
        [shape(rows, units), shape(rows, units), shape(n_exp, capacity, dtype=f32)],
        [VMEM] * (2 * far + 6) + [ANY] * 2,
        24,
        scratch=half_scratch,
        after=[keep1],
        out_specs=[ANY, ANY, VMEM],
        aliases=[(2 * far + 6, 0), (2 * far + 7, 1)],
    )(
        *far1, *far0, weight, proj, hidden, gate_factor, up_factor, own_score,
        gate_preact_gradient, up_preact_gradient,
    )
    _, from_y1 = across(1, across1, core1[1:], [score, core1[0]])
    returned = lax.all_to_all(score, "exp", split_axis=0, concat_axis=0)
    down_matrix_gradient, combine_weight_gradient = call(
        functools.partial(last_body, capacity, n_exp, cuts),
        [shape(shard, width), shape(topk, tok_rows, dtype=f32)],
        [VMEM, VMEM, SMEM] + [VMEM] * (1 + 3 * len(cuts)),
        16,
        scratch=[
            pltpu.VMEM((shard, width), bf16),
            pltpu.VMEM((topk, tok_rows), f32),
            pltpu.SemaphoreType.DMA((len(cuts) + 1,)),
        ],
        out_specs=[ANY, ANY],
    )(
        token_expert_choice.T, slots.T, counts, returned,
        keep0, core0, from_y0, keep1, core1[0], from_y1,
    )
    return (
        gate_preact_gradient[None, None],
        up_preact_gradient[None, None],
        down_matrix_gradient[None],
        combine_weight_gradient.T,
    )


def direct(
    out_grad,
    combine,
    token_expert_choice,
    slots,
    counts,
    down_weight,
    stored_gate_preact,
    stored_up_preact,
):
    experts_here = lax.axis_size("exp")
    capacity = stored_gate_preact.shape[2] // experts_here
    tok_rows = out_grad.shape[0]
    model_width = out_grad.shape[1]
    slot_index = jnp.where(
        slots < capacity, token_expert_choice * capacity + slots, experts_here * capacity
    )
    flat_index = slot_index.reshape(-1)
    row_ids = jnp.broadcast_to(
        jnp.arange(tok_rows, dtype=jnp.int32)[:, None] + 1, slot_index.shape
    ).reshape(-1)
    sender_rows = (
        jnp.zeros((experts_here * capacity,), jnp.int32).at[flat_index].set(row_ids, mode="drop")
    )
    padded_grad = jnp.concatenate([jnp.zeros((1, model_width), out_grad.dtype), out_grad], axis=0)
    send_grad = padded_grad[sender_rows].reshape(experts_here, capacity, model_width)
    send_weight = (
        jnp.zeros((experts_here * capacity,), combine.dtype)
        .at[flat_index]
        .set(combine.reshape(-1), mode="drop")
    )
    send_weight = send_weight.reshape(experts_here, capacity)
    send_count = counts.reshape(experts_here, 1)
    recv_grad, received_weight, recv_count = (
        lax.all_to_all(send_grad, "exp", split_axis=0, concat_axis=0, tiled=True),
        lax.all_to_all(send_weight, "exp", split_axis=0, concat_axis=0, tiled=True),
        lax.all_to_all(send_count, "exp", split_axis=0, concat_axis=0, tiled=True),
    )
    live_mask = (jnp.arange(capacity, dtype=jnp.int32)[None, :] < recv_count).astype(jnp.float32)
    scaled = (live_mask * received_weight.astype(jnp.float32)).reshape(-1)
    live_rows = live_mask.reshape(-1)
    grad_rows = recv_grad.reshape(-1, model_width)
    proj = lax.dot_general(
        grad_rows,
        lax.all_gather(down_weight, "edp", axis=1, tiled=True)[0],
        (((1,), (1,)), ((), ())),
        preferred_element_type=jnp.float32,
    )
    gate_pre = stored_gate_preact[0, 0].astype(jnp.float32)
    up_pre = stored_up_preact[0, 0].astype(jnp.float32)
    sigmoid_gate = jax.nn.sigmoid(gate_pre)
    silu_gate = gate_pre * sigmoid_gate
    hidden = (silu_gate * up_pre).astype(jnp.bfloat16)
    weighted = (scaled[:, None] * grad_rows.astype(jnp.float32)).astype(jnp.bfloat16)
    grad_hidden = scaled[:, None] * proj
    gate_preact_gradient = (
        grad_hidden * up_pre * sigmoid_gate * (1.0 + gate_pre * (1.0 - sigmoid_gate))
    ).astype(jnp.bfloat16)
    up_preact_gradient = (grad_hidden * silu_gate).astype(jnp.bfloat16)
    score = (live_rows * jnp.sum(proj * hidden.astype(jnp.float32), axis=1)).reshape(
        experts_here, capacity
    )
    returned_scores = lax.all_to_all(score, "exp", split_axis=0, concat_axis=0, tiled=True)
    summed = lax.psum_scatter(
        lax.dot_general(
            hidden, weighted, (((0,), (0,)), ((), ())), preferred_element_type=jnp.float32
        ),
        "edp",
        scatter_dimension=0,
        tiled=True,
    )
    returned = jnp.concatenate([returned_scores.reshape(-1), jnp.zeros((1,), jnp.float32)])
    combine_weight_gradient = returned[slot_index]
    down_matrix_gradient = summed.astype(jnp.bfloat16)[None]
    return (
        gate_preact_gradient[None, None],
        up_preact_gradient[None, None],
        down_matrix_gradient,
        combine_weight_gradient,
    )


def solution(mesh):
    n_exp, n_edp = mesh.shape["exp"], mesh.shape["edp"]

    def on_device(*arrays):
        tok_rows = arrays[0].shape[0]
        capacity = arrays[6].shape[2] // n_exp
        if n_exp == 8 and n_edp == 4 and tok_rows == LANES and tok_rows <= 2 * capacity:
            return relayed(*arrays)
        return direct(*arrays)

    return jax.shard_map(
        on_device,
        mesh=mesh,
        in_specs=(
            P(("exp", "edp"), None),
            P(("exp", "edp"), None),
            P(("exp", "edp"), None),
            P(("exp", "edp"), None),
            P(("exp", "edp"), None),
            P("exp", "edp", None),
            P("exp", "edp", None, None),
            P("exp", "edp", None, None),
        ),
        out_specs=(
            P("exp", "edp", None, None),
            P("exp", "edp", None, None),
            P("exp", "edp", None),
            P(("exp", "edp"), None),
        ),
        check_vma=False,
    )
```

```python
import functools

import jax
import jax.numpy as jnp
from jax import lax
from jax.experimental import pallas as pl
from jax.experimental.pallas import tpu as pltpu
from jax.sharding import PartitionSpec as P


def flip(n, mask):
    return [(i, i ^ mask) for i in range(n)]


def column_cuts(width):
    unit = width // 20
    return [(0, 15 * unit), (15 * unit, width)]


VMEM = pl.BlockSpec(memory_space=pltpu.VMEM)
SMEM = pl.BlockSpec(memory_space=pltpu.SMEM)
BLOCK = pl.BlockSpec()
ANY = pl.BlockSpec(memory_space=pl.ANY)
LANES = 128
CODE, WEIGHT, META_ROWS = 0, 8, 16


def call(body, outs, specs, megabytes, flops=0, moved=0, scratch=(), after=(), out_specs=None, aliases=()):
    def ordered(*refs):
        body(*refs[len(after) :])

    kernel = pl.pallas_call(
        ordered,
        out_shape=outs,
        in_specs=[ANY] * len(after) + list(specs),
        out_specs=out_specs or [VMEM] * len(outs),
        scratch_shapes=scratch,
        input_output_aliases={len(after) + i: o for i, o in aliases},
        compiler_params=pltpu.CompilerParams(vmem_limit_bytes=megabytes * 1024 * 1024),
        cost_estimate=pl.CostEstimate(flops=flops, bytes_accessed=moved, transcendentals=0),
    )
    return functools.partial(kernel, *after)


def routing_body(
    capacity, n_exp, choice_ref, slot_ref, combine_ref, counts_ref, tok_ref, meta_ref, *outs
):
    topk = choice_ref.shape[0]
    choice = choice_ref[...]
    slot = slot_ref[...]
    limit = jnp.zeros_like(slot)
    for expert in range(n_exp):
        limit = jnp.where(choice == expert, counts_ref[0, expert], limit)
    kept = slot < capacity
    live = kept & (slot < limit)
    meta_ref[...] = jnp.zeros_like(meta_ref)
    meta_ref[CODE : CODE + topk, :] = jnp.where(kept, choice * capacity + slot, -1).astype(jnp.float32)
    meta_ref[WEIGHT : WEIGHT + topk, :] = jnp.where(live, combine_ref[...].astype(jnp.float32), 0.0)
    select(capacity, topk, meta_ref, tok_ref[...], outs)


def places(target, capacity):
    return (lax.broadcasted_iota(jnp.int32, (capacity, LANES), 0) + target).astype(jnp.float32)


def pick(meta, topk, want):
    hit = meta[CODE : CODE + 1, :] == want
    for k in range(1, topk):
        hit = hit | (meta[CODE + k : CODE + k + 1, :] == want)
    return jnp.where(hit, 1.0, 0.0)


def weight_of(meta, topk, want):
    weight = jnp.zeros(want.shape, jnp.float32)
    for k in range(topk):
        weight = jnp.where(
            meta[CODE + k : CODE + k + 1, :] == want, meta[WEIGHT + k : WEIGHT + k + 1, :], weight
        )
    return jnp.sum(weight, axis=1, keepdims=True)


def select(capacity, topk, meta, rows, outs, own_meta=None):
    here = lax.axis_index("exp")
    columns = rows.shape[1]
    wants = [places((here ^ m) * capacity, capacity) for m in range(len(outs))]
    onehot = jnp.concatenate([pick(meta, topk, w) for w in wants], axis=0).astype(jnp.bfloat16)
    chosen = jnp.dot(onehot, rows, preferred_element_type=jnp.float32).astype(jnp.bfloat16)
    for m, out in enumerate(outs):
        out[:, :columns] = chosen[m * capacity : (m + 1) * capacity]
        if own_meta is not None:
            lane = lax.broadcasted_iota(jnp.int32, (capacity, LANES), 1)
            weight, own_weight = (weight_of(x, topk, wants[m]) for x in (meta, own_meta))
            out[:, columns:] = jnp.where(lane < LANES // 2, weight, own_weight).astype(jnp.bfloat16)


def select_first_body(capacity, topk, cut, raw_ref, meta_ref, own_meta_ref, *outs):
    select(capacity, topk, meta_ref, raw_ref[:, cut[0] : cut[1]], outs, own_meta_ref)


def select_more_body(capacity, topk, cut, raw_ref, meta_ref, *outs):
    select(capacity, topk, meta_ref, raw_ref[:, cut[0] : cut[1]], outs)


def source_rows(capacity, n):
    source = lax.axis_index("exp") ^ n
    return pl.ds(pl.multiple_of(source * capacity, capacity), capacity)


def factors_body(
    capacity, n_edp, gate_ref, up_ref, meta_ref,
    hidden_ref, gate_factor_ref, up_factor_ref, turned_ref, meta_out_ref, scratch,
):
    data = lax.axis_index("edp")
    rows, units = gate_ref.shape
    shard = units // n_edp
    for n in range(rows // capacity):
        at = pl.ds(n * capacity, capacity)
        there = source_rows(capacity, n)
        gate_pre = gate_ref[there, :].astype(jnp.float32)
        up_pre = up_ref[there, :].astype(jnp.float32)
        sigmoid_gate = jax.nn.sigmoid(gate_pre)
        silu_gate = gate_pre * sigmoid_gate
        hidden_ref[at, :] = (silu_gate * up_pre).astype(jnp.bfloat16)
        gate_factor_ref[at, :] = up_pre * sigmoid_gate * (1.0 + gate_pre * (1.0 - sigmoid_gate))
        up_factor_ref[at, :] = silu_gate
    meta_out_ref[...] = meta_ref[...]
    scratch[...] = hidden_ref[...].T
    for n in range(n_edp):
        turned_ref[n] = scratch[pl.ds(pl.multiple_of((data ^ n) * shard, 64), shard), :]


def add_cores(across_ref, *refs):
    *from_core, sum_ref = refs
    start = 0
    for ref in from_core:
        rows = pl.ds(start, ref.shape[0])
        start += ref.shape[0]
        sum_ref[rows, :] = (across_ref[rows, :] + ref[...].astype(jnp.float32)).astype(jnp.bfloat16)


def summed_out(cut, sums, out_ref, held, sem):
    keep_ref, from_core_ref, from_y_ref = sums
    held[...] = (
        keep_ref[...] + from_core_ref[...].astype(jnp.float32) + from_y_ref[...].astype(jnp.float32)
    ).astype(jnp.bfloat16)
    copy = pltpu.make_async_copy(held, out_ref.at[:, pl.ds(cut[0], cut[1] - cut[0])], sem)
    copy.start()
    return copy


def last_body(cut, *refs):
    *sums, _, out_ref, held, sem = refs
    summed_out(cut, sums, out_ref, held, sem).wait()


def returned_body(capacity, n_exp, cut, choice_ref, slot_ref, counts_ref, score_ref, far_half_ref, *refs):
    sums, refs = refs[:3], refs[5:]
    out_ref, weight_ref, gate_ref, up_ref, held, held_weight, sems, half_sems = refs
    far = n_exp // 2
    copies = []
    for m in range(0, far, 2):
        copies += copies_out(far, m, far, far_half_ref, (gate_ref, up_ref), half_sems)
    copies.append(summed_out(cut, sums, out_ref, held, sems.at[0]))
    topk, tokens = choice_ref.shape
    choice = choice_ref[...]
    slot = slot_ref[...]
    limit = jnp.zeros_like(slot)
    for expert in range(n_exp):
        limit = jnp.where(choice == expert, counts_ref[0, expert], limit)
    live = (slot < capacity) & (slot < limit)
    table = score_ref[...]
    high = table.astype(jnp.bfloat16)
    rest = table - high.astype(jnp.float32)
    middle = rest.astype(jnp.bfloat16)
    low = (rest - middle.astype(jnp.float32)).astype(jnp.bfloat16)
    split = jnp.concatenate([high, middle, low], axis=0)
    rank = lax.broadcasted_iota(jnp.int32, (capacity, tokens), 0)
    expert = lax.broadcasted_iota(jnp.int32, (n_exp, tokens), 0)
    onehot = jnp.concatenate(
        [jnp.where(rank == slot[k : k + 1, :], 1.0, 0.0).astype(jnp.bfloat16) for k in range(topk)], axis=1
    )
    parts = jnp.dot(split, onehot, preferred_element_type=jnp.float32)
    every = parts[:n_exp] + parts[n_exp : 2 * n_exp] + parts[2 * n_exp :]
    found = []
    for k in range(topk):
        mine = jnp.where(expert == choice[k : k + 1, :], every[:, k * tokens : (k + 1) * tokens], 0.0)
        found.append(jnp.sum(mine, axis=0, keepdims=True))
    held_weight[...] = jnp.where(live, jnp.concatenate(found, axis=0), 0.0)
    copies.append(pltpu.make_async_copy(held_weight, weight_ref, sems.at[1]))
    copies[-1].start()
    for copy in copies:
        copy.wait()


def weigh(far, cut, own, others, scales, weighted):
    capacity = own[0].shape[0]
    columns = cut[1] - cut[0]
    for half, pieces in enumerate((own, others)):
        shift = cut[0] if half == 0 else 0
        for m in range(far):
            at = pl.ds((half * far + m) * capacity, capacity)
            scale = jnp.broadcast_to(weights_of(scales[m : m + 1], half == 0), (capacity, LANES))
            for i in range(0, columns, LANES):
                weighted[at, i : i + LANES] = (
                    scale * pieces[m][:, shift + i : shift + i + LANES].astype(jnp.float32)
                ).astype(jnp.bfloat16)


def terms(tile, turned_ref, weighted, outs):
    for i in range(weighted.shape[1] // tile):
        lanes = pl.ds(i * tile, tile)
        for n, refs in outs:
            term = jnp.dot(turned_ref[n], weighted[:, lanes], preferred_element_type=jnp.float32)
            high = term.shape[0] // len(refs)
            for j, ref in enumerate(refs):
                ref[:, lanes] = term[j * high : (j + 1) * high].astype(ref.dtype)


def first_term_body(far, cut, tile, turned_ref, *refs):
    own, others, (send_ref, weighted) = refs[:far], refs[far : 2 * far], refs[2 * far :]
    weigh(far, cut, own, others, others, weighted)
    terms(tile, turned_ref, weighted, [(3, [send_ref])])


def more_terms_body(tile, shards, turned_ref, weighted, *refs):
    terms(tile, turned_ref, weighted, [(n, [ref]) for n, ref in zip(shards, refs)])


def term_body(far, cut, tile, turned_ref, *refs):
    own, others, scales, (own_ref, across_ref, send_ref, *send_across_refs, weighted) = (
        refs[:far], refs[far : 2 * far], refs[2 * far : 3 * far], refs[3 * far :]
    )
    weigh(far, cut, own, others, scales, weighted)
    outs = [(3, send_across_refs), (2, [across_ref]), (1, [send_ref]), (0, [own_ref])]
    terms(tile, turned_ref, weighted, outs)


def nt(a, b):
    return lax.dot_general(a, b, (((1,), (1,)), ((), ())), preferred_element_type=jnp.float32)


def finish(proj, weights, hidden, gate_factor, up_factor):
    part = proj * hidden.astype(jnp.float32)
    lanes = part[:, :LANES]
    for i in range(LANES, part.shape[1], LANES):
        lanes = lanes + part[:, i : i + LANES]
    score = jnp.sum(lanes.T, axis=0, keepdims=True)
    scaled = weights * proj
    gate = (gate_factor * scaled).astype(jnp.bfloat16)
    up = (up_factor * scaled).astype(jnp.bfloat16)
    return gate, up, score


def weights_of(refs, own):
    at = LANES // 2 if own else 0
    return jnp.concatenate(
        [r[:, r.shape[1] - LANES :][:, at : at + 1] for r in refs], axis=0
    ).astype(jnp.float32)


def project_own_body(far, *refs):
    shards, own, (weight_ref, proj_ref) = refs[:4], refs[4 : 4 + far], refs[4 + far :]
    data = lax.axis_index("edp")
    shard = shards[0].shape[0]
    for n in range(4):
        weight_ref[pl.ds(pl.multiple_of((data ^ n) * shard, 64), shard), :] = shards[n][...]
    proj_ref[...] = nt(jnp.concatenate([p[...] for p in own], axis=0), weight_ref[...])


def finish_half(first, far, proj, weights, hidden_ref, gate_factor_ref, up_factor_ref, held, then):
    here = lax.axis_index("exp")
    count = 2 * (proj.shape[0] // far)
    scores = []
    for m in range(0, far, 2):
        near = slice(m * count // 2, m * count // 2 + count)
        at = slice((first + m) * count // 2, (first + m) * count // 2 + count)
        gate, up, score = finish(
            proj[near], weights[near], hidden_ref[at, :], gate_factor_ref[at, :], up_factor_ref[at, :]
        )
        scores.append(score)
        for i in range(2):
            mine = slice(i * count // 2, (i + 1) * count // 2)
            within = pl.multiple_of(lax.rem(here ^ i, 2) * (count // 2), count // 2)
            there = pl.ds(m // 2 * count + within, count // 2)
            held[0, there, :] = gate[mine]
            held[1, there, :] = up[mine]
        then(m)
    return scores


def copies_out(first, m, far, held, outs, sems):
    count = 2 * (held.shape[1] // far)
    lower = pl.multiple_of(((lax.axis_index("exp") ^ (first + m)) // 2) * count, count)
    copies = []
    for i, out in enumerate(outs):
        source = held.at[i, pl.ds(m // 2 * count, count), :]
        copies.append(pltpu.make_async_copy(source, out.at[pl.ds(lower, count), :], sems.at[m // 2, i]))
        copies[-1].start()
    return copies


def project_far_body(far, cut, *refs):
    pieces, refs = refs[:far], refs[far:]
    weight_ref, own_proj_ref, hidden_ref, gate_factor_ref, up_factor_ref, *outs = refs
    proj_ref, gate_ref, up_ref, score_ref, held, sems = outs
    copies = []
    scores = finish_half(
        0, far, own_proj_ref[...], weights_of(pieces, True), hidden_ref, gate_factor_ref, up_factor_ref,
        held, lambda m: copies.extend(copies_out(0, m, far, held, (gate_ref, up_ref), sems)),
    )
    for i, score in enumerate(scores):
        score_ref[i : i + 1, :] = score
    rows = jnp.concatenate([p[:, : cut[1] - cut[0]] for p in pieces], axis=0)
    proj_ref[...] = nt(rows, weight_ref[:, cut[0] : cut[1]])
    for copy in copies:
        copy.wait()


def final_body(far, cut, *refs):
    pieces, scales, refs = refs[:far], refs[far : 2 * far], refs[2 * far :]
    (
        weight_ref, proj_ref, hidden_ref, gate_factor_ref, up_factor_ref, own_score_ref,
        score_ref, held,
    ) = refs
    here = lax.axis_index("exp")
    capacity = pieces[0].shape[0]
    rows = jnp.concatenate([p[...] for p in pieces], axis=0)
    proj = proj_ref[...] + nt(rows, weight_ref[:, cut[0] : cut[1]])
    scores = finish_half(
        far, far, proj, weights_of(scales, False), hidden_ref, gate_factor_ref, up_factor_ref,
        held, lambda m: None,
    )
    for m in range(0, far, 2):
        for first, score in ((far + m, scores[m // 2]), (m, own_score_ref[m // 2 : m // 2 + 1, :])):
            for i in range(2):
                score_ref[pl.ds(here ^ (first + i), 1), :] = score[:, i * capacity : (i + 1) * capacity]


def relayed(
    out_grad,
    combine,
    token_expert_choice,
    slots,
    counts,
    down_weight,
    stored_gate_preact,
    stored_up_preact,
):
    n_exp = lax.axis_size("exp")
    n_edp = lax.axis_size("edp")
    capacity = stored_gate_preact.shape[2] // n_exp
    units = stored_gate_preact.shape[3]
    rows = n_exp * capacity
    tok_rows, width = out_grad.shape
    topk = slots.shape[1]
    shard = units // n_edp
    far = n_exp // 2
    cuts = column_cuts(width)
    sizes = [b - a for a, b in cuts]
    splits = [1, 2]
    bf16, f32 = jnp.bfloat16, jnp.float32

    def shape(*dims, dtype=bf16):
        return jax.ShapeDtypeStruct(dims, dtype)

    def hop(x, axis, mask, after=None):
        if after is not None:
            x, _ = lax.optimization_barrier((x, after))
        return lax.ppermute(x, axis, flip(lax.axis_size(axis), mask))

    def spread(found):
        return [found[0]] + [hop(found[m], "exp", m) for m in range(1, far)]

    meta, *found = call(
        functools.partial(routing_body, capacity, n_exp),
        [shape(META_ROWS, LANES, dtype=f32)] + [shape(capacity, width)] * far,
        [BLOCK, BLOCK, BLOCK, SMEM, BLOCK],
        56,
        flops=2 * far * capacity * tok_rows * width,
        moved=out_grad.size * 4,
    )(token_expert_choice.T, slots.T, combine.T, counts, out_grad)
    raw = hop(out_grad, "exp", far)
    own = spread(found)
    hidden, gate_factor, up_factor, turned, meta = call(
        functools.partial(factors_body, capacity, n_edp),
        [
            shape(rows, units),
            shape(rows, units, dtype=f32),
            shape(rows, units, dtype=f32),
            shape(n_edp, shard, rows),
            shape(META_ROWS, LANES, dtype=f32),
        ],
        [VMEM] * 3,
        24,
        flops=40 * rows * units,
        moved=16 * rows * units,
        scratch=[pltpu.VMEM((units, rows), bf16)],
        after=[own[0]],
    )(stored_gate_preact[0, 0], stored_up_preact[0, 0], meta)
    weight_y = hop(down_weight[0], "edp", 2)
    far_meta = hop(meta, "exp", far, own[1])

    def term(k, others, scales, after=()):
        return call(
            functools.partial(term_body, far, cuts[k], 640),
            [shape(shard, sizes[k], dtype=f32)] * 2
            + [shape(shard, sizes[k])]
            + [shape(shard // splits[k], sizes[k])] * splits[k],
            [VMEM] * (1 + 3 * far),
            24,
            flops=2 * rows * units * sizes[k],
            moved=4 * (rows + units) * sizes[k],
            scratch=[pltpu.VMEM((rows, sizes[k]), bf16)],
            after=after,
        )(turned, *own, *others, *scales)

    def cores(send):
        return [hop(x, "edp", 1) for x in send]

    def across(k, mine, from_core, after=()):
        (sent,) = call(add_cores, [shape(shard, sizes[k])], [VMEM] * (1 + splits[k]), 8, after=after)(
            mine, *from_core
        )
        return sent, hop(sent, "edp", 2)

    found = call(
        functools.partial(select_first_body, capacity, topk, cuts[0]),
        [shape(capacity, sizes[0] + LANES)] * far,
        [VMEM] * 3,
        16,
        flops=2 * far * capacity * tok_rows * sizes[0],
        moved=4 * far * capacity * sizes[0],
        after=[*own[1:], hidden, weight_y],
    )(raw, far_meta, meta)
    far0 = spread(found)
    weight_core = hop(down_weight[0], "edp", 1, found[0])
    weight_both = hop(weight_y, "edp", 1, found[0])
    weight, own_proj = call(
        functools.partial(project_own_body, far),
        [shape(units, width), shape(far * capacity, units, dtype=f32)],
        [VMEM] * (4 + far),
        32,
    )(down_weight[0], weight_core, weight_y, weight_both, *own)
    first0, weighted = call(
        functools.partial(first_term_body, far, cuts[0], 640),
        [shape(shard, sizes[0]), shape(rows, sizes[0])],
        [VMEM] * (1 + 2 * far),
        24,
        after=[own_proj],
    )(turned, *own, *far0)
    first0 = hop(first0, "edp", 1)
    def more_terms(shards, outs, after=()):
        return call(
            functools.partial(more_terms_body, 640, shards), outs, [VMEM] * 2, 24, after=after
        )(turned, weighted)

    across0, send0 = more_terms([2, 1], [shape(shard, sizes[0], dtype=f32), shape(shard, sizes[0])])
    core0 = hop(send0, "edp", 1)
    sent0, from_y0 = across(0, across0, [first0])
    found = call(
        functools.partial(select_more_body, capacity, topk, cuts[1]),
        [shape(capacity, sizes[1])] * far,
        [VMEM] * 2,
        16,
        flops=2 * far * capacity * tok_rows * sizes[1],
        moved=4 * far * capacity * sizes[1],
        after=[sent0],
    )(raw, far_meta)
    far1 = spread(found)
    half_scratch = [
        pltpu.VMEM((2, far * capacity, units), bf16),
        pltpu.SemaphoreType.DMA((far // 2, 2)),
    ]
    proj, gate_preact_gradient, up_preact_gradient, own_score = call(
        functools.partial(project_far_body, far, cuts[0]),
        [
            shape(far * capacity, units, dtype=f32),
            shape(rows, units),
            shape(rows, units),
            shape(far // 2, 2 * capacity, dtype=f32),
        ],
        [VMEM] * (5 + far),
        24,
        scratch=half_scratch,
        after=[sent0, far1[0], core0],
        out_specs=[VMEM, ANY, ANY, VMEM],
    )(*far0, weight, own_proj, hidden, gate_factor, up_factor)
    (keep0,) = more_terms([0], [shape(shard, sizes[0], dtype=f32)], [proj])
    keep1, across1, *send1 = term(1, far1, far0, [keep0])
    core1 = cores(send1)
    score, far_half = call(
        functools.partial(final_body, far, cuts[1]),
        [shape(n_exp, capacity, dtype=f32), shape(2, far * capacity, units)],
        [VMEM] * (2 * far + 6),
        24,
        after=[keep1],
    )(*far1, *far0, weight, proj, hidden, gate_factor, up_factor, own_score)
    _, from_y1 = across(1, across1, core1[1:], [score, core1[0]])
    returned = lax.all_to_all(score, "exp", split_axis=0, concat_axis=0)
    down_matrix_gradient, combine_weight_gradient, gate_preact_gradient, up_preact_gradient = call(
        functools.partial(returned_body, capacity, n_exp, cuts[0]),
        [shape(shard, width), shape(topk, tok_rows, dtype=f32), shape(rows, units), shape(rows, units)],
        [VMEM, VMEM, SMEM] + [VMEM] * 5 + [ANY] * 2,
        16,
        scratch=[
            pltpu.VMEM((shard, sizes[0]), bf16),
            pltpu.VMEM((topk, tok_rows), f32),
            pltpu.SemaphoreType.DMA((2,)),
            half_scratch[1],
        ],
        out_specs=[ANY] * 4,
        aliases=[(8, 2), (9, 3)],
    )(
        token_expert_choice.T, slots.T, counts, returned, far_half, keep0, core0, from_y0,
        gate_preact_gradient, up_preact_gradient,
    )
    (down_matrix_gradient,) = call(
        functools.partial(last_body, cuts[1]),
        [shape(shard, width)],
        [VMEM] * 3 + [ANY],
        8,
        scratch=[pltpu.VMEM((shard, sizes[1]), bf16), pltpu.SemaphoreType.DMA],
        out_specs=[ANY],
        aliases=[(3, 0)],
    )(keep1, core1[0], from_y1, down_matrix_gradient)
    return (
        gate_preact_gradient[None, None],
        up_preact_gradient[None, None],
        down_matrix_gradient[None],
        combine_weight_gradient.T,
    )


def direct(
    out_grad,
    combine,
    token_expert_choice,
    slots,
    counts,
    down_weight,
    stored_gate_preact,
    stored_up_preact,
):
    experts_here = lax.axis_size("exp")
    capacity = stored_gate_preact.shape[2] // experts_here
    tok_rows = out_grad.shape[0]
    model_width = out_grad.shape[1]
    slot_index = jnp.where(
        slots < capacity, token_expert_choice * capacity + slots, experts_here * capacity
    )
    flat_index = slot_index.reshape(-1)
    row_ids = jnp.broadcast_to(
        jnp.arange(tok_rows, dtype=jnp.int32)[:, None] + 1, slot_index.shape
    ).reshape(-1)
    sender_rows = (
        jnp.zeros((experts_here * capacity,), jnp.int32).at[flat_index].set(row_ids, mode="drop")
    )
    padded_grad = jnp.concatenate([jnp.zeros((1, model_width), out_grad.dtype), out_grad], axis=0)
    send_grad = padded_grad[sender_rows].reshape(experts_here, capacity, model_width)
    send_weight = (
        jnp.zeros((experts_here * capacity,), combine.dtype)
        .at[flat_index]
        .set(combine.reshape(-1), mode="drop")
    )
    send_weight = send_weight.reshape(experts_here, capacity)
    send_count = counts.reshape(experts_here, 1)
    recv_grad, received_weight, recv_count = (
        lax.all_to_all(send_grad, "exp", split_axis=0, concat_axis=0, tiled=True),
        lax.all_to_all(send_weight, "exp", split_axis=0, concat_axis=0, tiled=True),
        lax.all_to_all(send_count, "exp", split_axis=0, concat_axis=0, tiled=True),
    )
    live_mask = (jnp.arange(capacity, dtype=jnp.int32)[None, :] < recv_count).astype(jnp.float32)
    scaled = (live_mask * received_weight.astype(jnp.float32)).reshape(-1)
    live_rows = live_mask.reshape(-1)
    grad_rows = recv_grad.reshape(-1, model_width)
    proj = lax.dot_general(
        grad_rows,
        lax.all_gather(down_weight, "edp", axis=1, tiled=True)[0],
        (((1,), (1,)), ((), ())),
        preferred_element_type=jnp.float32,
    )
    gate_pre = stored_gate_preact[0, 0].astype(jnp.float32)
    up_pre = stored_up_preact[0, 0].astype(jnp.float32)
    sigmoid_gate = jax.nn.sigmoid(gate_pre)
    silu_gate = gate_pre * sigmoid_gate
    hidden = (silu_gate * up_pre).astype(jnp.bfloat16)
    weighted = (scaled[:, None] * grad_rows.astype(jnp.float32)).astype(jnp.bfloat16)
    grad_hidden = scaled[:, None] * proj
    gate_preact_gradient = (
        grad_hidden * up_pre * sigmoid_gate * (1.0 + gate_pre * (1.0 - sigmoid_gate))
    ).astype(jnp.bfloat16)
    up_preact_gradient = (grad_hidden * silu_gate).astype(jnp.bfloat16)
    score = (live_rows * jnp.sum(proj * hidden.astype(jnp.float32), axis=1)).reshape(
        experts_here, capacity
    )
    returned_scores = lax.all_to_all(score, "exp", split_axis=0, concat_axis=0, tiled=True)
    summed = lax.psum_scatter(
        lax.dot_general(
            hidden, weighted, (((0,), (0,)), ((), ())), preferred_element_type=jnp.float32
        ),
        "edp",
        scatter_dimension=0,
        tiled=True,
    )
    returned = jnp.concatenate([returned_scores.reshape(-1), jnp.zeros((1,), jnp.float32)])
    combine_weight_gradient = returned[slot_index]
    down_matrix_gradient = summed.astype(jnp.bfloat16)[None]
    return (
        gate_preact_gradient[None, None],
        up_preact_gradient[None, None],
        down_matrix_gradient,
        combine_weight_gradient,
    )


def solution(mesh):
    n_exp, n_edp = mesh.shape["exp"], mesh.shape["edp"]

    def on_device(*arrays):
        tok_rows = arrays[0].shape[0]
        capacity = arrays[6].shape[2] // n_exp
        if n_exp == 8 and n_edp == 4 and tok_rows == LANES and tok_rows <= 2 * capacity:
            return relayed(*arrays)
        return direct(*arrays)

    return jax.shard_map(
        on_device,
        mesh=mesh,
        in_specs=(
            P(("exp", "edp"), None),
            P(("exp", "edp"), None),
            P(("exp", "edp"), None),
            P(("exp", "edp"), None),
            P(("exp", "edp"), None),
            P("exp", "edp", None),
            P("exp", "edp", None, None),
            P("exp", "edp", None, None),
        ),
        out_specs=(
            P("exp", "edp", None, None),
            P("exp", "edp", None, None),
            P("exp", "edp", None),
            P(("exp", "edp"), None),
        ),
        check_vma=False,
    )
```

```python
import functools

import jax
import jax.numpy as jnp
from jax import lax
from jax.experimental import pallas as pl
from jax.experimental.pallas import tpu as pltpu
from jax.sharding import PartitionSpec as P


def flip(n, mask):
    return [(i, i ^ mask) for i in range(n)]


def column_cuts(width):
    unit = width // 20
    return [(0, 15 * unit), (15 * unit, width)]


VMEM = pl.BlockSpec(memory_space=pltpu.VMEM)
SMEM = pl.BlockSpec(memory_space=pltpu.SMEM)
BLOCK = pl.BlockSpec()
ANY = pl.BlockSpec(memory_space=pl.ANY)
LANES = 128
CODE, WEIGHT, LIVE, META_ROWS = 0, 8, 16, 24


def call(body, outs, specs, megabytes, flops=0, moved=0, scratch=(), after=(), out_specs=None, aliases=()):
    def ordered(*refs):
        body(*refs[len(after) :])

    kernel = pl.pallas_call(
        ordered,
        out_shape=outs,
        in_specs=[ANY] * len(after) + list(specs),
        out_specs=out_specs or [VMEM] * len(outs),
        scratch_shapes=scratch,
        input_output_aliases={len(after) + i: o for i, o in aliases},
        compiler_params=pltpu.CompilerParams(vmem_limit_bytes=megabytes * 1024 * 1024),
        cost_estimate=pl.CostEstimate(flops=flops, bytes_accessed=moved, transcendentals=0),
    )
    return functools.partial(kernel, *after)


def routing_body(
    capacity, n_exp, far, choice_ref, slot_ref, combine_ref, counts_ref, tok_ref, meta_ref, *outs
):
    topk = choice_ref.shape[0]
    choice = choice_ref[...]
    slot = slot_ref[...]
    limit = jnp.zeros_like(slot)
    for expert in range(n_exp):
        limit = jnp.where(choice == expert, counts_ref[0, expert], limit)
    kept = slot < capacity
    live = kept & (slot < limit)
    meta_ref[...] = jnp.zeros_like(meta_ref)
    meta_ref[CODE : CODE + topk, :] = jnp.where(kept, choice * capacity + slot, -1).astype(jnp.float32)
    meta_ref[WEIGHT : WEIGHT + topk, :] = jnp.where(live, combine_ref[...].astype(jnp.float32), 0.0)
    meta_ref[LIVE : LIVE + topk, :] = jnp.where(live, 1.0, 0.0)
    select(capacity, topk, meta_ref, tok_ref[...], outs, first=far - len(outs))


def places(target, capacity):
    return (lax.broadcasted_iota(jnp.int32, (capacity, LANES), 0) + target).astype(jnp.float32)


def pick(meta, topk, want):
    hit = meta[CODE : CODE + 1, :] == want
    for k in range(1, topk):
        hit = hit | (meta[CODE + k : CODE + k + 1, :] == want)
    return jnp.where(hit, 1.0, 0.0)


def weight_of(meta, topk, want):
    weight = jnp.zeros(want.shape, jnp.float32)
    for k in range(topk):
        weight = jnp.where(
            meta[CODE + k : CODE + k + 1, :] == want, meta[WEIGHT + k : WEIGHT + k + 1, :], weight
        )
    return jnp.sum(weight, axis=1, keepdims=True)


def select(capacity, topk, meta, rows, outs, own_meta=None, first=0):
    here = lax.axis_index("exp")
    columns = rows.shape[1]
    wants = [places((here ^ (first + m)) * capacity, capacity) for m in range(len(outs))]
    onehot = jnp.concatenate([pick(meta, topk, w) for w in wants], axis=0).astype(jnp.bfloat16)
    chosen = jnp.dot(onehot, rows, preferred_element_type=jnp.float32).astype(jnp.bfloat16)
    for m, out in enumerate(outs):
        out[:, :columns] = chosen[m * capacity : (m + 1) * capacity]
        if own_meta is not None:
            lane = lax.broadcasted_iota(jnp.int32, (capacity, LANES), 1)
            weight, own_weight = (weight_of(x, topk, wants[m]) for x in (meta, own_meta))
            out[:, columns:] = jnp.where(lane < LANES // 2, weight, own_weight).astype(jnp.bfloat16)


def select_own_body(capacity, topk, meta_ref, tok_ref, *outs):
    select(capacity, topk, meta_ref, tok_ref[...], outs)


def select_first_body(capacity, topk, cut, raw_ref, meta_ref, own_meta_ref, *outs):
    select(capacity, topk, meta_ref, raw_ref[:, cut[0] : cut[1]], outs, own_meta_ref)


def select_more_body(capacity, topk, cut, raw_ref, meta_ref, *outs):
    select(capacity, topk, meta_ref, raw_ref[:, cut[0] : cut[1]], outs)


def source_rows(capacity, n):
    source = lax.axis_index("exp") ^ n
    return pl.ds(pl.multiple_of(source * capacity, capacity), capacity)


def factors_body(
    capacity, n_edp, gate_ref, up_ref, meta_ref, shard_ref,
    hidden_ref, gate_factor_ref, up_factor_ref, turned_ref, meta_out_ref, shard_out_ref, scratch,
):
    data = lax.axis_index("edp")
    rows, units = gate_ref.shape
    shard = units // n_edp
    for n in range(rows // capacity):
        at = pl.ds(n * capacity, capacity)
        there = source_rows(capacity, n)
        gate_pre = gate_ref[there, :].astype(jnp.float32)
        up_pre = up_ref[there, :].astype(jnp.float32)
        sigmoid_gate = jax.nn.sigmoid(gate_pre)
        silu_gate = gate_pre * sigmoid_gate
        hidden_ref[at, :] = (silu_gate * up_pre).astype(jnp.bfloat16)
        gate_factor_ref[at, :] = up_pre * sigmoid_gate * (1.0 + gate_pre * (1.0 - sigmoid_gate))
        up_factor_ref[at, :] = silu_gate
    meta_out_ref[...] = meta_ref[...]
    shard_out_ref[...] = shard_ref[...]
    scratch[...] = hidden_ref[...].T
    for n in range(n_edp):
        turned_ref[n] = scratch[pl.ds(pl.multiple_of((data ^ n) * shard, 64), shard), :]


def add_cores(across_ref, *refs):
    *from_core, sum_ref = refs
    start = 0
    for ref in from_core:
        rows = pl.ds(start, ref.shape[0])
        start += ref.shape[0]
        sum_ref[rows, :] = (across_ref[rows, :] + ref[...].astype(jnp.float32)).astype(jnp.bfloat16)


def summed_out(cut, sums, out_ref, held, sem):
    keep_ref, from_core_ref, from_y_ref = sums
    held[...] = (
        keep_ref[...] + from_core_ref[...].astype(jnp.float32) + from_y_ref[...].astype(jnp.float32)
    ).astype(jnp.bfloat16)
    copy = pltpu.make_async_copy(held, out_ref.at[:, pl.ds(cut[0], cut[1] - cut[0])], sem)
    copy.start()
    return copy


def last_body(cut, *refs):
    *sums, _, out_ref, held, sem = refs
    summed_out(cut, sums, out_ref, held, sem).wait()


def returned_body(capacity, n_exp, cut, choice_ref, slot_ref, meta_ref, score_ref, far_half_ref, *refs):
    sums, refs = refs[:3], refs[5:]
    out_ref, weight_ref, gate_ref, up_ref, held, held_weight, sems, half_sems = refs
    far = n_exp // 2
    copies = []
    for m in range(0, far, 2):
        copies += copies_out(far, m, far, far_half_ref, (gate_ref, up_ref), half_sems)
    copies.append(summed_out(cut, sums, out_ref, held, sems.at[0]))
    topk, tokens = choice_ref.shape
    choice = choice_ref[...]
    slot = slot_ref[...]
    live = meta_ref[LIVE : LIVE + topk, :] > 0.0
    table = score_ref[...]
    high = table.astype(jnp.bfloat16)
    rest = table - high.astype(jnp.float32)
    middle = rest.astype(jnp.bfloat16)
    low = (rest - middle.astype(jnp.float32)).astype(jnp.bfloat16)
    split = jnp.concatenate([high, middle, low], axis=0)
    rank = lax.broadcasted_iota(jnp.int32, (capacity, tokens), 0)
    expert = lax.broadcasted_iota(jnp.int32, (n_exp, tokens), 0)
    onehot = jnp.concatenate(
        [jnp.where(rank == slot[k : k + 1, :], 1.0, 0.0).astype(jnp.bfloat16) for k in range(topk)], axis=1
    )
    parts = jnp.dot(split, onehot, preferred_element_type=jnp.float32)
    every = parts[:n_exp] + parts[n_exp : 2 * n_exp] + parts[2 * n_exp :]
    found = []
    for k in range(topk):
        mine = jnp.where(expert == choice[k : k + 1, :], every[:, k * tokens : (k + 1) * tokens], 0.0)
        found.append(jnp.sum(mine, axis=0, keepdims=True))
    held_weight[...] = jnp.where(live, jnp.concatenate(found, axis=0), 0.0)
    copies.append(pltpu.make_async_copy(held_weight, weight_ref, sems.at[1]))
    copies[-1].start()
    for copy in copies:
        copy.wait()


def weigh(far, cut, own, others, scales, weighted):
    capacity = own[0].shape[0]
    columns = cut[1] - cut[0]
    for half, pieces in enumerate((own, others)):
        shift = cut[0] if half == 0 else 0
        for m in range(far):
            at = pl.ds((half * far + m) * capacity, capacity)
            scale = jnp.broadcast_to(weights_of(scales[m : m + 1], half == 0), (capacity, LANES))
            for i in range(0, columns, LANES):
                weighted[at, i : i + LANES] = (
                    scale * pieces[m][:, shift + i : shift + i + LANES].astype(jnp.float32)
                ).astype(jnp.bfloat16)


def terms(tile, turned_ref, weighted, outs):
    for i in range(weighted.shape[1] // tile):
        lanes = pl.ds(i * tile, tile)
        for n, refs in outs:
            term = jnp.dot(turned_ref[n], weighted[:, lanes], preferred_element_type=jnp.float32)
            high = term.shape[0] // len(refs)
            for j, ref in enumerate(refs):
                ref[:, lanes] = term[j * high : (j + 1) * high].astype(ref.dtype)


def first_term_body(far, cut, tile, turned_ref, *refs):
    own, others, (send_ref, weighted) = refs[:far], refs[far : 2 * far], refs[2 * far :]
    weigh(far, cut, own, others, others, weighted)
    terms(tile, turned_ref, weighted, [(3, [send_ref])])


def more_terms_body(tile, shards, turned_ref, weighted, *refs):
    terms(tile, turned_ref, weighted, [(n, [ref]) for n, ref in zip(shards, refs)])


def term_body(far, cut, tile, turned_ref, *refs):
    own, others, scales, (own_ref, across_ref, send_ref, *send_across_refs, weighted) = (
        refs[:far], refs[far : 2 * far], refs[2 * far : 3 * far], refs[3 * far :]
    )
    weigh(far, cut, own, others, scales, weighted)
    outs = [(3, send_across_refs), (2, [across_ref]), (1, [send_ref]), (0, [own_ref])]
    terms(tile, turned_ref, weighted, outs)


def nt(a, b):
    return lax.dot_general(a, b, (((1,), (1,)), ((), ())), preferred_element_type=jnp.float32)


def finish(proj, weights, hidden, gate_factor, up_factor):
    part = proj * hidden.astype(jnp.float32)
    lanes = part[:, :LANES]
    for i in range(LANES, part.shape[1], LANES):
        lanes = lanes + part[:, i : i + LANES]
    score = jnp.sum(lanes.T, axis=0, keepdims=True)
    scaled = weights * proj
    gate = (gate_factor * scaled).astype(jnp.bfloat16)
    up = (up_factor * scaled).astype(jnp.bfloat16)
    return gate, up, score


def weights_of(refs, own):
    at = LANES // 2 if own else 0
    return jnp.concatenate(
        [r[:, r.shape[1] - LANES :][:, at : at + 1] for r in refs], axis=0
    ).astype(jnp.float32)


def project_own_body(far, *refs):
    shards, own, (weight_ref, proj_ref) = refs[:4], refs[4 : 4 + far], refs[4 + far :]
    data = lax.axis_index("edp")
    shard = shards[0].shape[0]
    for n in range(4):
        weight_ref[pl.ds(pl.multiple_of((data ^ n) * shard, 64), shard), :] = shards[n][...]
    proj_ref[...] = nt(jnp.concatenate([p[...] for p in own], axis=0), weight_ref[...])


def finish_half(first, far, proj, weights, hidden_ref, gate_factor_ref, up_factor_ref, held, then):
    here = lax.axis_index("exp")
    count = 2 * (proj.shape[0] // far)
    scores = []
    for m in range(0, far, 2):
        near = slice(m * count // 2, m * count // 2 + count)
        at = slice((first + m) * count // 2, (first + m) * count // 2 + count)
        gate, up, score = finish(
            proj[near], weights[near], hidden_ref[at, :], gate_factor_ref[at, :], up_factor_ref[at, :]
        )
        scores.append(score)
        for i in range(2):
            mine = slice(i * count // 2, (i + 1) * count // 2)
            within = pl.multiple_of(lax.rem(here ^ i, 2) * (count // 2), count // 2)
            there = pl.ds(m // 2 * count + within, count // 2)
            held[0, there, :] = gate[mine]
            held[1, there, :] = up[mine]
        then(m)
    return scores


def copies_out(first, m, far, held, outs, sems):
    count = 2 * (held.shape[1] // far)
    lower = pl.multiple_of(((lax.axis_index("exp") ^ (first + m)) // 2) * count, count)
    copies = []
    for i, out in enumerate(outs):
        source = held.at[i, pl.ds(m // 2 * count, count), :]
        copies.append(pltpu.make_async_copy(source, out.at[pl.ds(lower, count), :], sems.at[m // 2, i]))
        copies[-1].start()
    return copies


def project_far_body(far, cut, *refs):
    pieces, refs = refs[:far], refs[far:]
    weight_ref, own_proj_ref, hidden_ref, gate_factor_ref, up_factor_ref, *outs = refs
    proj_ref, gate_ref, up_ref, score_ref, held, sems = outs
    copies = []
    scores = finish_half(
        0, far, own_proj_ref[...], weights_of(pieces, True), hidden_ref, gate_factor_ref, up_factor_ref,
        held, lambda m: copies.extend(copies_out(0, m, far, held, (gate_ref, up_ref), sems)),
    )
    for i, score in enumerate(scores):
        score_ref[i : i + 1, :] = score
    rows = jnp.concatenate([p[:, : cut[1] - cut[0]] for p in pieces], axis=0)
    proj_ref[...] = nt(rows, weight_ref[:, cut[0] : cut[1]])
    for copy in copies:
        copy.wait()


def final_body(far, cut, *refs):
    pieces, scales, refs = refs[:far], refs[far : 2 * far], refs[2 * far :]
    (
        weight_ref, proj_ref, hidden_ref, gate_factor_ref, up_factor_ref, own_score_ref,
        score_ref, held,
    ) = refs
    here = lax.axis_index("exp")
    capacity = pieces[0].shape[0]
    rows = jnp.concatenate([p[...] for p in pieces], axis=0)
    proj = proj_ref[...] + nt(rows, weight_ref[:, cut[0] : cut[1]])
    scores = finish_half(
        far, far, proj, weights_of(scales, False), hidden_ref, gate_factor_ref, up_factor_ref,
        held, lambda m: None,
    )
    for m in range(0, far, 2):
        for first, score in ((far + m, scores[m // 2]), (m, own_score_ref[m // 2 : m // 2 + 1, :])):
            for i in range(2):
                score_ref[pl.ds(here ^ (first + i), 1), :] = score[:, i * capacity : (i + 1) * capacity]


def relayed(
    out_grad,
    combine,
    token_expert_choice,
    slots,
    counts,
    down_weight,
    stored_gate_preact,
    stored_up_preact,
):
    n_exp = lax.axis_size("exp")
    n_edp = lax.axis_size("edp")
    capacity = stored_gate_preact.shape[2] // n_exp
    units = stored_gate_preact.shape[3]
    rows = n_exp * capacity
    tok_rows, width = out_grad.shape
    topk = slots.shape[1]
    shard = units // n_edp
    far = n_exp // 2
    cuts = column_cuts(width)
    sizes = [b - a for a, b in cuts]
    splits = [1, 2]
    bf16, f32 = jnp.bfloat16, jnp.float32

    def shape(*dims, dtype=bf16):
        return jax.ShapeDtypeStruct(dims, dtype)

    def hop(x, axis, mask, after=None):
        if after is not None:
            x, _ = lax.optimization_barrier((x, after))
        return lax.ppermute(x, axis, flip(lax.axis_size(axis), mask))

    def spread(found):
        return [found[0]] + [hop(found[m], "exp", m) for m in range(1, far)]

    meta, *found = call(
        functools.partial(routing_body, capacity, n_exp, far),
        [shape(META_ROWS, LANES, dtype=f32)] + [shape(capacity, width)] * (far // 2),
        [BLOCK, BLOCK, BLOCK, SMEM, BLOCK],
        56,
        flops=2 * far * capacity * tok_rows * width,
        moved=out_grad.size * 4,
    )(token_expert_choice.T, slots.T, combine.T, counts, out_grad)
    raw = hop(out_grad, "exp", far)
    own = [hop(x, "exp", far // 2 + m) for m, x in enumerate(found)]
    hidden, gate_factor, up_factor, turned, meta, weight_here = call(
        functools.partial(factors_body, capacity, n_edp),
        [
            shape(rows, units),
            shape(rows, units, dtype=f32),
            shape(rows, units, dtype=f32),
            shape(n_edp, shard, rows),
            shape(META_ROWS, LANES, dtype=f32),
            shape(shard, width),
        ],
        [VMEM] * 4,
        24,
        flops=40 * rows * units,
        moved=16 * rows * units,
        scratch=[pltpu.VMEM((units, rows), bf16)],
    )(stored_gate_preact[0, 0], stored_up_preact[0, 0], meta, down_weight[0])
    weight_y = hop(down_weight[0], "edp", 2)
    far_meta = hop(meta, "exp", far, own[0])

    found = call(
        functools.partial(select_own_body, capacity, topk),
        [shape(capacity, width)] * (far // 2),
        [VMEM] * 2,
        16,
        after=[hidden],
    )(meta, out_grad)
    own = [found[0]] + [hop(found[m], "exp", m) for m in range(1, far // 2)] + own

    def term(k, others, scales, after=()):
        return call(
            functools.partial(term_body, far, cuts[k], 640),
            [shape(shard, sizes[k], dtype=f32)] * 2
            + [shape(shard, sizes[k])]
            + [shape(shard // splits[k], sizes[k])] * splits[k],
            [VMEM] * (1 + 3 * far),
            24,
            flops=2 * rows * units * sizes[k],
            moved=4 * (rows + units) * sizes[k],
            scratch=[pltpu.VMEM((rows, sizes[k]), bf16)],
            after=after,
        )(turned, *own, *others, *scales)

    def cores(send):
        return [hop(x, "edp", 1) for x in send]

    def across(k, mine, from_core, after=()):
        (sent,) = call(add_cores, [shape(shard, sizes[k])], [VMEM] * (1 + splits[k]), 8, after=after)(
            mine, *from_core
        )
        return sent, hop(sent, "edp", 2)

    found = call(
        functools.partial(select_first_body, capacity, topk, cuts[0]),
        [shape(capacity, sizes[0] + LANES)] * far,
        [VMEM] * 3,
        16,
        flops=2 * far * capacity * tok_rows * sizes[0],
        moved=4 * far * capacity * sizes[0],
        after=[*own[1:], hidden, weight_y],
    )(raw, far_meta, meta)
    far0 = spread(found)
    weight_core = hop(weight_here, "edp", 1, own[far - 1])
    weight_both = hop(weight_y, "edp", 1, found[0])
    weight, own_proj = call(
        functools.partial(project_own_body, far),
        [shape(units, width), shape(far * capacity, units, dtype=f32)],
        [VMEM] * (4 + far),
        32,
    )(weight_here, weight_core, weight_y, weight_both, *own)
    first0, weighted = call(
        functools.partial(first_term_body, far, cuts[0], 640),
        [shape(shard, sizes[0]), shape(rows, sizes[0])],
        [VMEM] * (1 + 2 * far),
        24,
        after=[own_proj],
    )(turned, *own, *far0)
    first0 = hop(first0, "edp", 1)
    def more_terms(shards, outs, after=()):
        return call(
            functools.partial(more_terms_body, 640, shards), outs, [VMEM] * 2, 24, after=after
        )(turned, weighted)

    across0, send0 = more_terms([2, 1], [shape(shard, sizes[0], dtype=f32), shape(shard, sizes[0])])
    core0 = hop(send0, "edp", 1)
    sent0, from_y0 = across(0, across0, [first0])
    found = call(
        functools.partial(select_more_body, capacity, topk, cuts[1]),
        [shape(capacity, sizes[1])] * far,
        [VMEM] * 2,
        16,
        flops=2 * far * capacity * tok_rows * sizes[1],
        moved=4 * far * capacity * sizes[1],
        after=[sent0],
    )(raw, far_meta)
    far1 = spread(found)
    half_scratch = [
        pltpu.VMEM((2, far * capacity, units), bf16),
        pltpu.SemaphoreType.DMA((far // 2, 2)),
    ]
    proj, gate_preact_gradient, up_preact_gradient, own_score = call(
        functools.partial(project_far_body, far, cuts[0]),
        [
            shape(far * capacity, units, dtype=f32),
            shape(rows, units),
            shape(rows, units),
            shape(far // 2, 2 * capacity, dtype=f32),
        ],
        [VMEM] * (5 + far),
        24,
        scratch=half_scratch,
        after=[sent0, far1[0], core0],
        out_specs=[VMEM, ANY, ANY, VMEM],
    )(*far0, weight, own_proj, hidden, gate_factor, up_factor)
    (keep0,) = more_terms([0], [shape(shard, sizes[0], dtype=f32)], [proj])
    keep1, across1, *send1 = term(1, far1, far0, [keep0])
    core1 = cores(send1)
    score, far_half = call(
        functools.partial(final_body, far, cuts[1]),
        [shape(n_exp, capacity, dtype=f32), shape(2, far * capacity, units)],
        [VMEM] * (2 * far + 6),
        24,
        after=[keep1],
    )(*far1, *far0, weight, proj, hidden, gate_factor, up_factor, own_score)
    _, from_y1 = across(1, across1, core1[1:], [score, core1[0]])
    returned = lax.all_to_all(score, "exp", split_axis=0, concat_axis=0)
    down_matrix_gradient, combine_weight_gradient, gate_preact_gradient, up_preact_gradient = call(
        functools.partial(returned_body, capacity, n_exp, cuts[0]),
        [shape(shard, width), shape(topk, tok_rows, dtype=f32), shape(rows, units), shape(rows, units)],
        [VMEM] * 8 + [ANY] * 2,
        16,
        scratch=[
            pltpu.VMEM((shard, sizes[0]), bf16),
            pltpu.VMEM((topk, tok_rows), f32),
            pltpu.SemaphoreType.DMA((2,)),
            half_scratch[1],
        ],
        out_specs=[ANY] * 4,
        aliases=[(8, 2), (9, 3)],
    )(
        token_expert_choice.T, slots.T, meta, returned, far_half, keep0, core0, from_y0,
        gate_preact_gradient, up_preact_gradient,
    )
    (down_matrix_gradient,) = call(
        functools.partial(last_body, cuts[1]),
        [shape(shard, width)],
        [VMEM] * 3 + [ANY],
        8,
        scratch=[pltpu.VMEM((shard, sizes[1]), bf16), pltpu.SemaphoreType.DMA],
        out_specs=[ANY],
        aliases=[(3, 0)],
    )(keep1, core1[0], from_y1, down_matrix_gradient)
    return (
        gate_preact_gradient[None, None],
        up_preact_gradient[None, None],
        down_matrix_gradient[None],
        combine_weight_gradient.T,
    )


def direct(
    out_grad,
    combine,
    token_expert_choice,
    slots,
    counts,
    down_weight,
    stored_gate_preact,
    stored_up_preact,
):
    experts_here = lax.axis_size("exp")
    capacity = stored_gate_preact.shape[2] // experts_here
    tok_rows = out_grad.shape[0]
    model_width = out_grad.shape[1]
    slot_index = jnp.where(
        slots < capacity, token_expert_choice * capacity + slots, experts_here * capacity
    )
    flat_index = slot_index.reshape(-1)
    row_ids = jnp.broadcast_to(
        jnp.arange(tok_rows, dtype=jnp.int32)[:, None] + 1, slot_index.shape
    ).reshape(-1)
    sender_rows = (
        jnp.zeros((experts_here * capacity,), jnp.int32).at[flat_index].set(row_ids, mode="drop")
    )
    padded_grad = jnp.concatenate([jnp.zeros((1, model_width), out_grad.dtype), out_grad], axis=0)
    send_grad = padded_grad[sender_rows].reshape(experts_here, capacity, model_width)
    send_weight = (
        jnp.zeros((experts_here * capacity,), combine.dtype)
        .at[flat_index]
        .set(combine.reshape(-1), mode="drop")
    )
    send_weight = send_weight.reshape(experts_here, capacity)
    send_count = counts.reshape(experts_here, 1)
    recv_grad, received_weight, recv_count = (
        lax.all_to_all(send_grad, "exp", split_axis=0, concat_axis=0, tiled=True),
        lax.all_to_all(send_weight, "exp", split_axis=0, concat_axis=0, tiled=True),
        lax.all_to_all(send_count, "exp", split_axis=0, concat_axis=0, tiled=True),
    )
    live_mask = (jnp.arange(capacity, dtype=jnp.int32)[None, :] < recv_count).astype(jnp.float32)
    scaled = (live_mask * received_weight.astype(jnp.float32)).reshape(-1)
    live_rows = live_mask.reshape(-1)
    grad_rows = recv_grad.reshape(-1, model_width)
    proj = lax.dot_general(
        grad_rows,
        lax.all_gather(down_weight, "edp", axis=1, tiled=True)[0],
        (((1,), (1,)), ((), ())),
        preferred_element_type=jnp.float32,
    )
    gate_pre = stored_gate_preact[0, 0].astype(jnp.float32)
    up_pre = stored_up_preact[0, 0].astype(jnp.float32)
    sigmoid_gate = jax.nn.sigmoid(gate_pre)
    silu_gate = gate_pre * sigmoid_gate
    hidden = (silu_gate * up_pre).astype(jnp.bfloat16)
    weighted = (scaled[:, None] * grad_rows.astype(jnp.float32)).astype(jnp.bfloat16)
    grad_hidden = scaled[:, None] * proj
    gate_preact_gradient = (
        grad_hidden * up_pre * sigmoid_gate * (1.0 + gate_pre * (1.0 - sigmoid_gate))
    ).astype(jnp.bfloat16)
    up_preact_gradient = (grad_hidden * silu_gate).astype(jnp.bfloat16)
    score = (live_rows * jnp.sum(proj * hidden.astype(jnp.float32), axis=1)).reshape(
        experts_here, capacity
    )
    returned_scores = lax.all_to_all(score, "exp", split_axis=0, concat_axis=0, tiled=True)
    summed = lax.psum_scatter(
        lax.dot_general(
            hidden, weighted, (((0,), (0,)), ((), ())), preferred_element_type=jnp.float32
        ),
        "edp",
        scatter_dimension=0,
        tiled=True,
    )
    returned = jnp.concatenate([returned_scores.reshape(-1), jnp.zeros((1,), jnp.float32)])
    combine_weight_gradient = returned[slot_index]
    down_matrix_gradient = summed.astype(jnp.bfloat16)[None]
    return (
        gate_preact_gradient[None, None],
        up_preact_gradient[None, None],
        down_matrix_gradient,
        combine_weight_gradient,
    )


def solution(mesh):
    n_exp, n_edp = mesh.shape["exp"], mesh.shape["edp"]

    def on_device(*arrays):
        tok_rows = arrays[0].shape[0]
        capacity = arrays[6].shape[2] // n_exp
        if n_exp == 8 and n_edp == 4 and tok_rows == LANES and tok_rows <= 2 * capacity:
            return relayed(*arrays)
        return direct(*arrays)

    return jax.shard_map(
        on_device,
        mesh=mesh,
        in_specs=(
            P(("exp", "edp"), None),
            P(("exp", "edp"), None),
            P(("exp", "edp"), None),
            P(("exp", "edp"), None),
            P(("exp", "edp"), None),
            P("exp", "edp", None),
            P("exp", "edp", None, None),
            P("exp", "edp", None, None),
        ),
        out_specs=(
            P("exp", "edp", None, None),
            P("exp", "edp", None, None),
            P("exp", "edp", None),
            P(("exp", "edp"), None),
        ),
        check_vma=False,
    )
```

```python
import functools

import jax
import jax.numpy as jnp
from jax import lax
from jax.experimental import pallas as pl
from jax.experimental.pallas import tpu as pltpu
from jax.sharding import PartitionSpec as P


def flip(n, mask):
    return [(i, i ^ mask) for i in range(n)]


def column_cuts(width):
    unit = width // 20
    return [(0, 15 * unit), (15 * unit, width)]


VMEM = pl.BlockSpec(memory_space=pltpu.VMEM)
SMEM = pl.BlockSpec(memory_space=pltpu.SMEM)
BLOCK = pl.BlockSpec()
ANY = pl.BlockSpec(memory_space=pl.ANY)
LANES = 128
CODE, WEIGHT, LIVE, META_ROWS = 0, 8, 16, 24


def call(body, outs, specs, megabytes, flops=0, moved=0, scratch=(), after=(), out_specs=None, aliases=()):
    def ordered(*refs):
        body(*refs[len(after) :])

    kernel = pl.pallas_call(
        ordered,
        out_shape=outs,
        in_specs=[ANY] * len(after) + list(specs),
        out_specs=out_specs or [VMEM] * len(outs),
        scratch_shapes=scratch,
        input_output_aliases={len(after) + i: o for i, o in aliases},
        compiler_params=pltpu.CompilerParams(vmem_limit_bytes=megabytes * 1024 * 1024),
        cost_estimate=pl.CostEstimate(flops=flops, bytes_accessed=moved, transcendentals=0),
    )
    return functools.partial(kernel, *after)


def routing_body(
    capacity, n_exp, far, choice_ref, slot_ref, combine_ref, counts_ref, tok_ref, meta_ref, *outs
):
    topk = choice_ref.shape[0]
    choice = choice_ref[...]
    slot = slot_ref[...]
    limit = jnp.zeros_like(slot)
    for expert in range(n_exp):
        limit = jnp.where(choice == expert, counts_ref[0, expert], limit)
    kept = slot < capacity
    live = kept & (slot < limit)
    meta_ref[...] = jnp.zeros_like(meta_ref)
    meta_ref[CODE : CODE + topk, :] = jnp.where(kept, choice * capacity + slot, -1).astype(jnp.float32)
    meta_ref[WEIGHT : WEIGHT + topk, :] = jnp.where(live, combine_ref[...].astype(jnp.float32), 0.0)
    meta_ref[LIVE : LIVE + topk, :] = jnp.where(live, 1.0, 0.0)
    select(capacity, topk, meta_ref, tok_ref[...], outs, first=far - len(outs))


def places(target, capacity):
    return (lax.broadcasted_iota(jnp.int32, (capacity, LANES), 0) + target).astype(jnp.float32)


def pick(meta, topk, want):
    hit = meta[CODE : CODE + 1, :] == want
    for k in range(1, topk):
        hit = hit | (meta[CODE + k : CODE + k + 1, :] == want)
    return jnp.where(hit, 1.0, 0.0)


def weight_of(meta, topk, want):
    weight = jnp.zeros(want.shape, jnp.float32)
    for k in range(topk):
        weight = jnp.where(
            meta[CODE + k : CODE + k + 1, :] == want, meta[WEIGHT + k : WEIGHT + k + 1, :], weight
        )
    return jnp.sum(weight, axis=1, keepdims=True)


def select(capacity, topk, meta, rows, outs, own_meta=None, first=0):
    here = lax.axis_index("exp")
    columns = rows.shape[1]
    wants = [places((here ^ (first + m)) * capacity, capacity) for m in range(len(outs))]
    onehot = jnp.concatenate([pick(meta, topk, w) for w in wants], axis=0).astype(jnp.bfloat16)
    chosen = jnp.dot(onehot, rows, preferred_element_type=jnp.float32).astype(jnp.bfloat16)
    for m, out in enumerate(outs):
        out[:, :columns] = chosen[m * capacity : (m + 1) * capacity]
        if own_meta is not None:
            lane = lax.broadcasted_iota(jnp.int32, (capacity, LANES), 1)
            weight, own_weight = (weight_of(x, topk, wants[m]) for x in (meta, own_meta))
            out[:, columns:] = jnp.where(lane < LANES // 2, weight, own_weight).astype(jnp.bfloat16)


def select_own_body(capacity, topk, meta_ref, tok_ref, *outs):
    select(capacity, topk, meta_ref, tok_ref[...], outs)


def select_first_body(capacity, topk, cut, raw_ref, meta_ref, own_meta_ref, *outs):
    select(capacity, topk, meta_ref, raw_ref[:, cut[0] : cut[1]], outs, own_meta_ref)


def select_more_body(capacity, topk, cut, raw_ref, meta_ref, *outs):
    select(capacity, topk, meta_ref, raw_ref[:, cut[0] : cut[1]], outs)


def source_rows(capacity, n):
    source = lax.axis_index("exp") ^ n
    return pl.ds(pl.multiple_of(source * capacity, capacity), capacity)


def factors_body(
    capacity, n_edp, gate_ref, up_ref, meta_ref, shard_ref,
    hidden_ref, gate_factor_ref, up_factor_ref, turned_ref, meta_out_ref, shard_out_ref, scratch,
):
    data = lax.axis_index("edp")
    rows, units = gate_ref.shape
    shard = units // n_edp
    for n in range(rows // capacity):
        at = pl.ds(n * capacity, capacity)
        there = source_rows(capacity, n)
        gate_pre = gate_ref[there, :].astype(jnp.float32)
        up_pre = up_ref[there, :].astype(jnp.float32)
        sigmoid_gate = jax.nn.sigmoid(gate_pre)
        silu_gate = gate_pre * sigmoid_gate
        hidden_ref[at, :] = (silu_gate * up_pre).astype(jnp.bfloat16)
        gate_factor_ref[at, :] = up_pre * sigmoid_gate * (1.0 + gate_pre * (1.0 - sigmoid_gate))
        up_factor_ref[at, :] = silu_gate
    meta_out_ref[...] = meta_ref[...]
    shard_out_ref[...] = shard_ref[...]
    scratch[...] = hidden_ref[...].T
    for n in range(n_edp):
        turned_ref[n] = scratch[pl.ds(pl.multiple_of((data ^ n) * shard, 64), shard), :]


def add_cores(across_ref, *refs):
    *from_core, sum_ref = refs
    start = 0
    for ref in from_core:
        rows = pl.ds(start, ref.shape[0])
        start += ref.shape[0]
        sum_ref[rows, :] = (across_ref[rows, :] + ref[...].astype(jnp.float32)).astype(jnp.bfloat16)


def summed_out(cut, sums, out_ref, held, sem):
    keep_ref, from_core_ref, from_y_ref = sums
    held[...] = (
        keep_ref[...] + from_core_ref[...].astype(jnp.float32) + from_y_ref[...].astype(jnp.float32)
    ).astype(jnp.bfloat16)
    copy = pltpu.make_async_copy(held, out_ref.at[:, pl.ds(cut[0], cut[1] - cut[0])], sem)
    copy.start()
    return copy


def last_body(cut, *refs):
    *sums, _, out_ref, held, sem = refs
    summed_out(cut, sums, out_ref, held, sem).wait()


def returned_body(capacity, n_exp, cut, choice_ref, slot_ref, meta_ref, score_ref, far_half_ref, *refs):
    sums, refs = refs[:3], refs[5:]
    out_ref, weight_ref, gate_ref, up_ref, held, held_weight, sems, half_sems = refs
    far = n_exp // 2
    copies = []
    for m in range(0, far, 2):
        copies += copies_out(far, m, far, far_half_ref, (gate_ref, up_ref), half_sems)
    copies.append(summed_out(cut, sums, out_ref, held, sems.at[0]))
    topk, tokens = choice_ref.shape
    choice = choice_ref[...]
    slot = slot_ref[...]
    live = meta_ref[LIVE : LIVE + topk, :] > 0.0
    table = score_ref[...]
    high = table.astype(jnp.bfloat16)
    rest = table - high.astype(jnp.float32)
    middle = rest.astype(jnp.bfloat16)
    low = (rest - middle.astype(jnp.float32)).astype(jnp.bfloat16)
    split = jnp.concatenate([high, middle, low], axis=0)
    rank = lax.broadcasted_iota(jnp.int32, (capacity, tokens), 0)
    expert = lax.broadcasted_iota(jnp.int32, (n_exp, tokens), 0)
    onehot = jnp.concatenate(
        [jnp.where(rank == slot[k : k + 1, :], 1.0, 0.0).astype(jnp.bfloat16) for k in range(topk)], axis=1
    )
    parts = jnp.dot(split, onehot, preferred_element_type=jnp.float32)
    every = parts[:n_exp] + parts[n_exp : 2 * n_exp] + parts[2 * n_exp :]
    found = []
    for k in range(topk):
        mine = jnp.where(expert == choice[k : k + 1, :], every[:, k * tokens : (k + 1) * tokens], 0.0)
        found.append(jnp.sum(mine, axis=0, keepdims=True))
    held_weight[...] = jnp.where(live, jnp.concatenate(found, axis=0), 0.0)
    copies.append(pltpu.make_async_copy(held_weight, weight_ref, sems.at[1]))
    copies[-1].start()
    for copy in copies:
        copy.wait()


def weigh(far, cut, own, others, scales, weighted):
    capacity = own[0].shape[0]
    columns = cut[1] - cut[0]
    for half, pieces in enumerate((own, others)):
        shift = cut[0] if half == 0 else 0
        for m in range(far):
            at = pl.ds((half * far + m) * capacity, capacity)
            scale = weights_of(scales[m : m + 1], half == 0).astype(jnp.bfloat16)
            scale = jnp.broadcast_to(scale, (capacity, LANES))
            for i in range(0, columns, LANES):
                weighted[at, i : i + LANES] = scale * pieces[m][:, shift + i : shift + i + LANES]


def terms(tile, turned_ref, weighted, outs):
    for i in range(weighted.shape[1] // tile):
        lanes = pl.ds(i * tile, tile)
        for n, refs in outs:
            term = jnp.dot(turned_ref[n], weighted[:, lanes], preferred_element_type=jnp.float32)
            high = term.shape[0] // len(refs)
            for j, ref in enumerate(refs):
                ref[:, lanes] = term[j * high : (j + 1) * high].astype(ref.dtype)


def first_term_body(far, cut, tile, turned_ref, *refs):
    own, others, (send_ref, weighted) = refs[:far], refs[far : 2 * far], refs[2 * far :]
    weigh(far, cut, own, others, others, weighted)
    terms(tile, turned_ref, weighted, [(3, [send_ref])])


def more_terms_body(tile, shards, turned_ref, weighted, *refs):
    terms(tile, turned_ref, weighted, [(n, [ref]) for n, ref in zip(shards, refs)])


def term_body(far, cut, tile, turned_ref, *refs):
    own, others, scales, (own_ref, across_ref, send_ref, *send_across_refs, weighted) = (
        refs[:far], refs[far : 2 * far], refs[2 * far : 3 * far], refs[3 * far :]
    )
    weigh(far, cut, own, others, scales, weighted)
    outs = [(3, send_across_refs), (2, [across_ref]), (1, [send_ref]), (0, [own_ref])]
    terms(tile, turned_ref, weighted, outs)


def nt(a, b):
    return lax.dot_general(a, b, (((1,), (1,)), ((), ())), preferred_element_type=jnp.float32)


def finish(proj, weights, hidden, gate_factor, up_factor):
    part = proj * hidden.astype(jnp.float32)
    lanes = part[:, :LANES]
    for i in range(LANES, part.shape[1], LANES):
        lanes = lanes + part[:, i : i + LANES]
    score = jnp.sum(lanes.T, axis=0, keepdims=True)
    scaled = weights * proj
    gate = (gate_factor * scaled).astype(jnp.bfloat16)
    up = (up_factor * scaled).astype(jnp.bfloat16)
    return gate, up, score


def weights_of(refs, own):
    at = LANES // 2 if own else 0
    return jnp.concatenate(
        [r[:, r.shape[1] - LANES :][:, at : at + 1] for r in refs], axis=0
    ).astype(jnp.float32)


def project_own_body(far, *refs):
    shards, own, (weight_ref, proj_ref) = refs[:4], refs[4 : 4 + far], refs[4 + far :]
    data = lax.axis_index("edp")
    shard = shards[0].shape[0]
    for n in range(4):
        weight_ref[pl.ds(pl.multiple_of((data ^ n) * shard, 64), shard), :] = shards[n][...]
    proj_ref[...] = nt(jnp.concatenate([p[...] for p in own], axis=0), weight_ref[...])


def finish_half(first, far, proj, weights, hidden_ref, gate_factor_ref, up_factor_ref, held, then):
    here = lax.axis_index("exp")
    count = 2 * (proj.shape[0] // far)
    scores = []
    for m in range(0, far, 2):
        near = slice(m * count // 2, m * count // 2 + count)
        at = slice((first + m) * count // 2, (first + m) * count // 2 + count)
        gate, up, score = finish(
            proj[near], weights[near], hidden_ref[at, :], gate_factor_ref[at, :], up_factor_ref[at, :]
        )
        scores.append(score)
        for i in range(2):
            mine = slice(i * count // 2, (i + 1) * count // 2)
            within = pl.multiple_of(lax.rem(here ^ i, 2) * (count // 2), count // 2)
            there = pl.ds(m // 2 * count + within, count // 2)
            held[0, there, :] = gate[mine]
            held[1, there, :] = up[mine]
        then(m)
    return scores


def copies_out(first, m, far, held, outs, sems):
    count = 2 * (held.shape[1] // far)
    lower = pl.multiple_of(((lax.axis_index("exp") ^ (first + m)) // 2) * count, count)
    copies = []
    for i, out in enumerate(outs):
        source = held.at[i, pl.ds(m // 2 * count, count), :]
        copies.append(pltpu.make_async_copy(source, out.at[pl.ds(lower, count), :], sems.at[m // 2, i]))
        copies[-1].start()
    return copies


def project_far_body(far, cut, *refs):
    pieces, refs = refs[:far], refs[far:]
    weight_ref, own_proj_ref, hidden_ref, gate_factor_ref, up_factor_ref, *outs = refs
    proj_ref, gate_ref, up_ref, score_ref, held, sems = outs
    copies = []
    scores = finish_half(
        0, far, own_proj_ref[...], weights_of(pieces, True), hidden_ref, gate_factor_ref, up_factor_ref,
        held, lambda m: copies.extend(copies_out(0, m, far, held, (gate_ref, up_ref), sems)),
    )
    for i, score in enumerate(scores):
        score_ref[i : i + 1, :] = score
    rows = jnp.concatenate([p[:, : cut[1] - cut[0]] for p in pieces], axis=0)
    proj_ref[...] = nt(rows, weight_ref[:, cut[0] : cut[1]])
    for copy in copies:
        copy.wait()


def final_body(far, cut, *refs):
    pieces, scales, refs = refs[:far], refs[far : 2 * far], refs[2 * far :]
    (
        weight_ref, proj_ref, hidden_ref, gate_factor_ref, up_factor_ref, own_score_ref,
        score_ref, held,
    ) = refs
    here = lax.axis_index("exp")
    capacity = pieces[0].shape[0]
    rows = jnp.concatenate([p[...] for p in pieces], axis=0)
    proj = proj_ref[...] + nt(rows, weight_ref[:, cut[0] : cut[1]])
    scores = finish_half(
        far, far, proj, weights_of(scales, False), hidden_ref, gate_factor_ref, up_factor_ref,
        held, lambda m: None,
    )
    for m in range(0, far, 2):
        for first, score in ((far + m, scores[m // 2]), (m, own_score_ref[m // 2 : m // 2 + 1, :])):
            for i in range(2):
                score_ref[pl.ds(here ^ (first + i), 1), :] = score[:, i * capacity : (i + 1) * capacity]


def relayed(
    out_grad,
    combine,
    token_expert_choice,
    slots,
    counts,
    down_weight,
    stored_gate_preact,
    stored_up_preact,
):
    n_exp = lax.axis_size("exp")
    n_edp = lax.axis_size("edp")
    capacity = stored_gate_preact.shape[2] // n_exp
    units = stored_gate_preact.shape[3]
    rows = n_exp * capacity
    tok_rows, width = out_grad.shape
    topk = slots.shape[1]
    shard = units // n_edp
    far = n_exp // 2
    cuts = column_cuts(width)
    sizes = [b - a for a, b in cuts]
    splits = [1, 2]
    bf16, f32 = jnp.bfloat16, jnp.float32

    def shape(*dims, dtype=bf16):
        return jax.ShapeDtypeStruct(dims, dtype)

    def hop(x, axis, mask, after=None):
        if after is not None:
            x, _ = lax.optimization_barrier((x, after))
        return lax.ppermute(x, axis, flip(lax.axis_size(axis), mask))

    def spread(found):
        return [found[0]] + [hop(found[m], "exp", m) for m in range(1, far)]

    meta, *found = call(
        functools.partial(routing_body, capacity, n_exp, far),
        [shape(META_ROWS, LANES, dtype=f32)] + [shape(capacity, width)] * (far // 2),
        [BLOCK, BLOCK, BLOCK, SMEM, BLOCK],
        56,
        flops=2 * far * capacity * tok_rows * width,
        moved=out_grad.size * 4,
    )(token_expert_choice.T, slots.T, combine.T, counts, out_grad)
    raw = hop(out_grad, "exp", far)
    own = [hop(x, "exp", far // 2 + m) for m, x in enumerate(found)]
    hidden, gate_factor, up_factor, turned, meta, weight_here = call(
        functools.partial(factors_body, capacity, n_edp),
        [
            shape(rows, units),
            shape(rows, units, dtype=f32),
            shape(rows, units, dtype=f32),
            shape(n_edp, shard, rows),
            shape(META_ROWS, LANES, dtype=f32),
            shape(shard, width),
        ],
        [VMEM] * 4,
        24,
        flops=40 * rows * units,
        moved=16 * rows * units,
        scratch=[pltpu.VMEM((units, rows), bf16)],
    )(stored_gate_preact[0, 0], stored_up_preact[0, 0], meta, down_weight[0])
    weight_y = hop(down_weight[0], "edp", 2)
    far_meta = hop(meta, "exp", far, own[0])

    found = call(
        functools.partial(select_own_body, capacity, topk),
        [shape(capacity, width)] * (far // 2),
        [VMEM] * 2,
        16,
        after=[hidden],
    )(meta, out_grad)
    own = [found[0]] + [hop(found[m], "exp", m) for m in range(1, far // 2)] + own

    def term(k, others, scales, after=()):
        return call(
            functools.partial(term_body, far, cuts[k], 640),
            [shape(shard, sizes[k], dtype=f32)] * 2
            + [shape(shard, sizes[k])]
            + [shape(shard // splits[k], sizes[k])] * splits[k],
            [VMEM] * (1 + 3 * far),
            24,
            flops=2 * rows * units * sizes[k],
            moved=4 * (rows + units) * sizes[k],
            scratch=[pltpu.VMEM((rows, sizes[k]), bf16)],
            after=after,
        )(turned, *own, *others, *scales)

    def cores(send):
        return [hop(x, "edp", 1) for x in send]

    def across(k, mine, from_core, after=()):
        (sent,) = call(add_cores, [shape(shard, sizes[k])], [VMEM] * (1 + splits[k]), 8, after=after)(
            mine, *from_core
        )
        return sent, hop(sent, "edp", 2)

    found = call(
        functools.partial(select_first_body, capacity, topk, cuts[0]),
        [shape(capacity, sizes[0] + LANES)] * far,
        [VMEM] * 3,
        16,
        flops=2 * far * capacity * tok_rows * sizes[0],
        moved=4 * far * capacity * sizes[0],
        after=[*own[1:], hidden, weight_y],
    )(raw, far_meta, meta)
    far0 = spread(found)
    weight_core = hop(weight_here, "edp", 1, own[far - 1])
    weight_both = hop(weight_y, "edp", 1, found[0])
    weight, own_proj = call(
        functools.partial(project_own_body, far),
        [shape(units, width), shape(far * capacity, units, dtype=f32)],
        [VMEM] * (4 + far),
        32,
    )(weight_here, weight_core, weight_y, weight_both, *own)
    more = call(
        functools.partial(select_more_body, capacity, topk, cuts[1]),
        [shape(capacity, sizes[1])] * far,
        [VMEM] * 2,
        16,
        flops=2 * far * capacity * tok_rows * sizes[1],
        moved=4 * far * capacity * sizes[1],
        after=far0[:1],
    )(raw, far_meta)
    first0, weighted = call(
        functools.partial(first_term_body, far, cuts[0], 640),
        [shape(shard, sizes[0]), shape(rows, sizes[0])],
        [VMEM] * (1 + 2 * far),
        24,
        after=[own_proj, more[0]],
    )(turned, *own, *far0)
    first0 = hop(first0, "edp", 1)
    def more_terms(shards, outs, after=()):
        return call(
            functools.partial(more_terms_body, 640, shards), outs, [VMEM] * 2, 24, after=after
        )(turned, weighted)

    across0, send0 = more_terms([2, 1], [shape(shard, sizes[0], dtype=f32), shape(shard, sizes[0])])
    core0 = hop(send0, "edp", 1)
    sent0, from_y0 = across(0, across0, [first0])
    far1 = [more[0]] + [hop(more[m], "exp", m, sent0) for m in range(1, far)]
    half_scratch = [
        pltpu.VMEM((2, far * capacity, units), bf16),
        pltpu.SemaphoreType.DMA((far // 2, 2)),
    ]
    proj, gate_preact_gradient, up_preact_gradient, own_score = call(
        functools.partial(project_far_body, far, cuts[0]),
        [
            shape(far * capacity, units, dtype=f32),
            shape(rows, units),
            shape(rows, units),
            shape(far // 2, 2 * capacity, dtype=f32),
        ],
        [VMEM] * (5 + far),
        24,
        scratch=half_scratch,
        after=[sent0, far1[0], core0],
        out_specs=[VMEM, ANY, ANY, VMEM],
    )(*far0, weight, own_proj, hidden, gate_factor, up_factor)
    (keep0,) = more_terms([0], [shape(shard, sizes[0], dtype=f32)], [proj])
    keep1, across1, *send1 = term(1, far1, far0, [keep0])
    core1 = cores(send1)
    score, far_half = call(
        functools.partial(final_body, far, cuts[1]),
        [shape(n_exp, capacity, dtype=f32), shape(2, far * capacity, units)],
        [VMEM] * (2 * far + 6),
        24,
        after=[keep1],
    )(*far1, *far0, weight, proj, hidden, gate_factor, up_factor, own_score)
    _, from_y1 = across(1, across1, core1[1:], [score, core1[0]])
    returned = lax.all_to_all(score, "exp", split_axis=0, concat_axis=0)
    down_matrix_gradient, combine_weight_gradient, gate_preact_gradient, up_preact_gradient = call(
        functools.partial(returned_body, capacity, n_exp, cuts[0]),
        [shape(shard, width), shape(topk, tok_rows, dtype=f32), shape(rows, units), shape(rows, units)],
        [VMEM] * 8 + [ANY] * 2,
        16,
        scratch=[
            pltpu.VMEM((shard, sizes[0]), bf16),
            pltpu.VMEM((topk, tok_rows), f32),
            pltpu.SemaphoreType.DMA((2,)),
            half_scratch[1],
        ],
        out_specs=[ANY] * 4,
        aliases=[(8, 2), (9, 3)],
    )(
        token_expert_choice.T, slots.T, meta, returned, far_half, keep0, core0, from_y0,
        gate_preact_gradient, up_preact_gradient,
    )
    (down_matrix_gradient,) = call(
        functools.partial(last_body, cuts[1]),
        [shape(shard, width)],
        [VMEM] * 3 + [ANY],
        8,
        scratch=[pltpu.VMEM((shard, sizes[1]), bf16), pltpu.SemaphoreType.DMA],
        out_specs=[ANY],
        aliases=[(3, 0)],
    )(keep1, core1[0], from_y1, down_matrix_gradient)
    return (
        gate_preact_gradient[None, None],
        up_preact_gradient[None, None],
        down_matrix_gradient[None],
        combine_weight_gradient.T,
    )


def direct(
    out_grad,
    combine,
    token_expert_choice,
    slots,
    counts,
    down_weight,
    stored_gate_preact,
    stored_up_preact,
):
    experts_here = lax.axis_size("exp")
    capacity = stored_gate_preact.shape[2] // experts_here
    tok_rows = out_grad.shape[0]
    model_width = out_grad.shape[1]
    slot_index = jnp.where(
        slots < capacity, token_expert_choice * capacity + slots, experts_here * capacity
    )
    flat_index = slot_index.reshape(-1)
    row_ids = jnp.broadcast_to(
        jnp.arange(tok_rows, dtype=jnp.int32)[:, None] + 1, slot_index.shape
    ).reshape(-1)
    sender_rows = (
        jnp.zeros((experts_here * capacity,), jnp.int32).at[flat_index].set(row_ids, mode="drop")
    )
    padded_grad = jnp.concatenate([jnp.zeros((1, model_width), out_grad.dtype), out_grad], axis=0)
    send_grad = padded_grad[sender_rows].reshape(experts_here, capacity, model_width)
    send_weight = (
        jnp.zeros((experts_here * capacity,), combine.dtype)
        .at[flat_index]
        .set(combine.reshape(-1), mode="drop")
    )
    send_weight = send_weight.reshape(experts_here, capacity)
    send_count = counts.reshape(experts_here, 1)
    recv_grad, received_weight, recv_count = (
        lax.all_to_all(send_grad, "exp", split_axis=0, concat_axis=0, tiled=True),
        lax.all_to_all(send_weight, "exp", split_axis=0, concat_axis=0, tiled=True),
        lax.all_to_all(send_count, "exp", split_axis=0, concat_axis=0, tiled=True),
    )
    live_mask = (jnp.arange(capacity, dtype=jnp.int32)[None, :] < recv_count).astype(jnp.float32)
    scaled = (live_mask * received_weight.astype(jnp.float32)).reshape(-1)
    live_rows = live_mask.reshape(-1)
    grad_rows = recv_grad.reshape(-1, model_width)
    proj = lax.dot_general(
        grad_rows,
        lax.all_gather(down_weight, "edp", axis=1, tiled=True)[0],
        (((1,), (1,)), ((), ())),
        preferred_element_type=jnp.float32,
    )
    gate_pre = stored_gate_preact[0, 0].astype(jnp.float32)
    up_pre = stored_up_preact[0, 0].astype(jnp.float32)
    sigmoid_gate = jax.nn.sigmoid(gate_pre)
    silu_gate = gate_pre * sigmoid_gate
    hidden = (silu_gate * up_pre).astype(jnp.bfloat16)
    weighted = (scaled[:, None] * grad_rows.astype(jnp.float32)).astype(jnp.bfloat16)
    grad_hidden = scaled[:, None] * proj
    gate_preact_gradient = (
        grad_hidden * up_pre * sigmoid_gate * (1.0 + gate_pre * (1.0 - sigmoid_gate))
    ).astype(jnp.bfloat16)
    up_preact_gradient = (grad_hidden * silu_gate).astype(jnp.bfloat16)
    score = (live_rows * jnp.sum(proj * hidden.astype(jnp.float32), axis=1)).reshape(
        experts_here, capacity
    )
    returned_scores = lax.all_to_all(score, "exp", split_axis=0, concat_axis=0, tiled=True)
    summed = lax.psum_scatter(
        lax.dot_general(
            hidden, weighted, (((0,), (0,)), ((), ())), preferred_element_type=jnp.float32
        ),
        "edp",
        scatter_dimension=0,
        tiled=True,
    )
    returned = jnp.concatenate([returned_scores.reshape(-1), jnp.zeros((1,), jnp.float32)])
    combine_weight_gradient = returned[slot_index]
    down_matrix_gradient = summed.astype(jnp.bfloat16)[None]
    return (
        gate_preact_gradient[None, None],
        up_preact_gradient[None, None],
        down_matrix_gradient,
        combine_weight_gradient,
    )


def solution(mesh):
    n_exp, n_edp = mesh.shape["exp"], mesh.shape["edp"]

    def on_device(*arrays):
        tok_rows = arrays[0].shape[0]
        capacity = arrays[6].shape[2] // n_exp
        if n_exp == 8 and n_edp == 4 and tok_rows == LANES and tok_rows <= 2 * capacity:
            return relayed(*arrays)
        return direct(*arrays)

    return jax.shard_map(
        on_device,
        mesh=mesh,
        in_specs=(
            P(("exp", "edp"), None),
            P(("exp", "edp"), None),
            P(("exp", "edp"), None),
            P(("exp", "edp"), None),
            P(("exp", "edp"), None),
            P("exp", "edp", None),
            P("exp", "edp", None, None),
            P("exp", "edp", None, None),
        ),
        out_specs=(
            P("exp", "edp", None, None),
            P("exp", "edp", None, None),
            P("exp", "edp", None),
            P(("exp", "edp"), None),
        ),
        check_vma=False,
    )
```

```python
import functools

import jax
import jax.numpy as jnp
from jax import lax
from jax.experimental import pallas as pl
from jax.experimental.pallas import tpu as pltpu
from jax.sharding import PartitionSpec as P


def flip(n, mask):
    return [(i, i ^ mask) for i in range(n)]


def column_cuts(width):
    unit = width // 20
    return [(0, 15 * unit), (15 * unit, width)]


VMEM = pl.BlockSpec(memory_space=pltpu.VMEM)
SMEM = pl.BlockSpec(memory_space=pltpu.SMEM)
BLOCK = pl.BlockSpec()
ANY = pl.BlockSpec(memory_space=pl.ANY)
LANES = 128
CODE, WEIGHT, LIVE, META_ROWS = 0, 8, 16, 24


def call(body, outs, specs, megabytes, flops=0, moved=0, scratch=(), after=(), out_specs=None, aliases=()):
    def ordered(*refs):
        body(*refs[len(after) :])

    kernel = pl.pallas_call(
        ordered,
        out_shape=outs,
        in_specs=[ANY] * len(after) + list(specs),
        out_specs=out_specs or [VMEM] * len(outs),
        scratch_shapes=scratch,
        input_output_aliases={len(after) + i: o for i, o in aliases},
        compiler_params=pltpu.CompilerParams(vmem_limit_bytes=megabytes * 1024 * 1024),
        cost_estimate=pl.CostEstimate(flops=flops, bytes_accessed=moved, transcendentals=0),
    )
    return functools.partial(kernel, *after)


def routing_body(
    capacity, n_exp, far, choice_ref, slot_ref, combine_ref, counts_ref, tok_ref, meta_ref, *outs
):
    topk = choice_ref.shape[0]
    choice = choice_ref[...]
    slot = slot_ref[...]
    limit = jnp.zeros_like(slot)
    for expert in range(n_exp):
        limit = jnp.where(choice == expert, counts_ref[0, expert], limit)
    kept = slot < capacity
    live = kept & (slot < limit)
    meta_ref[...] = jnp.zeros_like(meta_ref)
    meta_ref[CODE : CODE + topk, :] = jnp.where(kept, choice * capacity + slot, -1).astype(jnp.float32)
    meta_ref[WEIGHT : WEIGHT + topk, :] = jnp.where(live, combine_ref[...].astype(jnp.float32), 0.0)
    meta_ref[LIVE : LIVE + topk, :] = jnp.where(live, 1.0, 0.0)
    select(capacity, topk, meta_ref, tok_ref[...], outs, first=far - len(outs))


def places(target, capacity):
    return (lax.broadcasted_iota(jnp.int32, (capacity, LANES), 0) + target).astype(jnp.float32)


def pick(meta, topk, want):
    hit = meta[CODE : CODE + 1, :] == want
    for k in range(1, topk):
        hit = hit | (meta[CODE + k : CODE + k + 1, :] == want)
    return jnp.where(hit, 1.0, 0.0)


def weight_of(meta, topk, want):
    weight = jnp.zeros(want.shape, jnp.float32)
    for k in range(topk):
        weight = jnp.where(
            meta[CODE + k : CODE + k + 1, :] == want, meta[WEIGHT + k : WEIGHT + k + 1, :], weight
        )
    return jnp.sum(weight, axis=1, keepdims=True)


def select(capacity, topk, meta, rows, outs, own_meta=None, first=0):
    here = lax.axis_index("exp")
    columns = rows.shape[1]
    wants = [places((here ^ (first + m)) * capacity, capacity) for m in range(len(outs))]
    onehot = jnp.concatenate([pick(meta, topk, w) for w in wants], axis=0).astype(jnp.bfloat16)
    chosen = jnp.dot(onehot, rows, preferred_element_type=jnp.float32).astype(jnp.bfloat16)
    for m, out in enumerate(outs):
        out[:, :columns] = chosen[m * capacity : (m + 1) * capacity]
        if own_meta is not None:
            lane = lax.broadcasted_iota(jnp.int32, (capacity, LANES), 1)
            weight, own_weight = (weight_of(x, topk, wants[m]) for x in (meta, own_meta))
            out[:, columns:] = jnp.where(lane < LANES // 2, weight, own_weight).astype(jnp.bfloat16)


def select_own_body(capacity, topk, meta_ref, tok_ref, *outs):
    select(capacity, topk, meta_ref, tok_ref[...], outs)


def select_first_body(capacity, topk, cut, raw_ref, meta_ref, own_meta_ref, *outs):
    select(capacity, topk, meta_ref, raw_ref[:, cut[0] : cut[1]], outs, own_meta_ref)


def select_more_body(capacity, topk, cut, raw_ref, meta_ref, *outs):
    select(capacity, topk, meta_ref, raw_ref[:, cut[0] : cut[1]], outs)


def source_rows(capacity, n):
    source = lax.axis_index("exp") ^ n
    return pl.ds(pl.multiple_of(source * capacity, capacity), capacity)


def factors_body(
    capacity, n_edp, gate_ref, up_ref, meta_ref, shard_ref,
    hidden_ref, gate_factor_ref, up_factor_ref, turned_ref, meta_out_ref, shard_out_ref, scratch,
):
    data = lax.axis_index("edp")
    rows, units = gate_ref.shape
    shard = units // n_edp
    for n in range(rows // capacity):
        at = pl.ds(n * capacity, capacity)
        there = source_rows(capacity, n)
        gate_pre = gate_ref[there, :].astype(jnp.float32)
        up_pre = up_ref[there, :].astype(jnp.float32)
        sigmoid_gate = jax.nn.sigmoid(gate_pre)
        silu_gate = gate_pre * sigmoid_gate
        hidden_ref[at, :] = (silu_gate * up_pre).astype(jnp.bfloat16)
        gate_factor_ref[at, :] = up_pre * sigmoid_gate * (1.0 + gate_pre * (1.0 - sigmoid_gate))
        up_factor_ref[at, :] = silu_gate
    meta_out_ref[...] = meta_ref[...]
    shard_out_ref[...] = shard_ref[...]
    scratch[...] = hidden_ref[...].T
    for n in range(n_edp):
        turned_ref[n] = scratch[pl.ds(pl.multiple_of((data ^ n) * shard, 64), shard), :]


def add_cores(across_ref, *refs):
    *from_core, sum_ref = refs
    start = 0
    for ref in from_core:
        rows = pl.ds(start, ref.shape[0])
        start += ref.shape[0]
        sum_ref[rows, :] = (across_ref[rows, :] + ref[...].astype(jnp.float32)).astype(jnp.bfloat16)


def summed_out(cut, sums, out_ref, held, sem):
    keep_ref, from_core_ref, from_y_ref = sums
    held[...] = (
        keep_ref[...] + from_core_ref[...].astype(jnp.float32) + from_y_ref[...].astype(jnp.float32)
    ).astype(jnp.bfloat16)
    copy = pltpu.make_async_copy(held, out_ref.at[:, pl.ds(cut[0], cut[1] - cut[0])], sem)
    copy.start()
    return copy


def last_body(cut, *refs):
    *sums, _, out_ref, held, sem = refs
    summed_out(cut, sums, out_ref, held, sem).wait()


def returned_body(capacity, n_exp, cut, choice_ref, slot_ref, meta_ref, score_ref, far_half_ref, *refs):
    sums, refs = refs[:3], refs[5:]
    out_ref, weight_ref, gate_ref, up_ref, held, held_weight, sems, half_sems = refs
    far = n_exp // 2
    copies = []
    for m in range(0, far, 2):
        copies += copies_out(far, m, far, far_half_ref, (gate_ref, up_ref), half_sems)
    copies.append(summed_out(cut, sums, out_ref, held, sems.at[0]))
    topk, tokens = choice_ref.shape
    choice = choice_ref[...]
    slot = slot_ref[...]
    live = meta_ref[LIVE : LIVE + topk, :] > 0.0
    table = score_ref[...]
    high = table.astype(jnp.bfloat16)
    rest = table - high.astype(jnp.float32)
    middle = rest.astype(jnp.bfloat16)
    low = (rest - middle.astype(jnp.float32)).astype(jnp.bfloat16)
    split = jnp.concatenate([high, middle, low], axis=0)
    rank = lax.broadcasted_iota(jnp.int32, (capacity, tokens), 0)
    expert = lax.broadcasted_iota(jnp.int32, (n_exp, tokens), 0)
    onehot = jnp.concatenate(
        [jnp.where(rank == slot[k : k + 1, :], 1.0, 0.0).astype(jnp.bfloat16) for k in range(topk)], axis=1
    )
    parts = jnp.dot(split, onehot, preferred_element_type=jnp.float32)
    every = parts[:n_exp] + parts[n_exp : 2 * n_exp] + parts[2 * n_exp :]
    found = []
    for k in range(topk):
        mine = jnp.where(expert == choice[k : k + 1, :], every[:, k * tokens : (k + 1) * tokens], 0.0)
        found.append(jnp.sum(mine, axis=0, keepdims=True))
    held_weight[...] = jnp.where(live, jnp.concatenate(found, axis=0), 0.0)
    copies.append(pltpu.make_async_copy(held_weight, weight_ref, sems.at[1]))
    copies[-1].start()
    for copy in copies:
        copy.wait()


def weighted_rows(far, start, tile, cut, own, others, scales):
    blocks = []
    for half, pieces in enumerate((own, others)):
        first = start + (cut[0] if half == 0 else 0)
        for m in range(far):
            scale = weights_of(scales[m : m + 1], half == 0).astype(jnp.bfloat16)
            blocks.append(jnp.broadcast_to(scale, (scale.shape[0], tile)) * pieces[m][:, first : first + tile])
    return jnp.concatenate(blocks, axis=0)


def terms(turned_ref, rows, lanes, outs):
    first = outs[0][0]
    refs = [ref for _, some in outs for ref in some]
    shard, depth = turned_ref.shape[1:]
    left = turned_ref[first : first + len(outs)].reshape(len(outs) * shard, depth)
    term = jnp.dot(left, rows, preferred_element_type=jnp.float32)
    at = 0
    for ref in refs:
        ref[:, lanes] = term[at : at + ref.shape[0]].astype(ref.dtype)
        at += ref.shape[0]


def first_term_body(far, cut, tile, turned_ref, *refs):
    own, others, (send_ref, weighted) = refs[:far], refs[far : 2 * far], refs[2 * far :]
    for start in range(0, cut[1] - cut[0], tile):
        lanes = pl.ds(start, tile)
        rows = weighted_rows(far, start, tile, cut, own, others, others)
        weighted[:, lanes] = rows
        terms(turned_ref, rows, lanes, [(3, [send_ref])])


def more_terms_body(tile, shards, turned_ref, weighted, *refs):
    for start in range(0, weighted.shape[1], tile):
        lanes = pl.ds(start, tile)
        terms(turned_ref, weighted[:, lanes], lanes, [(n, [ref]) for n, ref in zip(shards, refs)])


def term_body(far, cut, tile, turned_ref, *refs):
    own, others, scales, (own_ref, across_ref, send_ref, *send_across_refs) = (
        refs[:far], refs[far : 2 * far], refs[2 * far : 3 * far], refs[3 * far :]
    )
    for start in range(0, cut[1] - cut[0], tile):
        lanes = pl.ds(start, tile)
        rows = weighted_rows(far, start, tile, cut, own, others, scales)
        outs = [(0, [own_ref]), (1, [send_ref]), (2, [across_ref]), (3, send_across_refs)]
        terms(turned_ref, rows, lanes, outs)


def nt(a, b):
    return lax.dot_general(a, b, (((1,), (1,)), ((), ())), preferred_element_type=jnp.float32)


def finish(proj, weights, hidden, gate_factor, up_factor):
    part = proj * hidden.astype(jnp.float32)
    lanes = part[:, :LANES]
    for i in range(LANES, part.shape[1], LANES):
        lanes = lanes + part[:, i : i + LANES]
    score = jnp.sum(lanes.T, axis=0, keepdims=True)
    scaled = weights * proj
    gate = (gate_factor * scaled).astype(jnp.bfloat16)
    up = (up_factor * scaled).astype(jnp.bfloat16)
    return gate, up, score


def weights_of(refs, own):
    at = LANES // 2 if own else 0
    return jnp.concatenate(
        [r[:, r.shape[1] - LANES :][:, at : at + 1] for r in refs], axis=0
    ).astype(jnp.float32)


def project_own_body(far, *refs):
    shards, own, (weight_ref, proj_ref) = refs[:4], refs[4 : 4 + far], refs[4 + far :]
    data = lax.axis_index("edp")
    shard = shards[0].shape[0]
    for n in range(4):
        weight_ref[pl.ds(pl.multiple_of((data ^ n) * shard, 64), shard), :] = shards[n][...]
    proj_ref[...] = nt(jnp.concatenate([p[...] for p in own], axis=0), weight_ref[...])


def finish_half(first, far, proj, weights, hidden_ref, gate_factor_ref, up_factor_ref, held, then):
    here = lax.axis_index("exp")
    count = 2 * (proj.shape[0] // far)
    scores = []
    for m in range(0, far, 2):
        near = slice(m * count // 2, m * count // 2 + count)
        at = slice((first + m) * count // 2, (first + m) * count // 2 + count)
        gate, up, score = finish(
            proj[near], weights[near], hidden_ref[at, :], gate_factor_ref[at, :], up_factor_ref[at, :]
        )
        scores.append(score)
        for i in range(2):
            mine = slice(i * count // 2, (i + 1) * count // 2)
            within = pl.multiple_of(lax.rem(here ^ i, 2) * (count // 2), count // 2)
            there = pl.ds(m // 2 * count + within, count // 2)
            held[0, there, :] = gate[mine]
            held[1, there, :] = up[mine]
        then(m)
    return scores


def copies_out(first, m, far, held, outs, sems):
    count = 2 * (held.shape[1] // far)
    lower = pl.multiple_of(((lax.axis_index("exp") ^ (first + m)) // 2) * count, count)
    copies = []
    for i, out in enumerate(outs):
        source = held.at[i, pl.ds(m // 2 * count, count), :]
        copies.append(pltpu.make_async_copy(source, out.at[pl.ds(lower, count), :], sems.at[m // 2, i]))
        copies[-1].start()
    return copies


def project_far_body(far, cut, *refs):
    pieces, refs = refs[:far], refs[far:]
    weight_ref, own_proj_ref, hidden_ref, gate_factor_ref, up_factor_ref, *outs = refs
    proj_ref, gate_ref, up_ref, score_ref, held, sems = outs
    copies = []
    scores = finish_half(
        0, far, own_proj_ref[...], weights_of(pieces, True), hidden_ref, gate_factor_ref, up_factor_ref,
        held, lambda m: copies.extend(copies_out(0, m, far, held, (gate_ref, up_ref), sems)),
    )
    for i, score in enumerate(scores):
        score_ref[i : i + 1, :] = score
    rows = jnp.concatenate([p[:, : cut[1] - cut[0]] for p in pieces], axis=0)
    proj_ref[...] = nt(rows, weight_ref[:, cut[0] : cut[1]])
    for copy in copies:
        copy.wait()


def final_body(far, cut, *refs):
    pieces, scales, refs = refs[:far], refs[far : 2 * far], refs[2 * far :]
    (
        weight_ref, proj_ref, hidden_ref, gate_factor_ref, up_factor_ref, own_score_ref,
        score_ref, held,
    ) = refs
    here = lax.axis_index("exp")
    capacity = pieces[0].shape[0]
    rows = jnp.concatenate([p[...] for p in pieces], axis=0)
    proj = proj_ref[...] + nt(rows, weight_ref[:, cut[0] : cut[1]])
    scores = finish_half(
        far, far, proj, weights_of(scales, False), hidden_ref, gate_factor_ref, up_factor_ref,
        held, lambda m: None,
    )
    for m in range(0, far, 2):
        for first, score in ((far + m, scores[m // 2]), (m, own_score_ref[m // 2 : m // 2 + 1, :])):
            for i in range(2):
                score_ref[pl.ds(here ^ (first + i), 1), :] = score[:, i * capacity : (i + 1) * capacity]


def relayed(
    out_grad,
    combine,
    token_expert_choice,
    slots,
    counts,
    down_weight,
    stored_gate_preact,
    stored_up_preact,
):
    n_exp = lax.axis_size("exp")
    n_edp = lax.axis_size("edp")
    capacity = stored_gate_preact.shape[2] // n_exp
    units = stored_gate_preact.shape[3]
    rows = n_exp * capacity
    tok_rows, width = out_grad.shape
    topk = slots.shape[1]
    shard = units // n_edp
    far = n_exp // 2
    cuts = column_cuts(width)
    sizes = [b - a for a, b in cuts]
    splits = [1, 1]
    bf16, f32 = jnp.bfloat16, jnp.float32

    def shape(*dims, dtype=bf16):
        return jax.ShapeDtypeStruct(dims, dtype)

    def hop(x, axis, mask, after=None):
        if after is not None:
            x, _ = lax.optimization_barrier((x, after))
        return lax.ppermute(x, axis, flip(lax.axis_size(axis), mask))

    def spread(found):
        return [found[0]] + [hop(found[m], "exp", m) for m in range(1, far)]

    meta, *found = call(
        functools.partial(routing_body, capacity, n_exp, far),
        [shape(META_ROWS, LANES, dtype=f32)] + [shape(capacity, width)] * (far // 2),
        [BLOCK, BLOCK, BLOCK, SMEM, BLOCK],
        56,
        flops=2 * far * capacity * tok_rows * width,
        moved=out_grad.size * 4,
    )(token_expert_choice.T, slots.T, combine.T, counts, out_grad)
    raw = hop(out_grad, "exp", far)
    own = [hop(x, "exp", far // 2 + m) for m, x in enumerate(found)]
    hidden, gate_factor, up_factor, turned, meta, weight_here = call(
        functools.partial(factors_body, capacity, n_edp),
        [
            shape(rows, units),
            shape(rows, units, dtype=f32),
            shape(rows, units, dtype=f32),
            shape(n_edp, shard, rows),
            shape(META_ROWS, LANES, dtype=f32),
            shape(shard, width),
        ],
        [VMEM] * 4,
        24,
        flops=40 * rows * units,
        moved=16 * rows * units,
        scratch=[pltpu.VMEM((units, rows), bf16)],
    )(stored_gate_preact[0, 0], stored_up_preact[0, 0], meta, down_weight[0])
    weight_y = hop(down_weight[0], "edp", 2)
    far_meta = hop(meta, "exp", far, own[0])

    found = call(
        functools.partial(select_own_body, capacity, topk),
        [shape(capacity, width)] * (far // 2),
        [VMEM] * 2,
        16,
        after=[hidden],
    )(meta, out_grad)
    own = [found[0]] + [hop(found[m], "exp", m) for m in range(1, far // 2)] + own

    def term(k, others, scales, after=()):
        return call(
            functools.partial(term_body, far, cuts[k], sizes[k]),
            [shape(shard, sizes[k], dtype=f32)] * 2
            + [shape(shard, sizes[k])]
            + [shape(shard // splits[k], sizes[k])] * splits[k],
            [VMEM] * (1 + 3 * far),
            24,
            flops=2 * rows * units * sizes[k],
            moved=4 * (rows + units) * sizes[k],
            after=after,
        )(turned, *own, *others, *scales)

    def cores(send):
        return [hop(x, "edp", 1) for x in send]

    def across(k, mine, from_core, after=()):
        (sent,) = call(add_cores, [shape(shard, sizes[k])], [VMEM] * (1 + splits[k]), 8, after=after)(
            mine, *from_core
        )
        return sent, hop(sent, "edp", 2)

    found = call(
        functools.partial(select_first_body, capacity, topk, cuts[0]),
        [shape(capacity, sizes[0] + LANES)] * far,
        [VMEM] * 3,
        16,
        flops=2 * far * capacity * tok_rows * sizes[0],
        moved=4 * far * capacity * sizes[0],
        after=[*own[1:], hidden, weight_y],
    )(raw, far_meta, meta)
    far0 = spread(found)
    weight_core = hop(weight_here, "edp", 1, own[far - 1])
    weight_both = hop(weight_y, "edp", 1, found[0])
    weight, own_proj = call(
        functools.partial(project_own_body, far),
        [shape(units, width), shape(far * capacity, units, dtype=f32)],
        [VMEM] * (4 + far),
        32,
    )(weight_here, weight_core, weight_y, weight_both, *own)
    more = call(
        functools.partial(select_more_body, capacity, topk, cuts[1]),
        [shape(capacity, sizes[1])] * far,
        [VMEM] * 2,
        16,
        flops=2 * far * capacity * tok_rows * sizes[1],
        moved=4 * far * capacity * sizes[1],
        after=far0[:1],
    )(raw, far_meta)
    first0, weighted = call(
        functools.partial(first_term_body, far, cuts[0], sizes[0]),
        [shape(shard, sizes[0]), shape(rows, sizes[0])],
        [VMEM] * (1 + 2 * far),
        24,
        after=[own_proj, more[0]],
    )(turned, *own, *far0)
    first0 = hop(first0, "edp", 1)
    def more_terms(shards, outs, after=()):
        return call(
            functools.partial(more_terms_body, sizes[0], shards), outs, [VMEM] * 2, 24, after=after
        )(turned, weighted)

    send0, across0 = more_terms([1, 2], [shape(shard, sizes[0]), shape(shard, sizes[0], dtype=f32)])
    core0 = hop(send0, "edp", 1)
    sent0, from_y0 = across(0, across0, [first0])
    far1 = [more[0]] + [hop(more[m], "exp", m, sent0) for m in range(1, far)]
    half_scratch = [
        pltpu.VMEM((2, far * capacity, units), bf16),
        pltpu.SemaphoreType.DMA((far // 2, 2)),
    ]
    proj, gate_preact_gradient, up_preact_gradient, own_score = call(
        functools.partial(project_far_body, far, cuts[0]),
        [
            shape(far * capacity, units, dtype=f32),
            shape(rows, units),
            shape(rows, units),
            shape(far // 2, 2 * capacity, dtype=f32),
        ],
        [VMEM] * (5 + far),
        24,
        scratch=half_scratch,
        after=[sent0, far1[0], core0],
        out_specs=[VMEM, ANY, ANY, VMEM],
    )(*far0, weight, own_proj, hidden, gate_factor, up_factor)
    (keep0,) = more_terms([0], [shape(shard, sizes[0], dtype=f32)], [proj])
    keep1, across1, *send1 = term(1, far1, far0, [keep0])
    core1 = cores(send1)
    score, far_half = call(
        functools.partial(final_body, far, cuts[1]),
        [shape(n_exp, capacity, dtype=f32), shape(2, far * capacity, units)],
        [VMEM] * (2 * far + 6),
        24,
        after=[keep1],
    )(*far1, *far0, weight, proj, hidden, gate_factor, up_factor, own_score)
    _, from_y1 = across(1, across1, core1[1:], [score, core1[0]])
    returned = lax.all_to_all(score, "exp", split_axis=0, concat_axis=0)
    down_matrix_gradient, combine_weight_gradient, gate_preact_gradient, up_preact_gradient = call(
        functools.partial(returned_body, capacity, n_exp, cuts[0]),
        [shape(shard, width), shape(topk, tok_rows, dtype=f32), shape(rows, units), shape(rows, units)],
        [VMEM] * 8 + [ANY] * 2,
        16,
        scratch=[
            pltpu.VMEM((shard, sizes[0]), bf16),
            pltpu.VMEM((topk, tok_rows), f32),
            pltpu.SemaphoreType.DMA((2,)),
            half_scratch[1],
        ],
        out_specs=[ANY] * 4,
        aliases=[(8, 2), (9, 3)],
    )(
        token_expert_choice.T, slots.T, meta, returned, far_half, keep0, core0, from_y0,
        gate_preact_gradient, up_preact_gradient,
    )
    (down_matrix_gradient,) = call(
        functools.partial(last_body, cuts[1]),
        [shape(shard, width)],
        [VMEM] * 3 + [ANY],
        8,
        scratch=[pltpu.VMEM((shard, sizes[1]), bf16), pltpu.SemaphoreType.DMA],
        out_specs=[ANY],
        aliases=[(3, 0)],
    )(keep1, core1[0], from_y1, down_matrix_gradient)
    return (
        gate_preact_gradient[None, None],
        up_preact_gradient[None, None],
        down_matrix_gradient[None],
        combine_weight_gradient.T,
    )


def direct(
    out_grad,
    combine,
    token_expert_choice,
    slots,
    counts,
    down_weight,
    stored_gate_preact,
    stored_up_preact,
):
    experts_here = lax.axis_size("exp")
    capacity = stored_gate_preact.shape[2] // experts_here
    tok_rows = out_grad.shape[0]
    model_width = out_grad.shape[1]
    slot_index = jnp.where(
        slots < capacity, token_expert_choice * capacity + slots, experts_here * capacity
    )
    flat_index = slot_index.reshape(-1)
    row_ids = jnp.broadcast_to(
        jnp.arange(tok_rows, dtype=jnp.int32)[:, None] + 1, slot_index.shape
    ).reshape(-1)
    sender_rows = (
        jnp.zeros((experts_here * capacity,), jnp.int32).at[flat_index].set(row_ids, mode="drop")
    )
    padded_grad = jnp.concatenate([jnp.zeros((1, model_width), out_grad.dtype), out_grad], axis=0)
    send_grad = padded_grad[sender_rows].reshape(experts_here, capacity, model_width)
    send_weight = (
        jnp.zeros((experts_here * capacity,), combine.dtype)
        .at[flat_index]
        .set(combine.reshape(-1), mode="drop")
    )
    send_weight = send_weight.reshape(experts_here, capacity)
    send_count = counts.reshape(experts_here, 1)
    recv_grad, received_weight, recv_count = (
        lax.all_to_all(send_grad, "exp", split_axis=0, concat_axis=0, tiled=True),
        lax.all_to_all(send_weight, "exp", split_axis=0, concat_axis=0, tiled=True),
        lax.all_to_all(send_count, "exp", split_axis=0, concat_axis=0, tiled=True),
    )
    live_mask = (jnp.arange(capacity, dtype=jnp.int32)[None, :] < recv_count).astype(jnp.float32)
    scaled = (live_mask * received_weight.astype(jnp.float32)).reshape(-1)
    live_rows = live_mask.reshape(-1)
    grad_rows = recv_grad.reshape(-1, model_width)
    proj = lax.dot_general(
        grad_rows,
        lax.all_gather(down_weight, "edp", axis=1, tiled=True)[0],
        (((1,), (1,)), ((), ())),
        preferred_element_type=jnp.float32,
    )
    gate_pre = stored_gate_preact[0, 0].astype(jnp.float32)
    up_pre = stored_up_preact[0, 0].astype(jnp.float32)
    sigmoid_gate = jax.nn.sigmoid(gate_pre)
    silu_gate = gate_pre * sigmoid_gate
    hidden = (silu_gate * up_pre).astype(jnp.bfloat16)
    weighted = (scaled[:, None] * grad_rows.astype(jnp.float32)).astype(jnp.bfloat16)
    grad_hidden = scaled[:, None] * proj
    gate_preact_gradient = (
        grad_hidden * up_pre * sigmoid_gate * (1.0 + gate_pre * (1.0 - sigmoid_gate))
    ).astype(jnp.bfloat16)
    up_preact_gradient = (grad_hidden * silu_gate).astype(jnp.bfloat16)
    score = (live_rows * jnp.sum(proj * hidden.astype(jnp.float32), axis=1)).reshape(
        experts_here, capacity
    )
    returned_scores = lax.all_to_all(score, "exp", split_axis=0, concat_axis=0, tiled=True)
    summed = lax.psum_scatter(
        lax.dot_general(
            hidden, weighted, (((0,), (0,)), ((), ())), preferred_element_type=jnp.float32
        ),
        "edp",
        scatter_dimension=0,
        tiled=True,
    )
    returned = jnp.concatenate([returned_scores.reshape(-1), jnp.zeros((1,), jnp.float32)])
    combine_weight_gradient = returned[slot_index]
    down_matrix_gradient = summed.astype(jnp.bfloat16)[None]
    return (
        gate_preact_gradient[None, None],
        up_preact_gradient[None, None],
        down_matrix_gradient,
        combine_weight_gradient,
    )


def solution(mesh):
    n_exp, n_edp = mesh.shape["exp"], mesh.shape["edp"]

    def on_device(*arrays):
        tok_rows = arrays[0].shape[0]
        capacity = arrays[6].shape[2] // n_exp
        if n_exp == 8 and n_edp == 4 and tok_rows == LANES and tok_rows <= 2 * capacity:
            return relayed(*arrays)
        return direct(*arrays)

    return jax.shard_map(
        on_device,
        mesh=mesh,
        in_specs=(
            P(("exp", "edp"), None),
            P(("exp", "edp"), None),
            P(("exp", "edp"), None),
            P(("exp", "edp"), None),
            P(("exp", "edp"), None),
            P("exp", "edp", None),
            P("exp", "edp", None, None),
            P("exp", "edp", None, None),
        ),
        out_specs=(
            P("exp", "edp", None, None),
            P("exp", "edp", None, None),
            P("exp", "edp", None),
            P(("exp", "edp"), None),
        ),
        check_vma=False,
    )
```

```python
import functools

import jax
import jax.numpy as jnp
from jax import lax
from jax.experimental import pallas as pl
from jax.experimental.pallas import tpu as pltpu
from jax.sharding import PartitionSpec as P


def flip(n, mask):
    return [(i, i ^ mask) for i in range(n)]


def column_cuts(width):
    unit = width // 20
    return [(0, 15 * unit), (15 * unit, width)]


VMEM = pl.BlockSpec(memory_space=pltpu.VMEM)
SMEM = pl.BlockSpec(memory_space=pltpu.SMEM)
BLOCK = pl.BlockSpec()
ANY = pl.BlockSpec(memory_space=pl.ANY)
LANES = 128
CODE, WEIGHT, LIVE, META_ROWS = 0, 8, 16, 24


def call(body, outs, specs, megabytes, flops=0, moved=0, scratch=(), after=(), out_specs=None, aliases=()):
    def ordered(*refs):
        body(*refs[len(after) :])

    kernel = pl.pallas_call(
        ordered,
        out_shape=outs,
        in_specs=[ANY] * len(after) + list(specs),
        out_specs=out_specs or [VMEM] * len(outs),
        scratch_shapes=scratch,
        input_output_aliases={len(after) + i: o for i, o in aliases},
        compiler_params=pltpu.CompilerParams(vmem_limit_bytes=megabytes * 1024 * 1024),
        cost_estimate=pl.CostEstimate(flops=flops, bytes_accessed=moved, transcendentals=0),
    )
    return functools.partial(kernel, *after)


def routing_body(
    capacity, n_exp, far, choice_ref, slot_ref, combine_ref, counts_ref, tok_ref, meta_ref, *outs
):
    topk = choice_ref.shape[0]
    choice = choice_ref[...]
    slot = slot_ref[...]
    limit = jnp.zeros_like(slot)
    for expert in range(n_exp):
        limit = jnp.where(choice == expert, counts_ref[:, expert : expert + 1], limit)
    kept = slot < capacity
    live = kept & (slot < limit)
    meta_ref[...] = jnp.zeros_like(meta_ref)
    meta_ref[CODE : CODE + topk, :] = jnp.where(kept, choice * capacity + slot, -1).astype(jnp.float32)
    meta_ref[WEIGHT : WEIGHT + topk, :] = jnp.where(live, combine_ref[...].astype(jnp.float32), 0.0)
    meta_ref[LIVE : LIVE + topk, :] = jnp.where(live, 1.0, 0.0)
    select(capacity, topk, meta_ref, tok_ref[...], outs, first=far - len(outs))


def places(target, capacity):
    return (lax.broadcasted_iota(jnp.int32, (capacity, LANES), 0) + target).astype(jnp.float32)


def pick(meta, topk, want):
    hit = meta[CODE : CODE + 1, :] == want
    for k in range(1, topk):
        hit = hit | (meta[CODE + k : CODE + k + 1, :] == want)
    return jnp.where(hit, 1.0, 0.0)


def weight_of(meta, topk, want):
    weight = jnp.zeros(want.shape, jnp.float32)
    for k in range(topk):
        weight = jnp.where(
            meta[CODE + k : CODE + k + 1, :] == want, meta[WEIGHT + k : WEIGHT + k + 1, :], weight
        )
    return jnp.sum(weight, axis=1, keepdims=True)


def select(capacity, topk, meta, rows, outs, own_meta=None, first=0):
    here = lax.axis_index("exp")
    columns = rows.shape[1]
    wants = [places((here ^ (first + m)) * capacity, capacity) for m in range(len(outs))]
    onehot = jnp.concatenate([pick(meta, topk, w) for w in wants], axis=0).astype(jnp.bfloat16)
    chosen = jnp.dot(onehot, rows, preferred_element_type=jnp.float32).astype(jnp.bfloat16)
    for m, out in enumerate(outs):
        out[:, :columns] = chosen[m * capacity : (m + 1) * capacity]
        if own_meta is not None:
            lane = lax.broadcasted_iota(jnp.int32, (capacity, LANES), 1)
            weight, own_weight = (weight_of(x, topk, wants[m]) for x in (meta, own_meta))
            out[:, columns:] = jnp.where(lane < LANES // 2, weight, own_weight).astype(jnp.bfloat16)


def select_own_body(capacity, topk, meta_ref, tok_ref, *outs):
    select(capacity, topk, meta_ref, tok_ref[...], outs)


def select_first_body(capacity, topk, cut, raw_ref, meta_ref, own_meta_ref, *outs):
    select(capacity, topk, meta_ref, raw_ref[:, cut[0] : cut[1]], outs, own_meta_ref)


def select_more_body(capacity, topk, cut, raw_ref, meta_ref, *outs):
    select(capacity, topk, meta_ref, raw_ref[:, cut[0] : cut[1]], outs)


def source_rows(capacity, n):
    source = lax.axis_index("exp") ^ n
    return pl.ds(pl.multiple_of(source * capacity, capacity), capacity)


def factors_body(
    capacity, n_edp, gate_ref, up_ref, meta_ref, shard_ref,
    hidden_ref, gate_factor_ref, up_factor_ref, turned_ref, meta_out_ref, shard_out_ref, scratch,
):
    data = lax.axis_index("edp")
    rows, units = gate_ref.shape
    shard = units // n_edp
    for n in range(rows // capacity):
        at = pl.ds(n * capacity, capacity)
        there = source_rows(capacity, n)
        gate_pre = gate_ref[there, :].astype(jnp.float32)
        up_pre = up_ref[there, :].astype(jnp.float32)
        sigmoid_gate = jax.nn.sigmoid(gate_pre)
        silu_gate = gate_pre * sigmoid_gate
        hidden_ref[at, :] = (silu_gate * up_pre).astype(jnp.bfloat16)
        gate_factor_ref[at, :] = up_pre * sigmoid_gate * (1.0 + gate_pre * (1.0 - sigmoid_gate))
        up_factor_ref[at, :] = silu_gate
    meta_out_ref[...] = meta_ref[...]
    shard_out_ref[...] = shard_ref[...]
    scratch[...] = hidden_ref[...].T
    for n in range(n_edp):
        turned_ref[n] = scratch[pl.ds(pl.multiple_of((data ^ n) * shard, 64), shard), :]


def add_cores(across_ref, *refs):
    *from_core, sum_ref = refs
    start = 0
    for ref in from_core:
        rows = pl.ds(start, ref.shape[0])
        start += ref.shape[0]
        sum_ref[rows, :] = (across_ref[rows, :] + ref[...].astype(jnp.float32)).astype(jnp.bfloat16)


def summed_out(cut, sums, out_ref, held, sem):
    keep_ref, from_core_ref, from_y_ref = sums
    held[...] = (
        keep_ref[...] + from_core_ref[...].astype(jnp.float32) + from_y_ref[...].astype(jnp.float32)
    ).astype(jnp.bfloat16)
    copy = pltpu.make_async_copy(held, out_ref.at[:, pl.ds(cut[0], cut[1] - cut[0])], sem)
    copy.start()
    return copy


def last_body(cut, *refs):
    *sums, _, out_ref, held, sem = refs
    summed_out(cut, sums, out_ref, held, sem).wait()


def returned_body(capacity, n_exp, cut, choice_ref, slot_ref, meta_ref, score_ref, far_half_ref, *refs):
    sums, refs = refs[:3], refs[5:]
    out_ref, weight_ref, gate_ref, up_ref, held, held_weight, sems, half_sems = refs
    far = n_exp // 2
    copies = []
    for m in range(0, far, 2):
        copies += copies_out(far, m, far, far_half_ref, (gate_ref, up_ref), half_sems)
    copies.append(summed_out(cut, sums, out_ref, held, sems.at[0]))
    topk, tokens = choice_ref.shape
    choice = choice_ref[...]
    slot = slot_ref[...]
    live = meta_ref[LIVE : LIVE + topk, :] > 0.0
    table = score_ref[...]
    high = table.astype(jnp.bfloat16)
    rest = table - high.astype(jnp.float32)
    middle = rest.astype(jnp.bfloat16)
    low = (rest - middle.astype(jnp.float32)).astype(jnp.bfloat16)
    split = jnp.concatenate([high, middle, low], axis=0)
    rank = lax.broadcasted_iota(jnp.int32, (capacity, tokens), 0)
    expert = lax.broadcasted_iota(jnp.int32, (n_exp, tokens), 0)
    onehot = jnp.concatenate(
        [jnp.where(rank == slot[k : k + 1, :], 1.0, 0.0).astype(jnp.bfloat16) for k in range(topk)], axis=1
    )
    parts = jnp.dot(split, onehot, preferred_element_type=jnp.float32)
    every = parts[:n_exp] + parts[n_exp : 2 * n_exp] + parts[2 * n_exp :]
    found = []
    for k in range(topk):
        mine = jnp.where(expert == choice[k : k + 1, :], every[:, k * tokens : (k + 1) * tokens], 0.0)
        found.append(jnp.sum(mine, axis=0, keepdims=True))
    held_weight[...] = jnp.where(live, jnp.concatenate(found, axis=0), 0.0)
    copies.append(pltpu.make_async_copy(held_weight, weight_ref, sems.at[1]))
    copies[-1].start()
    for copy in copies:
        copy.wait()


def weighted_rows(far, start, tile, cut, own, others, scales):
    blocks = []
    for half, pieces in enumerate((own, others)):
        first = start + (cut[0] if half == 0 else 0)
        for m in range(far):
            scale = weights_of(scales[m : m + 1], half == 0).astype(jnp.bfloat16)
            blocks.append(jnp.broadcast_to(scale, (scale.shape[0], tile)) * pieces[m][:, first : first + tile])
    return jnp.concatenate(blocks, axis=0)


def terms(turned_ref, rows, lanes, outs):
    first = outs[0][0]
    refs = [ref for _, some in outs for ref in some]
    shard, depth = turned_ref.shape[1:]
    left = turned_ref[first : first + len(outs)].reshape(len(outs) * shard, depth)
    term = jnp.dot(left, rows, preferred_element_type=jnp.float32)
    at = 0
    for ref in refs:
        ref[:, lanes] = term[at : at + ref.shape[0]].astype(ref.dtype)
        at += ref.shape[0]


def first_term_body(far, cut, tile, turned_ref, *refs):
    own, others, (send_ref, weighted) = refs[:far], refs[far : 2 * far], refs[2 * far :]
    for start in range(0, cut[1] - cut[0], tile):
        lanes = pl.ds(start, tile)
        rows = weighted_rows(far, start, tile, cut, own, others, others)
        weighted[:, lanes] = rows
        terms(turned_ref, rows, lanes, [(3, [send_ref])])


def more_terms_body(tile, shards, turned_ref, weighted, *refs):
    for start in range(0, weighted.shape[1], tile):
        lanes = pl.ds(start, tile)
        terms(turned_ref, weighted[:, lanes], lanes, [(n, [ref]) for n, ref in zip(shards, refs)])


def term_body(far, cut, tile, turned_ref, *refs):
    own, others, scales, (own_ref, across_ref, send_ref, *send_across_refs) = (
        refs[:far], refs[far : 2 * far], refs[2 * far : 3 * far], refs[3 * far :]
    )
    for start in range(0, cut[1] - cut[0], tile):
        lanes = pl.ds(start, tile)
        rows = weighted_rows(far, start, tile, cut, own, others, scales)
        outs = [(0, [own_ref]), (1, [send_ref]), (2, [across_ref]), (3, send_across_refs)]
        terms(turned_ref, rows, lanes, outs)


def nt(a, b):
    return lax.dot_general(a, b, (((1,), (1,)), ((), ())), preferred_element_type=jnp.float32)


def finish(proj, weights, hidden, gate_factor, up_factor):
    part = proj * hidden.astype(jnp.float32)
    lanes = part[:, :LANES]
    for i in range(LANES, part.shape[1], LANES):
        lanes = lanes + part[:, i : i + LANES]
    score = jnp.sum(lanes.T, axis=0, keepdims=True)
    scaled = weights * proj
    gate = (gate_factor * scaled).astype(jnp.bfloat16)
    up = (up_factor * scaled).astype(jnp.bfloat16)
    return gate, up, score


def weights_of(refs, own):
    at = LANES // 2 if own else 0
    return jnp.concatenate(
        [r[:, r.shape[1] - LANES :][:, at : at + 1] for r in refs], axis=0
    ).astype(jnp.float32)


def project_own_body(far, *refs):
    shards, own, (weight_ref, proj_ref) = refs[:4], refs[4 : 4 + far], refs[4 + far :]
    data = lax.axis_index("edp")
    shard = shards[0].shape[0]
    for n in range(4):
        weight_ref[pl.ds(pl.multiple_of((data ^ n) * shard, 64), shard), :] = shards[n][...]
    proj_ref[...] = nt(jnp.concatenate([p[...] for p in own], axis=0), weight_ref[...])


def finish_half(first, far, proj, weights, hidden_ref, gate_factor_ref, up_factor_ref, held, then):
    here = lax.axis_index("exp")
    count = 2 * (proj.shape[0] // far)
    scores = []
    for m in range(0, far, 2):
        near = slice(m * count // 2, m * count // 2 + count)
        at = slice((first + m) * count // 2, (first + m) * count // 2 + count)
        gate, up, score = finish(
            proj[near], weights[near], hidden_ref[at, :], gate_factor_ref[at, :], up_factor_ref[at, :]
        )
        scores.append(score)
        for i in range(2):
            mine = slice(i * count // 2, (i + 1) * count // 2)
            within = pl.multiple_of(lax.rem(here ^ i, 2) * (count // 2), count // 2)
            there = pl.ds(m // 2 * count + within, count // 2)
            held[0, there, :] = gate[mine]
            held[1, there, :] = up[mine]
        then(m)
    return scores


def copies_out(first, m, far, held, outs, sems):
    count = 2 * (held.shape[1] // far)
    lower = pl.multiple_of(((lax.axis_index("exp") ^ (first + m)) // 2) * count, count)
    copies = []
    for i, out in enumerate(outs):
        source = held.at[i, pl.ds(m // 2 * count, count), :]
        copies.append(pltpu.make_async_copy(source, out.at[pl.ds(lower, count), :], sems.at[m // 2, i]))
        copies[-1].start()
    return copies


def project_far_body(far, cut, *refs):
    pieces, refs = refs[:far], refs[far:]
    weight_ref, own_proj_ref, hidden_ref, gate_factor_ref, up_factor_ref, *outs = refs
    proj_ref, gate_ref, up_ref, score_ref, held, sems = outs
    copies = []
    scores = finish_half(
        0, far, own_proj_ref[...], weights_of(pieces, True), hidden_ref, gate_factor_ref, up_factor_ref,
        held, lambda m: copies.extend(copies_out(0, m, far, held, (gate_ref, up_ref), sems)),
    )
    for i, score in enumerate(scores):
        score_ref[i : i + 1, :] = score
    rows = jnp.concatenate([p[:, : cut[1] - cut[0]] for p in pieces], axis=0)
    proj_ref[...] = nt(rows, weight_ref[:, cut[0] : cut[1]])
    for copy in copies:
        copy.wait()


def final_body(far, cut, *refs):
    pieces, scales, refs = refs[:far], refs[far : 2 * far], refs[2 * far :]
    (
        weight_ref, proj_ref, hidden_ref, gate_factor_ref, up_factor_ref, own_score_ref,
        score_ref, held,
    ) = refs
    here = lax.axis_index("exp")
    capacity = pieces[0].shape[0]
    rows = jnp.concatenate([p[...] for p in pieces], axis=0)
    proj = proj_ref[...] + nt(rows, weight_ref[:, cut[0] : cut[1]])
    scores = finish_half(
        far, far, proj, weights_of(scales, False), hidden_ref, gate_factor_ref, up_factor_ref,
        held, lambda m: None,
    )
    for m in range(0, far, 2):
        for first, score in ((far + m, scores[m // 2]), (m, own_score_ref[m // 2 : m // 2 + 1, :])):
            for i in range(2):
                score_ref[pl.ds(here ^ (first + i), 1), :] = score[:, i * capacity : (i + 1) * capacity]


def relayed(
    out_grad,
    combine,
    token_expert_choice,
    slots,
    counts,
    down_weight,
    stored_gate_preact,
    stored_up_preact,
):
    n_exp = lax.axis_size("exp")
    n_edp = lax.axis_size("edp")
    capacity = stored_gate_preact.shape[2] // n_exp
    units = stored_gate_preact.shape[3]
    rows = n_exp * capacity
    tok_rows, width = out_grad.shape
    topk = slots.shape[1]
    shard = units // n_edp
    far = n_exp // 2
    cuts = column_cuts(width)
    sizes = [b - a for a, b in cuts]
    splits = [1, 1]
    bf16, f32 = jnp.bfloat16, jnp.float32

    def shape(*dims, dtype=bf16):
        return jax.ShapeDtypeStruct(dims, dtype)

    def hop(x, axis, mask, after=None):
        if after is not None:
            x, _ = lax.optimization_barrier((x, after))
        return lax.ppermute(x, axis, flip(lax.axis_size(axis), mask))

    def spread(found):
        return [found[0]] + [hop(found[m], "exp", m) for m in range(1, far)]

    meta, *found = call(
        functools.partial(routing_body, capacity, n_exp, far),
        [shape(META_ROWS, LANES, dtype=f32)] + [shape(capacity, width)] * (far // 2),
        [BLOCK] * 5,
        56,
        flops=2 * far * capacity * tok_rows * width,
        moved=out_grad.size * 4,
    )(token_expert_choice.T, slots.T, combine.T, counts, out_grad)
    raw = hop(out_grad, "exp", far)
    own = [hop(x, "exp", far // 2 + m) for m, x in enumerate(found)]
    hidden, gate_factor, up_factor, turned, meta, weight_here = call(
        functools.partial(factors_body, capacity, n_edp),
        [
            shape(rows, units),
            shape(rows, units, dtype=f32),
            shape(rows, units, dtype=f32),
            shape(n_edp, shard, rows),
            shape(META_ROWS, LANES, dtype=f32),
            shape(shard, width),
        ],
        [VMEM] * 4,
        24,
        flops=40 * rows * units,
        moved=16 * rows * units,
        scratch=[pltpu.VMEM((units, rows), bf16)],
    )(stored_gate_preact[0, 0], stored_up_preact[0, 0], meta, down_weight[0])
    weight_y = hop(down_weight[0], "edp", 2)
    far_meta = hop(meta, "exp", far, own[0])

    found = call(
        functools.partial(select_own_body, capacity, topk),
        [shape(capacity, width)] * (far // 2),
        [VMEM] * 2,
        16,
        after=[hidden],
    )(meta, out_grad)
    own = [found[0]] + [hop(found[m], "exp", m) for m in range(1, far // 2)] + own

    def term(k, others, scales, after=()):
        return call(
            functools.partial(term_body, far, cuts[k], sizes[k]),
            [shape(shard, sizes[k], dtype=f32)] * 2
            + [shape(shard, sizes[k])]
            + [shape(shard // splits[k], sizes[k])] * splits[k],
            [VMEM] * (1 + 3 * far),
            24,
            flops=2 * rows * units * sizes[k],
            moved=4 * (rows + units) * sizes[k],
            after=after,
        )(turned, *own, *others, *scales)

    def cores(send):
        return [hop(x, "edp", 1) for x in send]

    def across(k, mine, from_core, after=()):
        (sent,) = call(add_cores, [shape(shard, sizes[k])], [VMEM] * (1 + splits[k]), 8, after=after)(
            mine, *from_core
        )
        return sent, hop(sent, "edp", 2)

    found = call(
        functools.partial(select_first_body, capacity, topk, cuts[0]),
        [shape(capacity, sizes[0] + LANES)] * far,
        [VMEM] * 3,
        16,
        flops=2 * far * capacity * tok_rows * sizes[0],
        moved=4 * far * capacity * sizes[0],
        after=[*own[1:], hidden, weight_y],
    )(raw, far_meta, meta)
    far0 = spread(found)
    weight_core = hop(weight_here, "edp", 1, own[far - 1])
    weight_both = hop(weight_y, "edp", 1, found[0])
    weight, own_proj = call(
        functools.partial(project_own_body, far),
        [shape(units, width), shape(far * capacity, units, dtype=f32)],
        [VMEM] * (4 + far),
        32,
    )(weight_here, weight_core, weight_y, weight_both, *own)
    more = call(
        functools.partial(select_more_body, capacity, topk, cuts[1]),
        [shape(capacity, sizes[1])] * far,
        [VMEM] * 2,
        16,
        flops=2 * far * capacity * tok_rows * sizes[1],
        moved=4 * far * capacity * sizes[1],
        after=far0[:1],
    )(raw, far_meta)
    first0, weighted = call(
        functools.partial(first_term_body, far, cuts[0], sizes[0]),
        [shape(shard, sizes[0]), shape(rows, sizes[0])],
        [VMEM] * (1 + 2 * far),
        24,
        after=[own_proj, more[0]],
    )(turned, *own, *far0)
    first0 = hop(first0, "edp", 1)
    def more_terms(shards, outs, after=()):
        return call(
            functools.partial(more_terms_body, sizes[0], shards), outs, [VMEM] * 2, 24, after=after
        )(turned, weighted)

    send0, across0 = more_terms([1, 2], [shape(shard, sizes[0]), shape(shard, sizes[0], dtype=f32)])
    core0 = hop(send0, "edp", 1)
    sent0, from_y0 = across(0, across0, [first0])
    far1 = [more[0]] + [hop(more[m], "exp", m, sent0) for m in range(1, far)]
    half_scratch = [
        pltpu.VMEM((2, far * capacity, units), bf16),
        pltpu.SemaphoreType.DMA((far // 2, 2)),
    ]
    proj, gate_preact_gradient, up_preact_gradient, own_score = call(
        functools.partial(project_far_body, far, cuts[0]),
        [
            shape(far * capacity, units, dtype=f32),
            shape(rows, units),
            shape(rows, units),
            shape(far // 2, 2 * capacity, dtype=f32),
        ],
        [VMEM] * (5 + far),
        24,
        scratch=half_scratch,
        after=[sent0, far1[0], core0],
        out_specs=[VMEM, ANY, ANY, VMEM],
    )(*far0, weight, own_proj, hidden, gate_factor, up_factor)
    (keep0,) = more_terms([0], [shape(shard, sizes[0], dtype=f32)], [proj])
    keep1, across1, *send1 = term(1, far1, far0, [keep0])
    core1 = cores(send1)
    score, far_half = call(
        functools.partial(final_body, far, cuts[1]),
        [shape(n_exp, capacity, dtype=f32), shape(2, far * capacity, units)],
        [VMEM] * (2 * far + 6),
        24,
        after=[keep1],
    )(*far1, *far0, weight, proj, hidden, gate_factor, up_factor, own_score)
    _, from_y1 = across(1, across1, core1[1:], [score, core1[0]])
    returned = lax.all_to_all(score, "exp", split_axis=0, concat_axis=0)
    down_matrix_gradient, combine_weight_gradient, gate_preact_gradient, up_preact_gradient = call(
        functools.partial(returned_body, capacity, n_exp, cuts[0]),
        [shape(shard, width), shape(topk, tok_rows, dtype=f32), shape(rows, units), shape(rows, units)],
        [VMEM] * 8 + [ANY] * 2,
        16,
        scratch=[
            pltpu.VMEM((shard, sizes[0]), bf16),
            pltpu.VMEM((topk, tok_rows), f32),
            pltpu.SemaphoreType.DMA((2,)),
            half_scratch[1],
        ],
        out_specs=[ANY] * 4,
        aliases=[(8, 2), (9, 3)],
    )(
        token_expert_choice.T, slots.T, meta, returned, far_half, keep0, core0, from_y0,
        gate_preact_gradient, up_preact_gradient,
    )
    (down_matrix_gradient,) = call(
        functools.partial(last_body, cuts[1]),
        [shape(shard, width)],
        [VMEM] * 3 + [ANY],
        8,
        scratch=[pltpu.VMEM((shard, sizes[1]), bf16), pltpu.SemaphoreType.DMA],
        out_specs=[ANY],
        aliases=[(3, 0)],
    )(keep1, core1[0], from_y1, down_matrix_gradient)
    return (
        gate_preact_gradient[None, None],
        up_preact_gradient[None, None],
        down_matrix_gradient[None],
        combine_weight_gradient.T,
    )


def direct(
    out_grad,
    combine,
    token_expert_choice,
    slots,
    counts,
    down_weight,
    stored_gate_preact,
    stored_up_preact,
):
    experts_here = lax.axis_size("exp")
    capacity = stored_gate_preact.shape[2] // experts_here
    tok_rows = out_grad.shape[0]
    model_width = out_grad.shape[1]
    slot_index = jnp.where(
        slots < capacity, token_expert_choice * capacity + slots, experts_here * capacity
    )
    flat_index = slot_index.reshape(-1)
    row_ids = jnp.broadcast_to(
        jnp.arange(tok_rows, dtype=jnp.int32)[:, None] + 1, slot_index.shape
    ).reshape(-1)
    sender_rows = (
        jnp.zeros((experts_here * capacity,), jnp.int32).at[flat_index].set(row_ids, mode="drop")
    )
    padded_grad = jnp.concatenate([jnp.zeros((1, model_width), out_grad.dtype), out_grad], axis=0)
    send_grad = padded_grad[sender_rows].reshape(experts_here, capacity, model_width)
    send_weight = (
        jnp.zeros((experts_here * capacity,), combine.dtype)
        .at[flat_index]
        .set(combine.reshape(-1), mode="drop")
    )
    send_weight = send_weight.reshape(experts_here, capacity)
    send_count = counts.reshape(experts_here, 1)
    recv_grad, received_weight, recv_count = (
        lax.all_to_all(send_grad, "exp", split_axis=0, concat_axis=0, tiled=True),
        lax.all_to_all(send_weight, "exp", split_axis=0, concat_axis=0, tiled=True),
        lax.all_to_all(send_count, "exp", split_axis=0, concat_axis=0, tiled=True),
    )
    live_mask = (jnp.arange(capacity, dtype=jnp.int32)[None, :] < recv_count).astype(jnp.float32)
    scaled = (live_mask * received_weight.astype(jnp.float32)).reshape(-1)
    live_rows = live_mask.reshape(-1)
    grad_rows = recv_grad.reshape(-1, model_width)
    proj = lax.dot_general(
        grad_rows,
        lax.all_gather(down_weight, "edp", axis=1, tiled=True)[0],
        (((1,), (1,)), ((), ())),
        preferred_element_type=jnp.float32,
    )
    gate_pre = stored_gate_preact[0, 0].astype(jnp.float32)
    up_pre = stored_up_preact[0, 0].astype(jnp.float32)
    sigmoid_gate = jax.nn.sigmoid(gate_pre)
    silu_gate = gate_pre * sigmoid_gate
    hidden = (silu_gate * up_pre).astype(jnp.bfloat16)
    weighted = (scaled[:, None] * grad_rows.astype(jnp.float32)).astype(jnp.bfloat16)
    grad_hidden = scaled[:, None] * proj
    gate_preact_gradient = (
        grad_hidden * up_pre * sigmoid_gate * (1.0 + gate_pre * (1.0 - sigmoid_gate))
    ).astype(jnp.bfloat16)
    up_preact_gradient = (grad_hidden * silu_gate).astype(jnp.bfloat16)
    score = (live_rows * jnp.sum(proj * hidden.astype(jnp.float32), axis=1)).reshape(
        experts_here, capacity
    )
    returned_scores = lax.all_to_all(score, "exp", split_axis=0, concat_axis=0, tiled=True)
    summed = lax.psum_scatter(
        lax.dot_general(
            hidden, weighted, (((0,), (0,)), ((), ())), preferred_element_type=jnp.float32
        ),
        "edp",
        scatter_dimension=0,
        tiled=True,
    )
    returned = jnp.concatenate([returned_scores.reshape(-1), jnp.zeros((1,), jnp.float32)])
    combine_weight_gradient = returned[slot_index]
    down_matrix_gradient = summed.astype(jnp.bfloat16)[None]
    return (
        gate_preact_gradient[None, None],
        up_preact_gradient[None, None],
        down_matrix_gradient,
        combine_weight_gradient,
    )


def solution(mesh):
    n_exp, n_edp = mesh.shape["exp"], mesh.shape["edp"]

    def on_device(*arrays):
        tok_rows = arrays[0].shape[0]
        capacity = arrays[6].shape[2] // n_exp
        if n_exp == 8 and n_edp == 4 and tok_rows == LANES and tok_rows <= 2 * capacity:
            return relayed(*arrays)
        return direct(*arrays)

    return jax.shard_map(
        on_device,
        mesh=mesh,
        in_specs=(
            P(("exp", "edp"), None),
            P(("exp", "edp"), None),
            P(("exp", "edp"), None),
            P(("exp", "edp"), None),
            P(("exp", "edp"), None),
            P("exp", "edp", None),
            P("exp", "edp", None, None),
            P("exp", "edp", None, None),
        ),
        out_specs=(
            P("exp", "edp", None, None),
            P("exp", "edp", None, None),
            P("exp", "edp", None),
            P(("exp", "edp"), None),
        ),
        check_vma=False,
    )
```
